256 devices in a mesh: ctx: 32 (over z, y), head: 8 (over x, core).
Axes of the slice: x: 4, y: 4, z: 8, core: 2. Of those that a mesh axis runs over, the one named last changes fastest.
Arguments:
- queries: bfloat16 [16384, 8192], P('ctx', 'head'), may hold values from -40 to 40
- keys: bfloat16 [16384, 1024], P('ctx', 'head'), may hold values from -6 to 6
- values: bfloat16 [16384, 1024], P('ctx', 'head'), may hold values from -6 to 6
- sink_logits: float32 [64], P('head'), may hold values from 3 to 9
- vert_blocks: int32 [64, 8], P('head'), may hold values from -1 to 127, as said below
- slash_offsets: int32 [64, 3], P('head'), may hold values from 0 to 4, as said below
- output_weight: bfloat16 [8192, 4096], P('head'), may hold values from -0.0625 to 0.0625
Outputs:
- mixed: bfloat16 [16384, 4096], P(('ctx', 'head'))
The draws below stay inside these ranges and needn't reach their ends.
Inputs may be any that keep to these rules, and one draw needn't show every extreme that they name: `vert_blocks`: in row h the valid entries are distinct block numbers and come first, the rest are -1; a row has 1 to 8 valid entries. The 8 heads that share a key-value head name exactly 24 distinct blocks together, and in each group some heads have 8 valid entries. `slash_offsets`: each row holds 3 distinct offsets, among them 0 and 4, in any order.
All inputs are finite; a program needn't handle non-finite values.
Results may differ from the reference program's by a relative error of at most 0.017.
Values may be sent and summed in bfloat16 or wider, within the bound.
No kernel may reach another device: no remote copies, remote signals or barrier semaphores. Data moves between devices by JAX's collectives and lax.ppermute only.
A program may use at most 128 MiB of HBM per device.

```python
import jax
import jax.numpy as jnp
from jax import lax

QUERY_HEAD_COUNT = 64
KEY_VALUE_HEADS = 8
HEAD_SIZE = 128
DO = 4096
KEY_BLOCK_ROWS = 128
VERTICAL_COUNT = 8
SLASH_BAND_COUNT = 3
D = 8192
UCAP = 24
NB_DEV = 4
KEY_BLOCK_COUNT = 128
TOKEN_COUNT = 16384
N_HEAD = 8


def shared_rows(key):
    first_part = jax.random.fold_in(key, 0)
    normal_sample = jnp.clip(jax.random.normal(first_part, (TOKEN_COUNT, KEY_VALUE_HEADS, HEAD_SIZE), jnp.float32), -6.0, 6.0)
    base_offset = normal_sample
    return base_offset


def draw_keys(key, part):
    base_offset = shared_rows(key)
    return base_offset.reshape(TOKEN_COUNT, KEY_VALUE_HEADS * HEAD_SIZE).astype(jnp.bfloat16)


def draw_queries(key, part):
    own_key = jax.random.fold_in(key, 13)
    return (2.5 * jnp.clip(jax.random.normal(own_key, (TOKEN_COUNT, QUERY_HEAD_COUNT * HEAD_SIZE), jnp.float32), -6.0, 6.0)).astype(jnp.bfloat16)


def draw_vert_blocks(key, part):
    key = jax.random.fold_in(key, 5)
    heads_per_group = QUERY_HEAD_COUNT // KEY_VALUE_HEADS

    def single_group(kv_index):
        group_key = jax.random.fold_in(key, kv_index)
        first_part, second_part, third, fourth = jax.random.split(group_key, 4)
        pool = jax.random.permutation(first_part, KEY_BLOCK_COUNT)[:UCAP].astype(jnp.int32)
        roles = jax.random.permutation(second_part, heads_per_group).astype(jnp.int32)
        head_keys = jax.random.split(third, heads_per_group)
        random_place = jax.vmap(lambda single: jax.random.permutation(single, UCAP)[:VERTICAL_COUNT].astype(jnp.int32))(head_keys)
        covering = roles[:, None] * VERTICAL_COUNT + jnp.arange(VERTICAL_COUNT, dtype=jnp.int32)[None, :]
        place = jnp.where(roles[:, None] < 3, covering, random_place)
        counts = jax.random.randint(fourth, (heads_per_group,), 1, VERTICAL_COUNT + 1)
        counts = jnp.where(roles < 3, VERTICAL_COUNT, counts)
        chosen_ids = pool[place]
        return jnp.where(jnp.arange(VERTICAL_COUNT)[None, :] < counts[:, None], chosen_ids, -1)
    return jax.vmap(single_group)(jnp.arange(KEY_VALUE_HEADS, dtype=jnp.int32)).reshape(QUERY_HEAD_COUNT, VERTICAL_COUNT).astype(jnp.int32)


def draw_slash_offsets(key, part):
    key = jax.random.fold_in(key, 7)
    first_part, second_part = jax.random.split(key)
    middle = jax.random.randint(first_part, (QUERY_HEAD_COUNT,), 1, NB_DEV)
    trio = jnp.stack([jnp.zeros((QUERY_HEAD_COUNT,), jnp.int32), jnp.full((QUERY_HEAD_COUNT,), NB_DEV, jnp.int32), middle.astype(jnp.int32)], axis=1)
    scores = jax.random.randint(second_part, (QUERY_HEAD_COUNT, 3), 0, 1 << 20) * 4 + jnp.arange(3)[None, :]
    order = jnp.argsort(scores, axis=1)
    return jnp.take_along_axis(trio, order, axis=1).astype(jnp.int32)


def shard_levels(key, extent, cuts, least, largest):
    gain = 1.0
    for position, shards_of in cuts:
        heights = jax.random.uniform(jax.random.fold_in(jax.random.fold_in(key, 6), position), (shards_of,), jnp.float32, least / len(cuts), largest / len(cuts))
        gain = gain * jnp.repeat(jnp.exp(heights), extent[position] // shards_of).reshape((-1,) + (1,) * (len(extent) - 1 - position))
    return gain


def bell_draw(key, extent, width, reach, cuts=(), kind=jnp.bfloat16):
    factor_of = shard_levels(key, extent, cuts, -0.22, 0.18) if cuts else 1.0
    drawn = jax.random.normal(key, extent, jnp.float32) * width * factor_of
    return jnp.minimum(jnp.maximum(drawn, -reach), reach).astype(kind)


def setup_inputs(seed: int = 0) -> dict:
    key_list = jax.random.split(jax.random.key(seed), 8)
    queries = draw_queries(jax.random.fold_in(key_list[7], 71), 0)
    keys = draw_keys(jax.random.fold_in(key_list[7], 71), 0)
    values = bell_draw(key_list[2], (TOKEN_COUNT, KEY_VALUE_HEADS * HEAD_SIZE), 1.0, 6.0, ((0, 32), (1, 8)))
    sink_logits = jnp.clip(3.0 + 6.0 * jax.random.uniform(key_list[3], (QUERY_HEAD_COUNT,), jnp.float32) ** shard_levels(key_list[3], (QUERY_HEAD_COUNT,), ((0, 8),), -0.2, 0.2), 3.0, 9.0)
    vert_blocks = draw_vert_blocks(jax.random.fold_in(key_list[7], 71), 0)
    slash_offsets = draw_slash_offsets(jax.random.fold_in(key_list[7], 71), 0)
    output_weight = bell_draw(key_list[6], (D, DO), D ** -0.5, 0.0625, ((0, 8),))
    return {"queries": queries, "keys": keys, "values": values, "sink_logits": sink_logits, "vert_blocks": vert_blocks, "slash_offsets": slash_offsets, "output_weight": output_weight}


def reference(queries, keys, values, sink_logits, vert_blocks, slash_offsets, output_weight):
    logit_scale = HEAD_SIZE ** -0.5
    heads_per_group = QUERY_HEAD_COUNT // KEY_VALUE_HEADS
    query_position = jnp.arange(TOKEN_COUNT, dtype=jnp.int32)
    within = jnp.arange(KEY_BLOCK_ROWS, dtype=jnp.int32)
    every_block = jnp.arange(KEY_BLOCK_COUNT, dtype=jnp.int32)

    def one_head(head_index):
        kv_index = head_index // heads_per_group
        query_head = lax.dynamic_slice_in_dim(queries, (head_index * HEAD_SIZE).astype(jnp.int32), HEAD_SIZE, 1)
        key_head = lax.dynamic_slice_in_dim(keys, (kv_index * HEAD_SIZE).astype(jnp.int32), HEAD_SIZE, 1)
        value_head = lax.dynamic_slice_in_dim(values, (kv_index * HEAD_SIZE).astype(jnp.int32), HEAD_SIZE, 1)
        vert_ids = vert_blocks[head_index]
        band_offsets = slash_offsets[head_index]
        vert_rows = (jnp.maximum(vert_ids, 0)[:, None] * KEY_BLOCK_ROWS + within[None, :]).reshape(-1)
        vert_keys = key_head[vert_rows]
        vert_vals = value_head[vert_rows]
        score_vert = jnp.dot(query_head, vert_keys.T, preferred_element_type=jnp.float32) * logit_scale
        vert_mask = jnp.repeat(vert_ids >= 0, KEY_BLOCK_ROWS)[None, :] & (vert_rows[None, :] <= query_position[:, None])
        band_block = every_block[:, None] - band_offsets[None, :]
        duplicate = jnp.any(band_block[:, :, None] == vert_ids[None, None, :], axis=2)
        band_valid = (band_block >= 0) & jnp.logical_not(duplicate)
        band_clip = jnp.maximum(band_block, 0)
        slash_key_rows = key_head.reshape(KEY_BLOCK_COUNT, KEY_BLOCK_ROWS, HEAD_SIZE)[band_clip].reshape(KEY_BLOCK_COUNT, SLASH_BAND_COUNT * KEY_BLOCK_ROWS, HEAD_SIZE)
        slash_value_rows = value_head.reshape(KEY_BLOCK_COUNT, KEY_BLOCK_ROWS, HEAD_SIZE)[band_clip].reshape(KEY_BLOCK_COUNT, SLASH_BAND_COUNT * KEY_BLOCK_ROWS, HEAD_SIZE)
        band_row = (band_clip[:, :, None] * KEY_BLOCK_ROWS + within[None, None, :]).reshape(KEY_BLOCK_COUNT, SLASH_BAND_COUNT * KEY_BLOCK_ROWS)
        query_block_rows = query_head.reshape(KEY_BLOCK_COUNT, KEY_BLOCK_ROWS, HEAD_SIZE).astype(jnp.float32)
        slash_scores = jnp.einsum("wih,wch->wic", query_block_rows, slash_key_rows.astype(jnp.float32)) * logit_scale
        position_blocks = query_position.reshape(KEY_BLOCK_COUNT, KEY_BLOCK_ROWS)
        band_mask = jnp.repeat(band_valid, KEY_BLOCK_ROWS, axis=1)[:, None, :] & (band_row[:, None, :] <= position_blocks[:, :, None])
        slash_scores = slash_scores.reshape(TOKEN_COUNT, SLASH_BAND_COUNT * KEY_BLOCK_ROWS)
        band_mask = band_mask.reshape(TOKEN_COUNT, SLASH_BAND_COUNT * KEY_BLOCK_ROWS)
        sink_value = sink_logits[head_index]
        row_max = jnp.maximum(jnp.maximum(jnp.max(jnp.where(vert_mask, score_vert, -jnp.inf), axis=1), jnp.max(jnp.where(band_mask, slash_scores, -jnp.inf), axis=1)), sink_value)
        exp_vert = jnp.where(vert_mask, jnp.exp(score_vert - row_max[:, None]), jnp.float32(0.0))
        exp_band = jnp.where(band_mask, jnp.exp(slash_scores - row_max[:, None]), jnp.float32(0.0))
        denominator = jnp.exp(sink_value - row_max) + jnp.sum(exp_vert, axis=1) + jnp.sum(exp_band, axis=1)
        weight_vert = (exp_vert / denominator[:, None]).astype(jnp.bfloat16)
        slash_weights = (exp_band / denominator[:, None]).astype(jnp.bfloat16)
        combined_output = jnp.dot(weight_vert, vert_vals, preferred_element_type=jnp.float32)
        combined_output = combined_output + jnp.einsum("wgx,wxu->wgu", slash_weights.reshape(KEY_BLOCK_COUNT, KEY_BLOCK_ROWS, SLASH_BAND_COUNT * KEY_BLOCK_ROWS).astype(jnp.float32), slash_value_rows.astype(jnp.float32)).reshape(TOKEN_COUNT, HEAD_SIZE)
        return combined_output.astype(jnp.bfloat16)

    head_outputs = lax.map(one_head, jnp.arange(QUERY_HEAD_COUNT, dtype=jnp.int32))
    attention = jnp.transpose(head_outputs, (1, 0, 2)).reshape(TOKEN_COUNT, QUERY_HEAD_COUNT * HEAD_SIZE)
    run_width = D // N_HEAD

    def add_group(running, group_index):
        start_row = (group_index * run_width).astype(jnp.int32)
        partial_product = jnp.dot(lax.dynamic_slice_in_dim(attention, start_row, run_width, 1), lax.dynamic_slice_in_dim(output_weight, start_row, run_width, 0), preferred_element_type=jnp.float32)
        rounded = lax.optimization_barrier(partial_product.astype(jnp.bfloat16))
        return running + rounded.astype(jnp.float32), None

    total, _ = lax.scan(add_group, jnp.zeros((TOKEN_COUNT, DO), jnp.float32), jnp.arange(N_HEAD, dtype=jnp.int32))
    return total.astype(jnp.bfloat16)
```

```python
import functools

import jax
import jax.numpy as jnp
from jax import lax
from jax.experimental import pallas as pl
from jax.experimental.pallas import tpu as pltpu
from jax.sharding import PartitionSpec as P

HEAD = 128
ROWS = 128
SLOTS = 24
ENTRIES = 11
BLOCKS = 128
RUNS = 4
SCALE = HEAD ** -0.5
LOG2E = 1.4426950408889634
NEVER = 1 << 20
Z, Y, X = 8, 4, 4


def z_pairs(step):
    return [(Y * z + y, Y * ((z + step) % Z) + y) for z in range(Z) for y in range(Y)]


def y_pairs(flip):
    return [(Y * z + y, Y * z + (y ^ flip)) for z in range(Z) for y in range(Y)]


def x_pairs(step):
    return [(2 * x + k, 2 * ((x + step) % X) + k) for x in range(X) for k in range(2)]


CORE_PAIRS = [(h, h ^ 1) for h in range(8)]


def attend(meta, idx, sink, thr, q, a0, a2, b0, b2, a1, a3, b1, b3, kp, vp, kc, vc, w, dep, keep, give, token,
           kv, qs, ws, att, sems):
    run, core, odd = meta[0], meta[1], meta[2]
    copies = []

    def copy(src, dst):
        c = pltpu.make_async_copy(src, dst, sems.at[len(copies)])
        c.start()
        copies.append(c)

    copy(q.at[pl.ds(pl.multiple_of(run * ROWS + core * 64, 64), 64)], qs.at[pl.ds(0, 64)])
    copy(q.at[pl.ds(pl.multiple_of(run * ROWS + (1 - core) * 64, 64), 64)], qs.at[pl.ds(64, 64)])
    for kind, (prev, cur) in enumerate(((kp, kc), (vp, vc))):
        copy(prev, kv.at[kind, pl.ds(SLOTS, RUNS)])
        copy(cur, kv.at[kind, pl.ds(SLOTS + RUNS, RUNS)])
    for kind, parts in ((odd, (a0, a2, b0, b2)), (1 - odd, (a1, a3, b1, b3))):
        for p, part in enumerate(parts):
            copy(part, kv.at[kind, pl.ds(0, SLOTS), pl.ds(32 * p, 32)])
    first = len(copies)
    copy(w, ws)
    for c in copies[:first]:
        c.wait()
    place = lax.broadcasted_iota(jnp.int32, (ROWS, 1), 0)
    place = place + jnp.where(place < 64, core * 64, -core * 64)
    for h in range(8):
        cols = slice(h * HEAD, (h + 1) * HEAD)
        rows = [idx[run, h, e] for e in range(ENTRIES)]
        keys = jnp.concatenate([kv[0, r] for r in rows], axis=0)
        scores = lax.dot_general(qs[:, cols], keys, (((1,), (1,)), ((), ())), preferred_element_type=jnp.float32)
        limit = thr[run, pl.ds(h, 1), :]
        scores = jnp.where(place >= limit, scores, -1e30)
        sink_raw = sink[h] * (1.0 / SCALE)
        top = jnp.maximum(jnp.max(scores, axis=1, keepdims=True), sink_raw)
        weights = jnp.exp2((scores - top) * (SCALE * LOG2E))
        total = jnp.sum(weights, axis=1, keepdims=True) + jnp.exp2((sink_raw - top) * (SCALE * LOG2E))
        values = jnp.concatenate([kv[1, r] for r in rows], axis=0)
        mixed = jnp.dot(weights.astype(jnp.bfloat16), values, preferred_element_type=jnp.float32)
        att[:, cols] = (mixed / total).astype(jnp.bfloat16)
    copies[first].wait()
    tile = 512
    for n in range(w.shape[1] // tile):
        cols = slice(n * tile, (n + 1) * tile)
        out = jnp.dot(att[...], ws[:, cols], preferred_element_type=jnp.float32).astype(jnp.bfloat16)
        keep[:, cols] = out[:64]
        give[:, cols] = out[64:]
    token[0] = dep[0] + 1


def block_attention(meta, idx, sink, thr, q, parts, band, w, dep):
    smem = pl.BlockSpec(memory_space=pltpu.SMEM)
    vmem = pl.BlockSpec(memory_space=pltpu.VMEM)
    anyw = pl.BlockSpec(memory_space=pl.ANY)
    half = jax.ShapeDtypeStruct((64, w.shape[1]), jnp.bfloat16)
    return pl.pallas_call(
        attend,
        out_shape=(half, half, jax.ShapeDtypeStruct((1,), jnp.int32)),
        in_specs=[smem, smem, smem, vmem] + [anyw] * 14 + [smem],
        out_specs=(vmem, vmem, smem),
        scratch_shapes=[
            pltpu.VMEM((2, SLOTS + 2 * RUNS, ROWS, HEAD), jnp.bfloat16),
            pltpu.VMEM((ROWS, q.shape[1]), jnp.bfloat16),
            pltpu.VMEM(w.shape, jnp.bfloat16),
            pltpu.VMEM((ROWS, q.shape[1]), jnp.bfloat16),
            pltpu.SemaphoreType.DMA((15,)),
        ],
        compiler_params=pltpu.CompilerParams(vmem_limit_bytes=32 * 1024 * 1024),
        cost_estimate=pl.CostEstimate(flops=2 * 10 ** 9, bytes_accessed=12 * 2 ** 20, transcendentals=1408 * 1024),
    )(meta, idx, sink, thr, q, *parts, *band, w, dep)


def total_of(*terms):
    return functools.reduce(lambda a, b: a + b, [t.astype(jnp.float32) for t in terms]).astype(jnp.bfloat16)


def tables(c, vert_blocks, slash_offsets):
    z, y = c // Y, c % Y
    block = jnp.arange(BLOCKS, dtype=jnp.int32)
    present = jnp.any(vert_blocks.reshape(-1, 1) == block[None, :], axis=0).astype(jnp.int32)
    rank = jnp.sum(jnp.where(block[:, None] > block[None, :], present[None, :], 0), axis=1)
    place = jnp.where(present > 0, rank, -1)
    slot = jnp.sum(jnp.where(vert_blocks[:, :, None] == block, rank, 0), axis=2)
    run = jnp.arange(RUNS, dtype=jnp.int32)
    own = RUNS * c + run
    band = own[:, None, None] - slash_offsets[None]
    listed = jnp.any(band[:, :, :, None] == vert_blocks[None, :, None, :], axis=3)
    band_idx = SLOTS + RUNS + run[:, None, None] - slash_offsets[None]
    idx = jnp.concatenate([jnp.broadcast_to(slot[None], (RUNS,) + slot.shape), band_idx], axis=2)
    n = jnp.arange(ROWS, dtype=jnp.int32)
    part, inner, row = n // 32, (n // 8) % 4, n % 8
    z_of = jnp.where(part < 2, z + 2 * inner, z + jnp.where(inner < 2, -1 - 2 * inner, 2 * inner - 3)) % Z
    y_of = (y // 2) ^ (part % 2)
    key_row = (z_of * 2 + y_of) * 8 + row
    diag = vert_blocks[None] == own[:, None, None]
    seen = (vert_blocks[None] >= 0) & (vert_blocks[None] < own[:, None, None])
    thr_vert = jnp.where(diag[..., None], key_row, jnp.where(seen[..., None], -1, NEVER))
    ok = (band >= 0) & jnp.logical_not(listed)
    at_own = slash_offsets[None] == 0
    thr_band = jnp.where(ok[..., None], jnp.where(at_own[..., None], n, -1), NEVER)
    thr = jnp.concatenate([thr_vert, thr_band], axis=2).reshape(RUNS, vert_blocks.shape[0], ENTRIES * ROWS)
    return place, idx, thr


def per_device(queries, keys, values, sink_logits, vert_blocks, slash_offsets, output_weight):
    c = lax.axis_index("ctx")
    h = lax.axis_index("head")
    x, core = h // 2, h % 2
    keys = keys.reshape(RUNS, ROWS, HEAD)
    values = values.reshape(RUNS, ROWS, HEAD)
    step = [(s, s + 1) for s in range(Z * Y - 1)]
    k_prev = lax.ppermute(keys, "ctx", step)
    v_prev = lax.ppermute(values, "ctx", step)
    place, idx, thr = tables(c, vert_blocks, slash_offsets)

    def slices(a):
        return jnp.transpose(a.reshape(RUNS, 16, 8, HEAD), (1, 0, 2, 3))

    spread = jnp.stack([slices(keys), slices(values)], axis=1).reshape(Z * Y, RUNS * 8, HEAD)
    got = lax.all_to_all(spread, "ctx", 0, 0, tiled=True).reshape(BLOCKS * 8, HEAD)
    r = jnp.arange(SLOTS * 8, dtype=jnp.int32)[:, None]
    col = jnp.arange(BLOCKS * 8, dtype=jnp.int32)[None, :]
    pick = (jnp.repeat(place, 8)[None, :] == r // 8) & (col % 8 == r % 8)
    mine = jnp.dot(pick.astype(jnp.bfloat16), got, preferred_element_type=jnp.float32)
    mine = mine.astype(jnp.bfloat16).reshape(SLOTS, 8, HEAD)

    def from_z(a, offset):
        return lax.ppermute(a, "ctx", z_pairs(-offset))

    z2, z4, z6 = from_z(mine, 2), from_z(mine, 4), from_z(mine, 6)
    a0 = jnp.concatenate([mine, z2, z4, z6], axis=1)
    low = from_z(jnp.concatenate([mine, z6], axis=1), -1)
    high = from_z(jnp.concatenate([mine, z2], axis=1), 1)
    b0 = jnp.concatenate([low, high], axis=1)
    a1, a2, a3 = [lax.ppermute(a0, "ctx", y_pairs(f)) for f in (1, 2, 3)]
    b1, b2, b3 = [lax.ppermute(b0, "ctx", y_pairs(f)) for f in (1, 2, 3)]
    parts = (a0, a2, b0, b2, a1, a3, b1, b3)

    dep = jnp.zeros((1,), jnp.int32)
    band = (k_prev, v_prev, keys, values)
    sums = {}
    for d in (2, 1, 3, 0):
        meta = jnp.stack([(x + d) % X, core, c % 2]).astype(jnp.int32)
        keep, give, dep = block_attention(meta, idx, sink_logits, thr, queries, parts, band, output_weight, dep)
        sums[d] = (keep, lax.ppermute(give, "head", CORE_PAIRS))
    mid = output_weight.shape[1] // 2

    def left(pair):
        return tuple(p[:, :mid] for p in pair)

    def right(pair):
        return tuple(p[:, mid:] for p in pair)

    def to_x(a, step):
        return lax.ppermute(a, "head", x_pairs(step))

    relay_left = to_x(total_of(*left(sums[2])), 1)
    relay_right = to_x(total_of(*right(sums[2])), -1)
    right_below = to_x(total_of(*right(sums[1])), 1)
    left_above = to_x(total_of(*left(sums[3])), -1)
    left_below = to_x(total_of(*left(sums[1]), relay_left), 1)
    right_above = to_x(total_of(*right(sums[3]), relay_right), -1)
    out_left = total_of(*left(sums[0]), left_below, left_above)
    out_right = total_of(*right(sums[0]), right_below, right_above)
    return jnp.concatenate([out_left, out_right], axis=1)


def solution(mesh):
    return jax.shard_map(
        per_device,
        mesh=mesh,
        in_specs=(
            P("ctx", "head"),
            P("ctx", "head"),
            P("ctx", "head"),
            P("head"),
            P("head", None),
            P("head", None),
            P("head", None),
        ),
        out_specs=P(("ctx", "head"), None),
        check_vma=False,
    )
```

```python
import functools

import jax
import jax.numpy as jnp
from jax import lax
from jax.experimental import pallas as pl
from jax.experimental.pallas import tpu as pltpu
from jax.sharding import PartitionSpec as P

HEAD = 128
ROWS = 128
HALF = 64
SLOTS = 24
LISTED = 8
BANDS = 3
BLOCKS = 128
RUNS = 4
HEADS = 8
TOKENS = RUNS * ROWS
SCALE = HEAD ** -0.5
FACTOR = SCALE * 1.4426950408889634
NEVER = 1 << 20
LOW = -1e30
Z, Y, X = 8, 4, 4
BF16, F32 = jnp.bfloat16, jnp.float32
SLOT, BASE, BAND, BAND_BASE, META = 0, 64, 128, 152, 248
TABLE = 256


def z_pairs(step):
    return [(Y * z + y, Y * ((z + step) % Z) + y) for z in range(Z) for y in range(Y)]


def y_pairs(flip):
    return [(Y * z + y, Y * z + (y ^ flip)) for z in range(Z) for y in range(Y)]


def x_pairs(step):
    return [(2 * x + k, 2 * ((x + step) % X) + k) for x in range(X) for k in range(2)]


CORE_PAIRS = [(h, h ^ 1) for h in range(HEADS)]


class Copies:
    def __init__(self, sems):
        self.sems, self.made = sems, []

    def start(self, src, dst):
        made = pltpu.make_async_copy(src, dst, self.sems.at[len(self.made)])
        made.start()
        self.made.append(made)

    def wait(self, count=None):
        for made in self.made[:count]:
            made.wait()
        self.made = [] if count is None else self.made[count:]


def key_places(table, late):
    z, y_half = table[META + 3], table[META + 4]
    n = lax.broadcasted_iota(jnp.int32, (1, HALF), 1)
    part, inner, row = n // 32, (n // 8) % 4, n % 8
    step = jnp.where(inner < 2, -1 - 2 * inner, 2 * inner - 3) if late else 2 * inner
    z_of = (z + step + Z) % Z
    return (z_of * 2 + (y_half ^ part)) * 8 + row


def load_half(copies, odd, own, far, near, cross, kv):
    for kind, parts in ((odd, (own, far)), (1 - odd, (near, cross))):
        for p, part in enumerate(parts):
            copies.start(part, kv.at[kind, :, pl.ds(32 * p, 32)])


def listed(table, kv, kind, h):
    return jnp.concatenate([kv[kind, table[SLOT + h * LISTED + e]] for e in range(LISTED)], axis=0)


def limits(table, places, h):
    return jnp.concatenate([places + table[BASE + h * LISTED + e] for e in range(LISTED)], axis=1)


def product(q, keys):
    return lax.dot_general(q, keys, (((1,), (1,)), ((), ())), preferred_element_type=F32)


def early_kernel(table, sink, q, w, a0, a2, a1, a3, kp, vp, kc, vc, acc, tops, sums, w_out, kv, band, qs, sems):
    copies = Copies(sems)
    copies.start(q, qs)
    for kind, (prev, cur) in enumerate(((kp, kc), (vp, vc))):
        copies.start(prev, band.at[kind, pl.ds(0, RUNS)])
        copies.start(cur, band.at[kind, pl.ds(RUNS, RUNS)])
    load_half(copies, table[META], a0, a2, a1, a3, kv)
    first = len(copies.made)
    copies.start(w, w_out)
    copies.wait(first)
    token = table[META + 2] + lax.broadcasted_iota(jnp.int32, (TOKENS, 1), 0)
    places = key_places(table, False)
    within = lax.broadcasted_iota(jnp.int32, (1, ROWS), 1)
    for h in range(HEADS):
        cols = slice(h * HEAD, (h + 1) * HEAD)
        qh = qs[:, cols]
        score = product(qh, listed(table, kv, 0, h))
        score = jnp.where(token >= limits(table, places, h), score, LOW)
        near = []
        for run in range(RUNS):
            rows = slice(run * ROWS, (run + 1) * ROWS)
            keys = jnp.concatenate([band[0, table[BAND + h * BANDS + j] + run] for j in range(BANDS)], axis=0)
            limit = jnp.concatenate(
                [within + table[BAND_BASE + (run * HEADS + h) * BANDS + j] for j in range(BANDS)], axis=1)
            near.append(jnp.where(token[rows] >= limit, product(qh[rows], keys), LOW))
        near = jnp.concatenate(near, axis=0)
        raw_sink = sink[h]
        top = jnp.maximum(jnp.max(score, axis=1, keepdims=True), jnp.max(near, axis=1, keepdims=True))
        top = jnp.maximum(top, raw_sink)
        weight = jnp.exp2((score - top) * FACTOR)
        near = jnp.exp2((near - top) * FACTOR)
        total = jnp.sum(weight, axis=1, keepdims=True) + jnp.sum(near, axis=1, keepdims=True)
        total = total + jnp.exp2((raw_sink - top) * FACTOR)
        mixed = jnp.dot(weight.astype(BF16), listed(table, kv, 1, h), preferred_element_type=F32)
        near = near.astype(BF16)
        for run in range(RUNS):
            rows = slice(run * ROWS, (run + 1) * ROWS)
            vals = jnp.concatenate([band[1, table[BAND + h * BANDS + j] + run] for j in range(BANDS)], axis=0)
            acc[rows, cols] = mixed[rows] + jnp.dot(near[rows], vals, preferred_element_type=F32)
        tops[:, h:h + 1] = top
        sums[:, h:h + 1] = total
    copies.wait()


def project(att, w, blocks, core, keeps, give):
    def rows(block, side):
        start = pl.multiple_of(block * ROWS + side * HALF, HALF)
        return att[pl.ds(start, HALF), :]

    lhs = jnp.concatenate([rows(b, core) for b in blocks] + [rows(b, 1 - core) for b in blocks], axis=0)
    tile = 512
    for n in range(w.shape[1] // tile):
        cols = slice(n * tile, (n + 1) * tile)
        out = jnp.dot(lhs, w[:, cols], preferred_element_type=F32).astype(BF16)
        for i, keep in enumerate(keeps):
            keep[:, cols] = out[i * HALF:(i + 1) * HALF]
        give[:, cols] = out[len(blocks) * HALF:]


def late_kernel(table, q, w, b0, b2, b1, b3, acc, tops, sums, att, keep, give, kv, qs, sems):
    copies = Copies(sems)
    copies.start(q, qs)
    load_half(copies, table[META], b0, b2, b1, b3, kv)
    copies.wait()
    token = table[META + 2] + lax.broadcasted_iota(jnp.int32, (TOKENS, 1), 0)
    places = key_places(table, True)
    for h in range(HEADS):
        cols = slice(h * HEAD, (h + 1) * HEAD)
        score = product(qs[:, cols], listed(table, kv, 0, h))
        score = jnp.where(token >= limits(table, places, h), score, LOW)
        before = tops[:, h:h + 1]
        top = jnp.maximum(jnp.max(score, axis=1, keepdims=True), before)
        weight = jnp.exp2((score - top) * FACTOR)
        fade = jnp.exp2((before - top) * FACTOR)
        total = jnp.sum(weight, axis=1, keepdims=True) + fade * sums[:, h:h + 1]
        mixed = jnp.dot(weight.astype(BF16), listed(table, kv, 1, h), preferred_element_type=F32)
        att[:, cols] = ((mixed + acc[:, cols] * fade) * (1.0 / total)).astype(BF16)
    project(att, w, [(table[META + 5] + 2) % X], table[META + 1], [keep], give)


def sides_kernel(table, att, w, keep_below, keep_above, give):
    x = table[META + 5]
    project(att, w, [(x + 1) % X, (x + 3) % X], table[META + 1], [keep_below, keep_above], give)


def own_kernel(table, att, w, after, keep, give):
    project(att, w, [table[META + 5]], table[META + 1], [keep], give)


SMEM = pl.BlockSpec(memory_space=pltpu.SMEM)
VMEM = pl.BlockSpec(memory_space=pltpu.VMEM)
ANY = pl.BlockSpec(memory_space=pl.ANY)


def call(body, ins, outs, scratch, micros, name):
    return pl.pallas_call(
        body,
        out_shape=tuple(pltpu.VMEM(shape, dtype) for shape, dtype in outs),
        in_specs=ins,
        out_specs=(VMEM,) * len(outs),
        scratch_shapes=scratch,
        compiler_params=pltpu.CompilerParams(vmem_limit_bytes=24 * 2 ** 20),
        cost_estimate=pl.CostEstimate(flops=int(micros * 1e9), bytes_accessed=2 ** 20, transcendentals=0),
        name=name,
    )


def total_of(*terms):
    return functools.reduce(lambda a, b: a + b, [t.astype(F32) for t in terms]).astype(BF16)


def tables(c, x, core, vert_blocks, slash_offsets):
    block = jnp.arange(BLOCKS, dtype=jnp.int32)
    ids = vert_blocks.reshape(-1)
    present = jnp.any(ids[:, None] == block[None, :], axis=0).astype(jnp.int32)
    rank = jnp.sum(jnp.where(block[:, None] > block[None, :], present[None, :], 0), axis=1)
    place = jnp.where(present > 0, rank, -1)
    slot = jnp.sum(jnp.where(ids[:, None] > block[None, :], present[None, :], 0), axis=1)
    slot = jnp.where(ids >= 0, slot, 0)
    base = jnp.where(ids >= 0, ids * ROWS, NEVER)
    run = jnp.arange(RUNS, dtype=jnp.int32)
    near = RUNS * c + run[:, None, None] - slash_offsets[None]
    dup = jnp.any(near[:, :, :, None] == vert_blocks[None, :, None, :], axis=3)
    near = jnp.where((near >= 0) & jnp.logical_not(dup), near * ROWS, NEVER)
    meta = jnp.stack([c % 2, core, TOKENS * c, c // Y, (c % Y) // 2, x, x * 0, x * 0]).astype(jnp.int32)
    parts = [slot, base, RUNS - slash_offsets.reshape(-1), near.reshape(-1), meta]
    return place, jnp.concatenate(parts)


def per_device(queries, keys, values, sink_logits, vert_blocks, slash_offsets, output_weight):
    c = lax.axis_index("ctx")
    h = lax.axis_index("head")
    x, core = h // 2, h % 2
    keys = keys.reshape(RUNS, ROWS, HEAD)
    values = values.reshape(RUNS, ROWS, HEAD)
    place, table = tables(c, x, core, vert_blocks, slash_offsets)

    def slices(a):
        return jnp.transpose(a.reshape(RUNS, 16, 8, HEAD), (1, 0, 2, 3))

    spread = jnp.stack([slices(keys), slices(values)], axis=1).reshape(Z * Y, RUNS * 8, HEAD)
    got = lax.all_to_all(spread, "ctx", 0, 0, tiled=True).reshape(BLOCKS * 8, HEAD)
    r = jnp.arange(SLOTS * 8, dtype=jnp.int32)[:, None]
    col = jnp.arange(BLOCKS * 8, dtype=jnp.int32)[None, :]
    pick = (jnp.repeat(place, 8)[None, :] == r // 8) & (col % 8 == r % 8)
    mine = jnp.dot(pick.astype(BF16), got, preferred_element_type=F32)
    mine = mine.astype(BF16).reshape(SLOTS, 8, HEAD)

    def from_z(a, offset):
        return lax.ppermute(a, "ctx", z_pairs(-offset))

    z2, z4, z6 = from_z(mine, 2), from_z(mine, 4), from_z(mine, 6)
    keys_late, values_late, z4 = lax.optimization_barrier((keys, values, z4))
    step = [(s, s + 1) for s in range(Z * Y - 1)]
    k_prev = lax.ppermute(keys_late, "ctx", step)
    v_prev = lax.ppermute(values_late, "ctx", step)
    a0 = jnp.concatenate([mine, z2, z4, z6], axis=1)
    low = from_z(jnp.concatenate([mine, z6], axis=1), -1)
    high = from_z(jnp.concatenate([mine, z2], axis=1), 1)
    b0 = jnp.concatenate([low, high], axis=1)
    a1, a2, a3 = [lax.ppermute(a0, "ctx", y_pairs(f)) for f in (1, 2, 3)]
    b1, b2, b3 = [lax.ppermute(b0, "ctx", y_pairs(f)) for f in (1, 2, 3)]

    width = output_weight.shape[1]
    kv = pltpu.VMEM((2, SLOTS, HALF, HEAD), BF16)
    held = pltpu.VMEM((TOKENS, HEADS * HEAD), BF16)
    part = ((HALF, width), BF16)
    far_queries = pltpu.with_memory_space_constraint(queries, pltpu.HBM)
    far_weight = pltpu.with_memory_space_constraint(output_weight, pltpu.HBM)
    acc, tops, sums, w = call(
        early_kernel, [SMEM, SMEM] + [ANY] * 10,
        [((TOKENS, HEADS * HEAD), F32), ((TOKENS, HEADS), F32), ((TOKENS, HEADS), F32), (output_weight.shape, BF16)],
        [kv, pltpu.VMEM((2, 2 * RUNS, ROWS, HEAD), BF16), held, pltpu.SemaphoreType.DMA((10,))], 8, "early",
    )(table, sink_logits * (1.0 / SCALE), far_queries, far_weight, a0, a2, a1, a3, k_prev, v_prev,
      *[pltpu.with_memory_space_constraint(a, pltpu.HBM) for a in (keys, values)])
    att, keep_far, give_far = call(
        late_kernel, [SMEM, ANY, VMEM] + [ANY] * 4 + [VMEM] * 3,
        [((TOKENS, HEADS * HEAD), BF16), part, part],
        [kv, held, pltpu.SemaphoreType.DMA((5,))], 1, "late",
    )(table, far_queries, w, b0, b2, b1, b3, acc, tops, sums)
    keep_below, keep_above, give_sides = call(
        sides_kernel, [SMEM, VMEM, VMEM], [part, part, ((2 * HALF, width), BF16)], [], 1, "sides",
    )(table, att, w)
    keep_own, give_own = call(
        own_kernel, [SMEM, VMEM, VMEM, ANY], [part, part], [], 1, "own",
    )(table, att, w, keep_below)

    def swap(a):
        return lax.ppermute(a, "head", CORE_PAIRS)

    def to_x(a, step):
        return lax.ppermute(a, "head", x_pairs(step))

    far, sides, own = swap(give_far), swap(give_sides), swap(give_own)
    below, above = sides[:HALF], sides[HALF:]
    mid = width // 2
    relay_left = to_x(total_of(keep_far[:, :mid], far[:, :mid]), 1)
    relay_right = to_x(total_of(keep_far[:, mid:], far[:, mid:]), -1)
    right_below = to_x(total_of(keep_below[:, mid:], below[:, mid:]), 1)
    left_above = to_x(total_of(keep_above[:, :mid], above[:, :mid]), -1)
    keep_below, keep_above, sides, relay_left, relay_right = lax.optimization_barrier(
        (keep_below, keep_above, sides, relay_left, relay_right))
    below, above = sides[:HALF], sides[HALF:]
    left_below = to_x(total_of(keep_below[:, :mid], below[:, :mid], relay_left), 1)
    right_above = to_x(total_of(keep_above[:, mid:], above[:, mid:], relay_right), -1)
    out_left = total_of(keep_own[:, :mid], own[:, :mid], left_below, left_above)
    out_right = total_of(keep_own[:, mid:], own[:, mid:], right_below, right_above)
    return jnp.concatenate([out_left, out_right], axis=1)


def solution(mesh):
    return jax.shard_map(
        per_device,
        mesh=mesh,
        in_specs=(
            P("ctx", "head"),
            P("ctx", "head"),
            P("ctx", "head"),
            P("head"),
            P("head", None),
            P("head", None),
            P("head", None),
        ),
        out_specs=P(("ctx", "head"), None),
        check_vma=False,
    )
```

```python
import functools

import jax
import jax.numpy as jnp
from jax import lax
from jax.experimental import pallas as pl
from jax.experimental.pallas import tpu as pltpu
from jax.sharding import PartitionSpec as P

HEAD = 128
ROWS = 128
HALF = 64
SLOTS = 24
LISTED = 8
BANDS = 3
BLOCKS = 128
RUNS = 4
HEADS = 8
TOKENS = RUNS * ROWS
SCALE = HEAD ** -0.5
FACTOR = SCALE * 1.4426950408889634
NEVER = 1 << 20
LOW = -1e30
Z, Y, X = 8, 4, 4
BF16, F32 = jnp.bfloat16, jnp.float32
SLOT, BASE, BAND, BAND_BASE, META = 0, 64, 128, 152, 248
TABLE = 256


def z_pairs(step):
    return [(Y * z + y, Y * ((z + step) % Z) + y) for z in range(Z) for y in range(Y)]


def y_pairs(flip):
    return [(Y * z + y, Y * z + (y ^ flip)) for z in range(Z) for y in range(Y)]


def x_pairs(step):
    return [(2 * x + k, 2 * ((x + step) % X) + k) for x in range(X) for k in range(2)]


CORE_PAIRS = [(h, h ^ 1) for h in range(HEADS)]


class Copies:
    def __init__(self, sems):
        self.sems, self.made = sems, []

    def start(self, src, dst):
        made = pltpu.make_async_copy(src, dst, self.sems.at[len(self.made)])
        made.start()
        self.made.append(made)

    def wait(self, count=None):
        for made in self.made[:count]:
            made.wait()
        self.made = [] if count is None else self.made[count:]


def key_places(table, late):
    z, y_half = table[META + 3], table[META + 4]
    n = lax.broadcasted_iota(jnp.int32, (1, HALF), 1)
    part, inner, row = n // 32, (n // 8) % 4, n % 8
    step = jnp.where(inner < 2, -1 - 2 * inner, 2 * inner - 3) if late else 2 * inner
    z_of = (z + step + Z) % Z
    return (z_of * 2 + (y_half ^ part)) * 8 + row


def load_half(copies, odd, own, far, near, cross, kv):
    for kind, parts in ((odd, (own, far)), (1 - odd, (near, cross))):
        for p, part in enumerate(parts):
            copies.start(part, kv.at[kind, :, pl.ds(32 * p, 32)])


def listed(table, kv, kind, h):
    return jnp.concatenate([kv[kind, table[SLOT + h * LISTED + e]] for e in range(LISTED)], axis=0)


def limits(table, places, h):
    return jnp.concatenate([places + table[BASE + h * LISTED + e] for e in range(LISTED)], axis=1)


def product(q, keys):
    return lax.dot_general(q, keys, (((1,), (1,)), ((), ())), preferred_element_type=F32)


def wide(column):
    return jnp.broadcast_to(column, (column.shape[0], HEAD))


def across(column_block, count):
    return jnp.concatenate([column_block] * count, axis=1)


def early_kernel(table, sink, q, w, a0, a2, a1, a3, prev, kc, vc, acc, tops, sums, w_out, kv, band, qs, sems):
    copies = Copies(sems)
    copies.start(q, qs)
    for kind, cur in enumerate((kc, vc)):
        copies.start(cur, band.at[kind, pl.ds(RUNS, RUNS)])
    load_half(copies, table[META], a0, a2, a1, a3, kv)
    first = len(copies.made)
    depth = w.shape[0] // 4
    for n in range(4):
        copies.start(w.at[pl.ds(n * depth, depth)], w_out.at[pl.ds(n * depth, depth)])
    for kind in range(2):
        for b in range(RUNS):
            rows = [prev[r, kind, b].astype(F32) for r in range(16)]
            band[kind, b] = jnp.concatenate(rows, axis=0).astype(BF16)
    copies.wait(first)
    token = table[META + 2] + lax.broadcasted_iota(jnp.int32, (TOKENS, 1), 0)
    places = key_places(table, False)
    within = lax.broadcasted_iota(jnp.int32, (1, ROWS), 1)
    for h in range(HEADS):
        cols = slice(h * HEAD, (h + 1) * HEAD)
        qh = qs[:, cols]
        score = product(qh, listed(table, kv, 0, h))
        score = jnp.where(token >= limits(table, places, h), score, LOW)
        near = []
        for run in range(RUNS):
            rows = slice(run * ROWS, (run + 1) * ROWS)
            keys = jnp.concatenate([band[0, table[BAND + h * BANDS + j] + run] for j in range(BANDS)], axis=0)
            limit = jnp.concatenate(
                [within + table[BAND_BASE + (run * HEADS + h) * BANDS + j] for j in range(BANDS)], axis=1)
            near.append(jnp.where(token[rows] >= limit, product(qh[rows], keys), LOW))
        near = jnp.concatenate(near, axis=0)
        raw_sink = sink[h]
        top = jnp.maximum(jnp.max(score, axis=1, keepdims=True), jnp.max(near, axis=1, keepdims=True))
        top = jnp.maximum(top, raw_sink)
        weight = jnp.exp2((score - top) * FACTOR)
        near = jnp.exp2((near - top) * FACTOR)
        total = jnp.sum(weight, axis=1, keepdims=True) + jnp.sum(near, axis=1, keepdims=True)
        total = total + jnp.exp2((raw_sink - top) * FACTOR)
        mixed = jnp.dot(weight.astype(BF16), listed(table, kv, 1, h), preferred_element_type=F32)
        near = near.astype(BF16)
        for run in range(RUNS):
            rows = slice(run * ROWS, (run + 1) * ROWS)
            vals = jnp.concatenate([band[1, table[BAND + h * BANDS + j] + run] for j in range(BANDS)], axis=0)
            acc[rows, cols] = mixed[rows] + jnp.dot(near[rows], vals, preferred_element_type=F32)
        tops[:, cols] = wide(top)
        sums[:, cols] = wide(total)
    copies.wait()


def project(att, w, blocks, core, keeps, give):
    def rows(block, side):
        start = pl.multiple_of(block * ROWS + side * HALF, HALF)
        return att[pl.ds(start, HALF), :]

    lhs = jnp.concatenate([rows(b, core) for b in blocks] + [rows(b, 1 - core) for b in blocks], axis=0)
    tile = 512
    for n in range(w.shape[1] // tile):
        cols = slice(n * tile, (n + 1) * tile)
        out = jnp.dot(lhs, w[:, cols], preferred_element_type=F32).astype(BF16)
        for i, keep in enumerate(keeps):
            keep[:, cols] = out[i * HALF:(i + 1) * HALF]
        give(n * tile, tile, out[len(blocks) * HALF:])


def late_kernel(table, q, w, b0, b2, b1, b3, acc, tops, sums, att, keep, give, kv, qs, sems):
    copies = Copies(sems)
    copies.start(q, qs)
    load_half(copies, table[META], b0, b2, b1, b3, kv)
    copies.wait()
    token = table[META + 2] + lax.broadcasted_iota(jnp.int32, (TOKENS, 1), 0)
    places = key_places(table, True)
    for h in range(HEADS):
        cols = slice(h * HEAD, (h + 1) * HEAD)
        score = product(qs[:, cols], listed(table, kv, 0, h))
        score = jnp.where(token >= limits(table, places, h), score, LOW)
        before = tops[:, cols]
        top = jnp.maximum(wide(jnp.max(score, axis=1, keepdims=True)), before)
        weight = jnp.exp2((score - across(top, LISTED * HALF // HEAD)) * FACTOR)
        fade = jnp.exp2((before - top) * FACTOR)
        total = wide(jnp.sum(weight, axis=1, keepdims=True)) + fade * sums[:, cols]
        mixed = jnp.dot(weight.astype(BF16), listed(table, kv, 1, h), preferred_element_type=F32)
        att[:, cols] = ((mixed + acc[:, cols] * fade) * (1.0 / total)).astype(BF16)
    project(att, w, [(table[META + 5] + 2) % X], table[META + 1], [keep], functools.partial(store, give))


def store(give, start, size, rows):
    give[:, start:start + size] = rows


def sides_kernel(table, att, w, keep_below, keep_above, direct, relayed):
    x, mid = table[META + 5], w.shape[1] // 2

    def give(start, size, rows):
        below, above = rows[:HALF], rows[HALF:]
        at = slice(start % mid, start % mid + size)
        if start < mid:
            relayed[:HALF, at], direct[HALF:, at] = below, above
        else:
            direct[:HALF, at], relayed[HALF:, at] = below, above

    project(att, w, [(x + 1) % X, (x + 3) % X], table[META + 1], [keep_below, keep_above], give)


def own_kernel(table, att, w, after, keep, give):
    project(att, w, [table[META + 5]], table[META + 1], [keep], functools.partial(store, give))


def final_kernel(keep, swapped, left_below, left_above, right_below, right_above, out):
    mid = out.shape[1] // 2
    for start, pair in ((0, (left_below, left_above)), (mid, (right_below, right_above))):
        cols = slice(start, start + mid)
        total = keep[:, cols].astype(F32) + swapped[:, cols].astype(F32)
        for part in pair:
            total = total + part[...].astype(F32)
        out[:, cols] = total.astype(BF16)


SMEM = pl.BlockSpec(memory_space=pltpu.SMEM)
VMEM = pl.BlockSpec(memory_space=pltpu.VMEM)
ANY = pl.BlockSpec(memory_space=pl.ANY)


def call(body, ins, outs, scratch, micros, name):
    return pl.pallas_call(
        body,
        out_shape=tuple(pltpu.VMEM(shape, dtype) for shape, dtype in outs),
        in_specs=ins,
        out_specs=(VMEM,) * len(outs),
        scratch_shapes=scratch,
        compiler_params=pltpu.CompilerParams(vmem_limit_bytes=24 * 2 ** 20),
        cost_estimate=pl.CostEstimate(flops=int(micros * 1e9), bytes_accessed=2 ** 20, transcendentals=0),
        name=name,
    )


def total_of(*terms):
    return functools.reduce(lambda a, b: a + b, [t.astype(F32) for t in terms]).astype(BF16)


def tables(c, x, core, vert_blocks, slash_offsets):
    block = jnp.arange(BLOCKS, dtype=jnp.int32)
    ids = vert_blocks.reshape(-1)
    present = jnp.any(ids[:, None] == block[None, :], axis=0).astype(jnp.int32)
    rank = jnp.sum(jnp.where(block[:, None] > block[None, :], present[None, :], 0), axis=1)
    place = jnp.where(present > 0, rank, -1)
    slot = jnp.sum(jnp.where(ids[:, None] > block[None, :], present[None, :], 0), axis=1)
    slot = jnp.where(ids >= 0, slot, 0)
    base = jnp.where(ids >= 0, ids * ROWS, NEVER)
    run = jnp.arange(RUNS, dtype=jnp.int32)
    near = RUNS * c + run[:, None, None] - slash_offsets[None]
    dup = jnp.any(near[:, :, :, None] == vert_blocks[None, :, None, :], axis=3)
    near = jnp.where((near >= 0) & jnp.logical_not(dup), near * ROWS, NEVER)
    meta = jnp.stack([c % 2, core, TOKENS * c, c // Y, (c % Y) // 2, x, x * 0, x * 0]).astype(jnp.int32)
    parts = [slot, base, RUNS - slash_offsets.reshape(-1), near.reshape(-1), meta]
    return place, jnp.concatenate(parts)


def per_device(queries, keys, values, sink_logits, vert_blocks, slash_offsets, output_weight):
    c = lax.axis_index("ctx")
    h = lax.axis_index("head")
    x, core = h // 2, h % 2
    keys = keys.reshape(RUNS, ROWS, HEAD)
    values = values.reshape(RUNS, ROWS, HEAD)
    place, table = tables(c, x, core, vert_blocks, slash_offsets)

    def slices(a):
        return jnp.transpose(a.reshape(RUNS, 16, 8, HEAD), (1, 0, 2, 3))

    spread = jnp.stack([slices(keys), slices(values)], axis=1).reshape(Z * Y, RUNS * 8, HEAD)
    prev = lax.ppermute(spread, "ctx", [(s, s + 1) for s in range(Z * Y - 1)]).reshape(16, 2, RUNS, 8, HEAD)
    got = lax.all_to_all(spread, "ctx", 0, 0, tiled=True).reshape(BLOCKS * 8, HEAD)
    r = jnp.arange(SLOTS * 8, dtype=jnp.int32)[:, None]
    col = jnp.arange(BLOCKS * 8, dtype=jnp.int32)[None, :]
    pick = (jnp.repeat(place, 8)[None, :] == r // 8) & (col % 8 == r % 8)
    mine = jnp.dot(pick.astype(BF16), got, preferred_element_type=F32)
    mine = mine.astype(BF16).reshape(SLOTS, 8, HEAD)

    def from_z(a, offset):
        return lax.ppermute(a, "ctx", z_pairs(-offset))

    z2, z4, z6 = from_z(mine, 2), from_z(mine, 4), from_z(mine, 6)
    a0 = jnp.concatenate([mine, z2, z4, z6], axis=1)
    low = from_z(jnp.concatenate([mine, z6], axis=1), -1)
    high = from_z(jnp.concatenate([mine, z2], axis=1), 1)
    b0 = jnp.concatenate([low, high], axis=1)
    a1, a2, a3 = [lax.ppermute(a0, "ctx", y_pairs(f)) for f in (1, 2, 3)]
    b1, b2, b3 = [lax.ppermute(b0, "ctx", y_pairs(f)) for f in (1, 2, 3)]

    width = output_weight.shape[1]
    kv = pltpu.VMEM((2, SLOTS, HALF, HEAD), BF16)
    held = pltpu.VMEM((TOKENS, HEADS * HEAD), BF16)
    part = ((HALF, width), BF16)
    far_queries = pltpu.with_memory_space_constraint(queries, pltpu.HBM)
    far_weight = pltpu.with_memory_space_constraint(output_weight, pltpu.HBM)
    acc, tops, sums, w = call(
        early_kernel, [SMEM, SMEM] + [ANY] * 6 + [VMEM, ANY, ANY],
        [((TOKENS, HEADS * HEAD), F32)] * 3 + [(output_weight.shape, BF16)],
        [kv, pltpu.VMEM((2, 2 * RUNS, ROWS, HEAD), BF16), held, pltpu.SemaphoreType.DMA((11,))], 8, "early",
    )(table, sink_logits * (1.0 / SCALE), far_queries, far_weight, a0, a2, a1, a3, prev,
      *[pltpu.with_memory_space_constraint(a, pltpu.HBM) for a in (keys, values)])
    att, keep_far, give_far = call(
        late_kernel, [SMEM, ANY, VMEM] + [ANY] * 4 + [VMEM] * 3,
        [((TOKENS, HEADS * HEAD), BF16), part, part],
        [kv, held, pltpu.SemaphoreType.DMA((5,))], 1, "late",
    )(table, far_queries, w, b0, b2, b1, b3, acc, tops, sums)
    halves = ((2 * HALF, width // 2), BF16)
    keep_below, keep_above, give_direct, give_relayed = call(
        sides_kernel, [SMEM, VMEM, VMEM], [part, part, halves, halves], [], 1, "sides",
    )(table, att, w)
    def swap(a):
        return lax.ppermute(a, "head", CORE_PAIRS)

    def to_x(a, step):
        return lax.ppermute(a, "head", x_pairs(step))

    far, direct, relayed = swap(give_far), swap(give_direct), swap(give_relayed)
    mid = width // 2
    far_left = total_of(keep_far[:, :mid], far[:, :mid])
    far_right = total_of(keep_far[:, mid:], far[:, mid:])
    relay_left, relay_right = to_x(far_left, 1), to_x(far_right, -1)
    keep_own, give_own = call(
        own_kernel, [SMEM, VMEM, VMEM, ANY], [part, part], [], 1, "own",
    )(table, att, w, far_left)

    own = swap(give_own)
    right_below = to_x(total_of(keep_below[:, mid:], direct[:HALF]), 1)
    left_above = to_x(total_of(keep_above[:, :mid], direct[HALF:]), -1)
    keep_below, keep_above, relayed, relay_left, relay_right = lax.optimization_barrier(
        (keep_below, keep_above, relayed, relay_left, relay_right))
    left_below = to_x(total_of(keep_below[:, :mid], relayed[:HALF], relay_left), 1)
    right_above = to_x(total_of(keep_above[:, mid:], relayed[HALF:], relay_right), -1)
    return pl.pallas_call(
        final_kernel,
        out_shape=jax.ShapeDtypeStruct((HALF, width), BF16),
        in_specs=[VMEM] * 6,
        out_specs=VMEM,
        compiler_params=pltpu.CompilerParams(vmem_limit_bytes=8 * 2 ** 20),
        name="final",
    )(keep_own, own, left_below, left_above, right_below, right_above)


def solution(mesh):
    return jax.shard_map(
        per_device,
        mesh=mesh,
        in_specs=(
            P("ctx", "head"),
            P("ctx", "head"),
            P("ctx", "head"),
            P("head"),
            P("head", None),
            P("head", None),
            P("head", None),
        ),
        out_specs=P(("ctx", "head"), None),
        check_vma=False,
    )
```

```python
import functools

import jax
import jax.numpy as jnp
from jax import lax
from jax.experimental import pallas as pl
from jax.experimental.pallas import tpu as pltpu
from jax.sharding import PartitionSpec as P

HEAD = 128
ROWS = 128
HALF = 64
SLOTS = 24
LISTED = 8
BANDS = 3
BLOCKS = 128
RUNS = 4
HEADS = 8
TOKENS = RUNS * ROWS
SCALE = HEAD ** -0.5
FACTOR = SCALE * 1.4426950408889634
NEVER = 1 << 20
LOW = -1e30
Z, Y, X = 8, 4, 4
BF16, F32 = jnp.bfloat16, jnp.float32
META = BLOCKS


def z_pairs(step):
    return [(Y * z + y, Y * ((z + step) % Z) + y) for z in range(Z) for y in range(Y)]


def y_pairs(flip):
    return [(Y * z + y, Y * z + (y ^ flip)) for z in range(Z) for y in range(Y)]


def x_pairs(step):
    return [(2 * x + k, 2 * ((x + step) % X) + k) for x in range(X) for k in range(2)]


CORE_PAIRS = [(h, h ^ 1) for h in range(HEADS)]


class Copies:
    def __init__(self, sems):
        self.sems, self.made = sems, []

    def start(self, src, dst):
        made = pltpu.make_async_copy(src, dst, self.sems.at[len(self.made)])
        made.start()
        self.made.append(made)

    def wait(self, count=None):
        for made in self.made[:count]:
            made.wait()
        self.made = [] if count is None else self.made[count:]


def key_places(table, late):
    z, y_half = table[META + 3], table[META + 4]
    n = lax.broadcasted_iota(jnp.int32, (1, HALF), 1)
    part, inner, row = n // 32, (n // 8) % 4, n % 8
    step = jnp.where(inner < 2, -1 - 2 * inner, 2 * inner - 3) if late else 2 * inner
    z_of = (z + step + Z) % Z
    return (z_of * 2 + (y_half ^ part)) * 8 + row


def load_half(copies, odd, own, far, near, cross, kv):
    for kind, parts in ((odd, (own, far)), (1 - odd, (near, cross))):
        for p, part in enumerate(parts):
            copies.start(part, kv.at[kind, :, pl.ds(32 * p, 32)])


def slots_of(table, vert, h):
    return [table[jnp.maximum(vert[h, e], 0)] for e in range(LISTED)]


def listed(kv, kind, slots):
    return jnp.concatenate([kv[kind, slot] for slot in slots], axis=0)


def limits(vert, places, h):
    ids = [vert[h, e] for e in range(LISTED)]
    return jnp.concatenate([places + jnp.where(i >= 0, i * ROWS, NEVER) for i in ids], axis=1)


def near_base(table, vert, slash, h, run, j):
    block = table[META + 2] + run - slash[h, j]
    use = block >= 0
    for e in range(LISTED):
        use = jnp.logical_and(use, vert[h, e] != block)
    return jnp.where(use, block * ROWS, NEVER)


def product(q, keys):
    return lax.dot_general(q, keys, (((1,), (1,)), ((), ())), preferred_element_type=F32)


def wide(column):
    return jnp.broadcast_to(column, (column.shape[0], HEAD))


def across(column_block, count):
    return jnp.concatenate([column_block] * count, axis=1)


def early_kernel(table, vert, slash, sink, q, w, a0, a2, a1, a3, prev, kc, vc, acc, tops, sums, w_out, qs, kv, band, sems):
    copies = Copies(sems)
    copies.start(q, qs)
    for kind, cur in enumerate((kc, vc)):
        copies.start(cur, band.at[kind, pl.ds(RUNS, RUNS)])
    load_half(copies, table[META], a0, a2, a1, a3, kv)
    first = len(copies.made)
    depth = w.shape[0] // 4
    for n in range(4):
        copies.start(w.at[pl.ds(n * depth, depth)], w_out.at[pl.ds(n * depth, depth)])
    for kind in range(2):
        for b in range(RUNS):
            rows = [prev[r, kind, b].astype(F32) for r in range(16)]
            band[kind, b] = jnp.concatenate(rows, axis=0).astype(BF16)
    copies.wait(first)
    token = TOKENS // RUNS * table[META + 2] + lax.broadcasted_iota(jnp.int32, (TOKENS, 1), 0)
    places = key_places(table, False)
    within = lax.broadcasted_iota(jnp.int32, (1, ROWS), 1)
    for h in range(HEADS):
        cols = slice(h * HEAD, (h + 1) * HEAD)
        qh = qs[:, cols]
        slots = slots_of(table, vert, h)
        score = product(qh, listed(kv, 0, slots))
        score = jnp.where(token >= limits(vert, places, h), score, LOW)
        near = []
        for run in range(RUNS):
            rows = slice(run * ROWS, (run + 1) * ROWS)
            keys = jnp.concatenate([band[0, RUNS + run - slash[h, j]] for j in range(BANDS)], axis=0)
            limit = jnp.concatenate(
                [within + near_base(table, vert, slash, h, run, j) for j in range(BANDS)], axis=1)
            near.append(jnp.where(token[rows] >= limit, product(qh[rows], keys), LOW))
        near = jnp.concatenate(near, axis=0)
        raw_sink = sink[h] * (1.0 / SCALE)
        top = jnp.maximum(jnp.max(score, axis=1, keepdims=True), jnp.max(near, axis=1, keepdims=True))
        top = jnp.maximum(top, raw_sink)
        weight = jnp.exp2((score - top) * FACTOR)
        near = jnp.exp2((near - top) * FACTOR)
        total = jnp.sum(weight, axis=1, keepdims=True) + jnp.sum(near, axis=1, keepdims=True)
        total = total + jnp.exp2((raw_sink - top) * FACTOR)
        mixed = jnp.dot(weight.astype(BF16), listed(kv, 1, slots), preferred_element_type=F32)
        near = near.astype(BF16)
        for run in range(RUNS):
            rows = slice(run * ROWS, (run + 1) * ROWS)
            vals = jnp.concatenate([band[1, RUNS + run - slash[h, j]] for j in range(BANDS)], axis=0)
            acc[rows, cols] = mixed[rows] + jnp.dot(near[rows], vals, preferred_element_type=F32)
        tops[:, cols] = wide(top)
        sums[:, cols] = wide(total)
    copies.wait()


def project(att, w, blocks, core, keeps, give):
    def rows(block, side):
        start = pl.multiple_of(block * ROWS + side * HALF, HALF)
        return att[pl.ds(start, HALF), :]

    lhs = jnp.concatenate([rows(b, core) for b in blocks] + [rows(b, 1 - core) for b in blocks], axis=0)
    tile = 512
    for n in range(w.shape[1] // tile):
        cols = slice(n * tile, (n + 1) * tile)
        out = jnp.dot(lhs, w[:, cols], preferred_element_type=F32).astype(BF16)
        for i, keep in enumerate(keeps):
            keep[:, cols] = out[i * HALF:(i + 1) * HALF]
        give(n * tile, tile, out[len(blocks) * HALF:])


def late_kernel(table, vert, qs, w, b0, b2, b1, b3, acc, tops, sums, att, keep, give, kv, sems):
    copies = Copies(sems)
    load_half(copies, table[META], b0, b2, b1, b3, kv)
    copies.wait()
    token = TOKENS // RUNS * table[META + 2] + lax.broadcasted_iota(jnp.int32, (TOKENS, 1), 0)
    places = key_places(table, True)
    for h in range(HEADS):
        cols = slice(h * HEAD, (h + 1) * HEAD)
        slots = slots_of(table, vert, h)
        score = product(qs[:, cols], listed(kv, 0, slots))
        score = jnp.where(token >= limits(vert, places, h), score, LOW)
        before = tops[:, cols]
        top = jnp.maximum(wide(jnp.max(score, axis=1, keepdims=True)), before)
        weight = jnp.exp2((score - across(top, LISTED * HALF // HEAD)) * FACTOR)
        fade = jnp.exp2((before - top) * FACTOR)
        total = wide(jnp.sum(weight, axis=1, keepdims=True)) + fade * sums[:, cols]
        mixed = jnp.dot(weight.astype(BF16), listed(kv, 1, slots), preferred_element_type=F32)
        att[:, cols] = ((mixed + acc[:, cols] * fade) * (1.0 / total)).astype(BF16)
    project(att, w, [(table[META + 5] + 2) % X], table[META + 1], [keep], functools.partial(store, give))


def store(give, start, size, rows):
    give[:, start:start + size] = rows


def sides_kernel(table, att, w, keep_below, keep_above, direct, relayed):
    x, mid = table[META + 5], w.shape[1] // 2

    def give(start, size, rows):
        below, above = rows[:HALF], rows[HALF:]
        at = slice(start % mid, start % mid + size)
        if start < mid:
            relayed[:HALF, at], direct[HALF:, at] = below, above
        else:
            direct[:HALF, at], relayed[HALF:, at] = below, above

    project(att, w, [(x + 1) % X, (x + 3) % X], table[META + 1], [keep_below, keep_above], give)


def own_kernel(table, att, w, after, keep, give):
    project(att, w, [table[META + 5]], table[META + 1], [keep], functools.partial(store, give))


def final_kernel(keep, swapped, left_below, left_above, right_below, right_above, out):
    mid = out.shape[1] // 2
    for start, pair in ((0, (left_below, left_above)), (mid, (right_below, right_above))):
        cols = slice(start, start + mid)
        total = keep[:, cols].astype(F32) + swapped[:, cols].astype(F32)
        for part in pair:
            total = total + part[...].astype(F32)
        out[:, cols] = total.astype(BF16)


SMEM = pl.BlockSpec(memory_space=pltpu.SMEM)
VMEM = pl.BlockSpec(memory_space=pltpu.VMEM)
ANY = pl.BlockSpec(memory_space=pl.ANY)


def call(body, ins, outs, scratch, micros, name):
    return pl.pallas_call(
        body,
        out_shape=tuple(pltpu.VMEM(shape, dtype) for shape, dtype in outs),
        in_specs=ins,
        out_specs=(VMEM,) * len(outs),
        scratch_shapes=scratch,
        compiler_params=pltpu.CompilerParams(vmem_limit_bytes=24 * 2 ** 20),
        cost_estimate=pl.CostEstimate(flops=int(micros * 1e9), bytes_accessed=int(micros * 2 ** 20), transcendentals=0),
        name=name,
    )


def total_of(*terms):
    return functools.reduce(lambda a, b: a + b, [t.astype(F32) for t in terms]).astype(BF16)


def tables(c, x, core, vert_blocks):
    block = jnp.arange(BLOCKS, dtype=jnp.int32)
    present = jnp.any(vert_blocks[:, :, None] == block, axis=(0, 1)).astype(jnp.int32)
    rank = jnp.sum(jnp.where(block[:, None] > block[None, :], present[None, :], 0), axis=1)
    meta = jnp.stack([c % 2, core, RUNS * c, c // Y, (c % Y) // 2, x]).astype(jnp.int32)
    return jnp.where(present > 0, rank, -1), jnp.concatenate([rank, meta])


def spread_kernel(keys, values, out, sems):
    copies = Copies(sems)
    for kind, a in enumerate((keys, values)):
        for b in range(RUNS):
            copies.start(a.at[b], out.at[:, kind, b])
    copies.wait()


def per_device(queries, keys, values, sink_logits, vert_blocks, slash_offsets, output_weight):
    c = lax.axis_index("ctx")
    h = lax.axis_index("head")
    x, core = h // 2, h % 2
    keys = keys.reshape(RUNS, ROWS, HEAD)
    values = values.reshape(RUNS, ROWS, HEAD)
    place, table = tables(c, x, core, vert_blocks)
    far_keys, far_values = [pltpu.with_memory_space_constraint(a.reshape(RUNS, 16, 8, HEAD), pltpu.HBM)
                            for a in (keys, values)]
    (spread,) = call(
        spread_kernel, [ANY, ANY], [((16, 2, RUNS, 8, HEAD), BF16)], [pltpu.SemaphoreType.DMA((2 * RUNS,))], 1, "spread",
    )(far_keys, far_values)
    spread = spread.reshape(Z * Y, RUNS * 8, HEAD)
    prev = lax.ppermute(spread, "ctx", [(s, s + 1) for s in range(Z * Y - 1)]).reshape(16, 2, RUNS, 8, HEAD)
    got = lax.all_to_all(spread, "ctx", 0, 0, tiled=True).reshape(BLOCKS * 8, HEAD)
    r = jnp.arange(SLOTS * 8, dtype=jnp.int32)[:, None]
    col = jnp.arange(BLOCKS * 8, dtype=jnp.int32)[None, :]
    pick = (jnp.repeat(place, 8)[None, :] == r // 8) & (col % 8 == r % 8)
    mine = jnp.dot(pick.astype(BF16), got, preferred_element_type=F32)
    mine = mine.astype(BF16).reshape(SLOTS, 8, HEAD)

    def from_z(a, offset):
        return lax.ppermute(a, "ctx", z_pairs(-offset))

    z2, z4, z6 = from_z(mine, 2), from_z(mine, 4), from_z(mine, 6)
    a0 = jnp.concatenate([mine, z2, z4, z6], axis=1)
    low = from_z(jnp.concatenate([mine, z6], axis=1), -1)
    high = from_z(jnp.concatenate([mine, z2], axis=1), 1)
    b0 = jnp.concatenate([low, high], axis=1)
    a1, a2, a3 = [lax.ppermute(a0, "ctx", y_pairs(f)) for f in (1, 2, 3)]
    b1, b2, b3 = [lax.ppermute(b0, "ctx", y_pairs(f)) for f in (1, 2, 3)]

    width = output_weight.shape[1]
    kv = pltpu.VMEM((2, SLOTS, HALF, HEAD), BF16)
    rows = ((TOKENS, HEADS * HEAD), BF16)
    part = ((HALF, width), BF16)
    far_queries = pltpu.with_memory_space_constraint(queries, pltpu.HBM)
    far_weight = pltpu.with_memory_space_constraint(output_weight, pltpu.HBM)
    acc, tops, sums, w, q = call(
        early_kernel, [SMEM] * 4 + [ANY] * 6 + [VMEM, ANY, ANY],
        [((TOKENS, HEADS * HEAD), F32)] * 3 + [(output_weight.shape, BF16), rows],
        [kv, pltpu.VMEM((2, 2 * RUNS, ROWS, HEAD), BF16), pltpu.SemaphoreType.DMA((11,))], 8, "early",
    )(table, vert_blocks, slash_offsets, sink_logits, far_queries, far_weight, a0, a2, a1, a3, prev,
      *[pltpu.with_memory_space_constraint(a, pltpu.HBM) for a in (keys, values)])
    att, keep_far, give_far = call(
        late_kernel, [SMEM, SMEM, VMEM, VMEM] + [ANY] * 4 + [VMEM] * 3,
        [rows, part, part], [kv, pltpu.SemaphoreType.DMA((4,))], 0.01, "late",
    )(table, vert_blocks, q, w, b0, b2, b1, b3, acc, tops, sums)
    halves = ((2 * HALF, width // 2), BF16)
    keep_below, keep_above, give_direct, give_relayed = call(
        sides_kernel, [SMEM, VMEM, VMEM], [part, part, halves, halves], [], 0.01, "sides",
    )(table, att, w)
    def swap(a):
        return lax.ppermute(a, "head", CORE_PAIRS)

    def to_x(a, step):
        return lax.ppermute(a, "head", x_pairs(step))

    far, direct, relayed = swap(give_far), swap(give_direct), swap(give_relayed)
    mid = width // 2
    far_left = total_of(keep_far[:, :mid], far[:, :mid])
    far_right = total_of(keep_far[:, mid:], far[:, mid:])
    relay_left, relay_right = to_x(far_left, 1), to_x(far_right, -1)
    keep_own, give_own = call(
        own_kernel, [SMEM, VMEM, VMEM, ANY], [part, part], [], 0.01, "own",
    )(table, att, w, far_left)

    own = swap(give_own)
    right_below = to_x(total_of(keep_below[:, mid:], direct[:HALF]), 1)
    left_above = to_x(total_of(keep_above[:, :mid], direct[HALF:]), -1)
    keep_below, keep_above, relayed, relay_left, relay_right = lax.optimization_barrier(
        (keep_below, keep_above, relayed, relay_left, relay_right))
    left_below = to_x(total_of(keep_below[:, :mid], relayed[:HALF], relay_left), 1)
    right_above = to_x(total_of(keep_above[:, mid:], relayed[HALF:], relay_right), -1)
    return pl.pallas_call(
        final_kernel,
        out_shape=jax.ShapeDtypeStruct((HALF, width), BF16),
        in_specs=[VMEM] * 6,
        out_specs=VMEM,
        compiler_params=pltpu.CompilerParams(vmem_limit_bytes=8 * 2 ** 20),
        name="final",
    )(keep_own, own, left_below, left_above, right_below, right_above)


def solution(mesh):
    return jax.shard_map(
        per_device,
        mesh=mesh,
        in_specs=(
            P("ctx", "head"),
            P("ctx", "head"),
            P("ctx", "head"),
            P("head"),
            P("head", None),
            P("head", None),
            P("head", None),
        ),
        out_specs=P(("ctx", "head"), None),
        check_vma=False,
    )
```

```python
import functools

import jax
import jax.numpy as jnp
from jax import lax
from jax.experimental import pallas as pl
from jax.experimental.pallas import tpu as pltpu
from jax.sharding import PartitionSpec as P

HEAD = 128
ROWS = 128
HALF = 64
SLOTS = 24
LISTED = 8
BANDS = 3
BLOCKS = 128
RUNS = 4
HEADS = 8
TOKENS = RUNS * ROWS
SCALE = HEAD ** -0.5
FACTOR = SCALE * 1.4426950408889634
NEVER = 1 << 20
LOW = -1e30
Z, Y, X = 8, 4, 4
BF16, F32 = jnp.bfloat16, jnp.float32
META = BLOCKS


def z_pairs(flip):
    return [(Y * z + y, Y * (z ^ flip) + y) for z in range(Z) for y in range(Y)]


def y_pairs(flip):
    return [(Y * z + y, Y * z + (y ^ flip)) for z in range(Z) for y in range(Y)]


def x_pairs(step):
    return [(2 * x + k, 2 * ((x + step) % X) + k) for x in range(X) for k in range(2)]


CORE_PAIRS = [(h, h ^ 1) for h in range(HEADS)]


class Copies:
    def __init__(self, sems):
        self.sems, self.made = sems, []

    def start(self, src, dst):
        made = pltpu.make_async_copy(src, dst, self.sems.at[len(self.made)])
        made.start()
        self.made.append(made)

    def wait(self, count=None):
        for made in self.made[:count]:
            made.wait()
        self.made = [] if count is None else self.made[count:]


def key_places(table, late):
    z, y_half = table[META + 3], table[META + 4]
    n = lax.broadcasted_iota(jnp.int32, (1, HALF), 1)
    part, inner, row = n // 32, (n // 8) % 4, n % 8
    z_of = z ^ ((inner % 2) * 4 + (inner // 2) * 2 + int(late))
    return (z_of * 2 + (y_half ^ part)) * 8 + row


def load_half(copies, odd, own, far, near, cross, kv):
    for kind, parts in ((odd, (own, far)), (1 - odd, (near, cross))):
        for p, part in enumerate(parts):
            copies.start(part, kv.at[kind, :, pl.ds(32 * p, 32)])


def slots_of(table, vert, h):
    return [table[jnp.maximum(vert[h, e], 0)] for e in range(LISTED)]


def listed(kv, kind, slots):
    return jnp.concatenate([kv[kind, slot] for slot in slots], axis=0)


def limits(vert, places, h):
    ids = [vert[h, e] for e in range(LISTED)]
    return jnp.concatenate([places + jnp.where(i >= 0, i * ROWS, NEVER) for i in ids], axis=1)


def near_base(table, vert, slash, h, run, j):
    block = table[META + 2] + run - slash[h, j]
    use = block >= 0
    for e in range(LISTED):
        use = jnp.logical_and(use, vert[h, e] != block)
    return jnp.where(use, block * ROWS, NEVER)


def product(q, keys):
    return lax.dot_general(q, keys, (((1,), (1,)), ((), ())), preferred_element_type=F32)


def wide(column):
    return jnp.broadcast_to(column, (column.shape[0], HEAD))


def across(column_block, count):
    return jnp.concatenate([column_block] * count, axis=1)


def early_kernel(table, vert, slash, sink, q, w, a0, a2, a1, a3, prev, kc, vc, acc, tops, sums, w_out, qs, kv, band, sems):
    copies = Copies(sems)
    copies.start(q, qs)
    for kind, cur in enumerate((kc, vc)):
        copies.start(cur, band.at[kind, pl.ds(RUNS, RUNS)])
    load_half(copies, table[META], a0, a2, a1, a3, kv)
    first = len(copies.made)
    depth = w.shape[0] // 4
    for n in range(4):
        copies.start(w.at[pl.ds(n * depth, depth)], w_out.at[pl.ds(n * depth, depth)])
    for kind in range(2):
        for b in range(RUNS):
            rows = [prev[r, kind, b].astype(F32) for r in range(16)]
            band[kind, b] = jnp.concatenate(rows, axis=0).astype(BF16)
    copies.wait(first)
    token = TOKENS // RUNS * table[META + 2] + lax.broadcasted_iota(jnp.int32, (TOKENS, 1), 0)
    places = key_places(table, False)
    within = lax.broadcasted_iota(jnp.int32, (1, ROWS), 1)
    for h in range(HEADS):
        cols = slice(h * HEAD, (h + 1) * HEAD)
        qh = qs[:, cols]
        slots = slots_of(table, vert, h)
        score = product(qh, listed(kv, 0, slots))
        score = jnp.where(token >= limits(vert, places, h), score, LOW)
        near = []
        for run in range(RUNS):
            rows = slice(run * ROWS, (run + 1) * ROWS)
            keys = jnp.concatenate([band[0, RUNS + run - slash[h, j]] for j in range(BANDS)], axis=0)
            limit = jnp.concatenate(
                [within + near_base(table, vert, slash, h, run, j) for j in range(BANDS)], axis=1)
            near.append(jnp.where(token[rows] >= limit, product(qh[rows], keys), LOW))
        near = jnp.concatenate(near, axis=0)
        raw_sink = sink[h] * (1.0 / SCALE)
        top = jnp.maximum(jnp.max(score, axis=1, keepdims=True), jnp.max(near, axis=1, keepdims=True))
        top = jnp.maximum(top, raw_sink)
        weight = jnp.exp2((score - top) * FACTOR)
        near = jnp.exp2((near - top) * FACTOR)
        total = jnp.sum(weight, axis=1, keepdims=True) + jnp.sum(near, axis=1, keepdims=True)
        total = total + jnp.exp2((raw_sink - top) * FACTOR)
        mixed = jnp.dot(weight.astype(BF16), listed(kv, 1, slots), preferred_element_type=F32)
        near = near.astype(BF16)
        for run in range(RUNS):
            rows = slice(run * ROWS, (run + 1) * ROWS)
            vals = jnp.concatenate([band[1, RUNS + run - slash[h, j]] for j in range(BANDS)], axis=0)
            acc[rows, cols] = mixed[rows] + jnp.dot(near[rows], vals, preferred_element_type=F32)
        tops[:, cols] = wide(top)
        sums[:, cols] = wide(total)
    copies.wait()


def project(att, w, blocks, core, keeps, give):
    def rows(block, side):
        start = pl.multiple_of(block * ROWS + side * HALF, HALF)
        return att[pl.ds(start, HALF), :]

    lhs = jnp.concatenate([rows(b, core) for b in blocks] + [rows(b, 1 - core) for b in blocks], axis=0)
    tile = 512
    for n in range(w.shape[1] // tile):
        cols = slice(n * tile, (n + 1) * tile)
        out = jnp.dot(lhs, w[:, cols], preferred_element_type=F32).astype(BF16)
        for i, keep in enumerate(keeps):
            keep[:, cols] = out[i * HALF:(i + 1) * HALF]
        give(n * tile, tile, out[len(blocks) * HALF:])


def late_kernel(table, vert, qs, w, b0, b2, b1, b3, acc, tops, sums, att, keep, give, kv, sems):
    copies = Copies(sems)
    load_half(copies, table[META], b0, b2, b1, b3, kv)
    copies.wait()
    token = TOKENS // RUNS * table[META + 2] + lax.broadcasted_iota(jnp.int32, (TOKENS, 1), 0)
    places = key_places(table, True)
    for h in range(HEADS):
        cols = slice(h * HEAD, (h + 1) * HEAD)
        slots = slots_of(table, vert, h)
        score = product(qs[:, cols], listed(kv, 0, slots))
        score = jnp.where(token >= limits(vert, places, h), score, LOW)
        before = tops[:, cols]
        top = jnp.maximum(wide(jnp.max(score, axis=1, keepdims=True)), before)
        weight = jnp.exp2((score - across(top, LISTED * HALF // HEAD)) * FACTOR)
        fade = jnp.exp2((before - top) * FACTOR)
        total = wide(jnp.sum(weight, axis=1, keepdims=True)) + fade * sums[:, cols]
        mixed = jnp.dot(weight.astype(BF16), listed(kv, 1, slots), preferred_element_type=F32)
        att[:, cols] = ((mixed + acc[:, cols] * fade) * (1.0 / total)).astype(BF16)
    project(att, w, [(table[META + 5] + 2) % X], table[META + 1], [keep], functools.partial(store, give))


def store(give, start, size, rows):
    give[:, start:start + size] = rows


def sides_kernel(table, att, w, keep_below, keep_above, direct, relayed):
    x, mid = table[META + 5], w.shape[1] // 2

    def give(start, size, rows):
        below, above = rows[:HALF], rows[HALF:]
        at = slice(start % mid, start % mid + size)
        if start < mid:
            relayed[:HALF, at], direct[HALF:, at] = below, above
        else:
            direct[:HALF, at], relayed[HALF:, at] = below, above

    project(att, w, [(x + 1) % X, (x + 3) % X], table[META + 1], [keep_below, keep_above], give)


def own_kernel(table, att, w, after, keep, give):
    project(att, w, [table[META + 5]], table[META + 1], [keep], functools.partial(store, give))


def final_kernel(keep, swapped, left_below, left_above, right_below, right_above, out):
    mid = out.shape[1] // 2
    for start, pair in ((0, (left_below, left_above)), (mid, (right_below, right_above))):
        cols = slice(start, start + mid)
        total = keep[:, cols].astype(F32) + swapped[:, cols].astype(F32)
        for part in pair:
            total = total + part[...].astype(F32)
        out[:, cols] = total.astype(BF16)


SMEM = pl.BlockSpec(memory_space=pltpu.SMEM)
VMEM = pl.BlockSpec(memory_space=pltpu.VMEM)
ANY = pl.BlockSpec(memory_space=pl.ANY)


def call(body, ins, outs, scratch, micros, name):
    return pl.pallas_call(
        body,
        out_shape=tuple(pltpu.VMEM(shape, dtype) for shape, dtype in outs),
        in_specs=ins,
        out_specs=(VMEM,) * len(outs),
        scratch_shapes=scratch,
        compiler_params=pltpu.CompilerParams(vmem_limit_bytes=24 * 2 ** 20),
        cost_estimate=pl.CostEstimate(flops=int(micros * 1e9), bytes_accessed=int(micros * 2 ** 20), transcendentals=0),
        name=name,
    )


def total_of(*terms):
    return functools.reduce(lambda a, b: a + b, [t.astype(F32) for t in terms]).astype(BF16)


def tables(c, x, core, vert_blocks):
    block = jnp.arange(BLOCKS, dtype=jnp.int32)
    present = jnp.any(vert_blocks[:, :, None] == block, axis=(0, 1)).astype(jnp.int32)
    rank = jnp.sum(jnp.where(block[:, None] > block[None, :], present[None, :], 0), axis=1)
    meta = jnp.stack([c % 2, core, RUNS * c, c // Y, (c % Y) // 2, x]).astype(jnp.int32)
    return jnp.where(present > 0, rank, -1), jnp.concatenate([rank, meta])


def spread_kernel(keys, values, out, sems):
    copies = Copies(sems)
    for kind, a in enumerate((keys, values)):
        for b in range(RUNS):
            copies.start(a.at[b], out.at[:, kind, b])
    copies.wait()


def per_device(queries, keys, values, sink_logits, vert_blocks, slash_offsets, output_weight):
    c = lax.axis_index("ctx")
    h = lax.axis_index("head")
    x, core = h // 2, h % 2
    keys = keys.reshape(RUNS, ROWS, HEAD)
    values = values.reshape(RUNS, ROWS, HEAD)
    place, table = tables(c, x, core, vert_blocks)
    far_keys, far_values = [pltpu.with_memory_space_constraint(a.reshape(RUNS, 16, 8, HEAD), pltpu.HBM)
                            for a in (keys, values)]
    (spread,) = call(
        spread_kernel, [ANY, ANY], [((16, 2, RUNS, 8, HEAD), BF16)], [pltpu.SemaphoreType.DMA((2 * RUNS,))], 1, "spread",
    )(far_keys, far_values)
    spread = spread.reshape(Z * Y, RUNS * 8, HEAD)
    prev = lax.ppermute(spread, "ctx", [(s, s + 1) for s in range(Z * Y - 1)]).reshape(16, 2, RUNS, 8, HEAD)
    got = lax.all_to_all(spread, "ctx", 0, 0, tiled=True).reshape(BLOCKS * 8, HEAD)
    prev, place = lax.optimization_barrier((prev, place))
    r = jnp.arange(SLOTS * 8, dtype=jnp.int32)[:, None]
    col = jnp.arange(BLOCKS * 8, dtype=jnp.int32)[None, :]
    pick = (jnp.repeat(place, 8)[None, :] == r // 8) & (col % 8 == r % 8)
    mine = jnp.dot(pick.astype(BF16), got, preferred_element_type=F32)
    mine = mine.astype(BF16).reshape(SLOTS, 8, HEAD)

    def from_z(a, flip):
        return lax.ppermute(a, "ctx", z_pairs(flip))

    pair = jnp.concatenate([mine, from_z(mine, 4)], axis=1)
    a0 = jnp.concatenate([pair, from_z(pair, 2)], axis=1)
    b0 = from_z(a0, 1)
    a1, a2, a3 = [lax.ppermute(a0, "ctx", y_pairs(f)) for f in (1, 2, 3)]
    b1, b2, b3 = [lax.ppermute(b0, "ctx", y_pairs(f)) for f in (1, 2, 3)]

    width = output_weight.shape[1]
    kv = pltpu.VMEM((2, SLOTS, HALF, HEAD), BF16)
    rows = ((TOKENS, HEADS * HEAD), BF16)
    part = ((HALF, width), BF16)
    far_queries = pltpu.with_memory_space_constraint(queries, pltpu.HBM)
    far_weight = pltpu.with_memory_space_constraint(output_weight, pltpu.HBM)
    acc, tops, sums, w, q = call(
        early_kernel, [SMEM] * 4 + [ANY] * 6 + [VMEM, ANY, ANY],
        [((TOKENS, HEADS * HEAD), F32)] * 3 + [(output_weight.shape, BF16), rows],
        [kv, pltpu.VMEM((2, 2 * RUNS, ROWS, HEAD), BF16), pltpu.SemaphoreType.DMA((11,))], 8, "early",
    )(table, vert_blocks, slash_offsets, sink_logits, far_queries, far_weight, a0, a2, a1, a3, prev,
      *[pltpu.with_memory_space_constraint(a, pltpu.HBM) for a in (keys, values)])
    att, keep_far, give_far = call(
        late_kernel, [SMEM, SMEM, VMEM, VMEM] + [ANY] * 4 + [VMEM] * 3,
        [rows, part, part], [kv, pltpu.SemaphoreType.DMA((4,))], 0.01, "late",
    )(table, vert_blocks, q, w, b0, b2, b1, b3, acc, tops, sums)
    halves = ((2 * HALF, width // 2), BF16)
    keep_below, keep_above, give_direct, give_relayed = call(
        sides_kernel, [SMEM, VMEM, VMEM], [part, part, halves, halves], [], 0.01, "sides",
    )(table, att, w)
    def swap(a):
        return lax.ppermute(a, "head", CORE_PAIRS)

    def to_x(a, step):
        return lax.ppermute(a, "head", x_pairs(step))

    far, direct, relayed = swap(give_far), swap(give_direct), swap(give_relayed)
    mid = width // 2
    far_left = total_of(keep_far[:, :mid], far[:, :mid])
    far_right = total_of(keep_far[:, mid:], far[:, mid:])
    relay_left, relay_right = to_x(far_left, 1), to_x(far_right, -1)
    keep_own, give_own = call(
        own_kernel, [SMEM, VMEM, VMEM, ANY], [part, part], [], 0.01, "own",
    )(table, att, w, far_left)

    own = swap(give_own)
    right_below = to_x(total_of(keep_below[:, mid:], direct[:HALF]), 1)
    left_above = to_x(total_of(keep_above[:, :mid], direct[HALF:]), -1)
    keep_below, keep_above, relayed, relay_left, relay_right = lax.optimization_barrier(
        (keep_below, keep_above, relayed, relay_left, relay_right))
    left_below = to_x(total_of(keep_below[:, :mid], relayed[:HALF], relay_left), 1)
    right_above = to_x(total_of(keep_above[:, mid:], relayed[HALF:], relay_right), -1)
    return pl.pallas_call(
        final_kernel,
        out_shape=jax.ShapeDtypeStruct((HALF, width), BF16),
        in_specs=[VMEM] * 6,
        out_specs=VMEM,
        compiler_params=pltpu.CompilerParams(vmem_limit_bytes=8 * 2 ** 20),
        name="final",
    )(keep_own, own, left_below, left_above, right_below, right_above)


def solution(mesh):
    return jax.shard_map(
        per_device,
        mesh=mesh,
        in_specs=(
            P("ctx", "head"),
            P("ctx", "head"),
            P("ctx", "head"),
            P("head"),
            P("head", None),
            P("head", None),
            P("head", None),
        ),
        out_specs=P(("ctx", "head"), None),
        check_vma=False,
    )
```

```python
import functools

import jax
import jax.numpy as jnp
from jax import lax
from jax.experimental import pallas as pl
from jax.experimental.pallas import tpu as pltpu
from jax.sharding import PartitionSpec as P

HEAD = 128
ROWS = 128
HALF = 64
SLOTS = 24
LISTED = 8
BANDS = 3
BLOCKS = 128
RUNS = 4
HEADS = 8
TOKENS = RUNS * ROWS
SCALE = HEAD ** -0.5
FACTOR = SCALE * 1.4426950408889634
NEVER = 1 << 20
LOW = -1e30
Z, Y, X = 8, 4, 4
BF16, F32 = jnp.bfloat16, jnp.float32
META = BLOCKS


def z_pairs(step):
    return [(Y * z + y, Y * ((z + step) % Z) + y) for z in range(Z) for y in range(Y)]


def y_pairs(flip):
    return [(Y * z + y, Y * z + (y ^ flip)) for z in range(Z) for y in range(Y)]


def x_pairs(step):
    return [(2 * x + k, 2 * ((x + step) % X) + k) for x in range(X) for k in range(2)]


CORE_PAIRS = [(h, h ^ 1) for h in range(HEADS)]


class Copies:
    def __init__(self, sems):
        self.sems, self.made = sems, []

    def start(self, src, dst):
        made = pltpu.make_async_copy(src, dst, self.sems.at[len(self.made)])
        made.start()
        self.made.append(made)

    def wait(self, count=None):
        for made in self.made[:count]:
            made.wait()
        self.made = [] if count is None else self.made[count:]


def key_places(table, late):
    z, y_half = table[META + 3], table[META + 4]
    n = lax.broadcasted_iota(jnp.int32, (1, HALF), 1)
    part, inner, row = n // 32, (n // 8) % 4, n % 8
    step = jnp.where(inner < 2, -1 - 2 * inner, 2 * inner - 3) if late else 2 * inner
    z_of = (z + step + Z) % Z
    return (z_of * 2 + (y_half ^ part)) * 8 + row


def load_half(copies, odd, own, far, near, cross, kv):
    for kind, parts in ((odd, (own, far)), (1 - odd, (near, cross))):
        for p, part in enumerate(parts):
            copies.start(part, kv.at[kind, :, pl.ds(32 * p, 32)])


def slots_of(table, vert, h):
    return [table[jnp.maximum(vert[h, e], 0)] for e in range(LISTED)]


def listed(kv, kind, slots):
    return jnp.concatenate([kv[kind, slot] for slot in slots], axis=0)


def limits(vert, places, h):
    ids = [vert[h, e] for e in range(LISTED)]
    return jnp.concatenate([places + jnp.where(i >= 0, i * ROWS, NEVER) for i in ids], axis=1)


def near_base(table, vert, slash, h, run, j):
    block = table[META + 2] + run - slash[h, j]
    use = block >= 0
    for e in range(LISTED):
        use = jnp.logical_and(use, vert[h, e] != block)
    return jnp.where(use, block * ROWS, NEVER)


def product(q, keys):
    return lax.dot_general(q, keys, (((1,), (1,)), ((), ())), preferred_element_type=F32)


def wide(column):
    return jnp.broadcast_to(column, (column.shape[0], HEAD))


def across(column_block, count):
    return jnp.concatenate([column_block] * count, axis=1)


def early_kernel(table, vert, slash, sink, q, w, a0, a2, a1, a3, prev, kc, vc, acc, tops, sums, w_out, qs, kv, band, sems):
    copies = Copies(sems)
    copies.start(q, qs)
    for kind, cur in enumerate((kc, vc)):
        copies.start(cur, band.at[kind, pl.ds(RUNS, RUNS)])
    load_half(copies, table[META], a0, a2, a1, a3, kv)
    first = len(copies.made)
    depth = w.shape[0] // 4
    for n in range(4):
        copies.start(w.at[pl.ds(n * depth, depth)], w_out.at[pl.ds(n * depth, depth)])
    for kind in range(2):
        for b in range(RUNS):
            rows = [prev[r, kind, b].astype(F32) for r in range(16)]
            band[kind, b] = jnp.concatenate(rows, axis=0).astype(BF16)
    copies.wait(first)
    token = TOKENS // RUNS * table[META + 2] + lax.broadcasted_iota(jnp.int32, (TOKENS, 1), 0)
    places = key_places(table, False)
    within = lax.broadcasted_iota(jnp.int32, (1, ROWS), 1)
    for h in range(HEADS):
        cols = slice(h * HEAD, (h + 1) * HEAD)
        qh = qs[:, cols]
        slots = slots_of(table, vert, h)
        score = product(qh, listed(kv, 0, slots))
        score = jnp.where(token >= limits(vert, places, h), score, LOW)
        near = []
        for run in range(RUNS):
            rows = slice(run * ROWS, (run + 1) * ROWS)
            keys = jnp.concatenate([band[0, RUNS + run - slash[h, j]] for j in range(BANDS)], axis=0)
            limit = jnp.concatenate(
                [within + near_base(table, vert, slash, h, run, j) for j in range(BANDS)], axis=1)
            near.append(jnp.where(token[rows] >= limit, product(qh[rows], keys), LOW))
        near = jnp.concatenate(near, axis=0)
        raw_sink = sink[h] * (1.0 / SCALE)
        top = jnp.maximum(jnp.max(score, axis=1, keepdims=True), jnp.max(near, axis=1, keepdims=True))
        top = jnp.maximum(top, raw_sink)
        weight = jnp.exp2((score - top) * FACTOR)
        near = jnp.exp2((near - top) * FACTOR)
        total = jnp.sum(weight, axis=1, keepdims=True) + jnp.sum(near, axis=1, keepdims=True)
        total = total + jnp.exp2((raw_sink - top) * FACTOR)
        mixed = jnp.dot(weight.astype(BF16), listed(kv, 1, slots), preferred_element_type=F32)
        near = near.astype(BF16)
        for run in range(RUNS):
            rows = slice(run * ROWS, (run + 1) * ROWS)
            vals = jnp.concatenate([band[1, RUNS + run - slash[h, j]] for j in range(BANDS)], axis=0)
            acc[rows, cols] = mixed[rows] + jnp.dot(near[rows], vals, preferred_element_type=F32)
        tops[:, cols] = wide(top)
        sums[:, cols] = wide(total)
    copies.wait()


def project(att, w, blocks, core, keeps, give):
    def rows(block, side):
        start = pl.multiple_of(block * ROWS + side * HALF, HALF)
        return att[pl.ds(start, HALF), :]

    lhs = jnp.concatenate([rows(b, core) for b in blocks] + [rows(b, 1 - core) for b in blocks], axis=0)
    tile = 512
    for n in range(w.shape[1] // tile):
        cols = slice(n * tile, (n + 1) * tile)
        out = jnp.dot(lhs, w[:, cols], preferred_element_type=F32).astype(BF16)
        for i, keep in enumerate(keeps):
            keep[:, cols] = out[i * HALF:(i + 1) * HALF]
        give(n * tile, tile, out[len(blocks) * HALF:])


def late_kernel(table, vert, qs, w, b0, b2, b1, b3, acc, tops, sums, att, keep, give, kv, sems):
    copies = Copies(sems)
    load_half(copies, table[META], b0, b2, b1, b3, kv)
    copies.wait()
    token = TOKENS // RUNS * table[META + 2] + lax.broadcasted_iota(jnp.int32, (TOKENS, 1), 0)
    places = key_places(table, True)
    for h in range(HEADS):
        cols = slice(h * HEAD, (h + 1) * HEAD)
        slots = slots_of(table, vert, h)
        score = product(qs[:, cols], listed(kv, 0, slots))
        score = jnp.where(token >= limits(vert, places, h), score, LOW)
        before = tops[:, cols]
        top = jnp.maximum(wide(jnp.max(score, axis=1, keepdims=True)), before)
        weight = jnp.exp2((score - across(top, LISTED * HALF // HEAD)) * FACTOR)
        fade = jnp.exp2((before - top) * FACTOR)
        total = wide(jnp.sum(weight, axis=1, keepdims=True)) + fade * sums[:, cols]
        mixed = jnp.dot(weight.astype(BF16), listed(kv, 1, slots), preferred_element_type=F32)
        att[:, cols] = ((mixed + acc[:, cols] * fade) * (1.0 / total)).astype(BF16)
    project(att, w, [(table[META + 5] + 2) % X], table[META + 1], [keep], functools.partial(store, give))


def store(give, start, size, rows):
    give[:, start:start + size] = rows


def sides_kernel(table, att, w, keep_below, keep_above, direct, relayed):
    x, mid = table[META + 5], w.shape[1] // 2

    def give(start, size, rows):
        below, above = rows[:HALF], rows[HALF:]
        at = slice(start % mid, start % mid + size)
        if start < mid:
            relayed[:HALF, at], direct[HALF:, at] = below, above
        else:
            direct[:HALF, at], relayed[HALF:, at] = below, above

    project(att, w, [(x + 1) % X, (x + 3) % X], table[META + 1], [keep_below, keep_above], give)


def own_kernel(table, att, w, after, keep, give):
    project(att, w, [table[META + 5]], table[META + 1], [keep], functools.partial(store, give))


def final_kernel(keep, swapped, left_below, left_above, right_below, right_above, out):
    mid = out.shape[1] // 2
    for start, pair in ((0, (left_below, left_above)), (mid, (right_below, right_above))):
        cols = slice(start, start + mid)
        total = keep[:, cols].astype(F32) + swapped[:, cols].astype(F32)
        for part in pair:
            total = total + part[...].astype(F32)
        out[:, cols] = total.astype(BF16)


SMEM = pl.BlockSpec(memory_space=pltpu.SMEM)
VMEM = pl.BlockSpec(memory_space=pltpu.VMEM)
ANY = pl.BlockSpec(memory_space=pl.ANY)


def call(body, ins, outs, scratch, micros, name):
    return pl.pallas_call(
        body,
        out_shape=tuple(pltpu.VMEM(shape, dtype) for shape, dtype in outs),
        in_specs=ins,
        out_specs=(VMEM,) * len(outs),
        scratch_shapes=scratch,
        compiler_params=pltpu.CompilerParams(vmem_limit_bytes=24 * 2 ** 20),
        cost_estimate=pl.CostEstimate(flops=int(micros * 1e9), bytes_accessed=int(micros * 2 ** 20), transcendentals=0),
        name=name,
    )


def total_of(*terms):
    return functools.reduce(lambda a, b: a + b, [t.astype(F32) for t in terms]).astype(BF16)


def tables(c, x, core, vert_blocks):
    block = jnp.arange(BLOCKS, dtype=jnp.int32)
    present = jnp.any(vert_blocks[:, :, None] == block, axis=(0, 1)).astype(jnp.int32)
    rank = jnp.sum(jnp.where(block[:, None] > block[None, :], present[None, :], 0), axis=1)
    meta = jnp.stack([c % 2, core, RUNS * c, c // Y, (c % Y) // 2, x]).astype(jnp.int32)
    return jnp.where(present > 0, rank, -1), jnp.concatenate([rank, meta])


def spread_kernel(keys, values, out, sems):
    copies = Copies(sems)
    for kind, a in enumerate((keys, values)):
        for b in range(RUNS):
            copies.start(a.at[b], out.at[:, kind, b])
    copies.wait()


def per_device(queries, keys, values, sink_logits, vert_blocks, slash_offsets, output_weight):
    c = lax.axis_index("ctx")
    h = lax.axis_index("head")
    x, core = h // 2, h % 2
    keys = keys.reshape(RUNS, ROWS, HEAD)
    values = values.reshape(RUNS, ROWS, HEAD)
    place, table = tables(c, x, core, vert_blocks)
    far_keys, far_values = [pltpu.with_memory_space_constraint(a.reshape(RUNS, 16, 8, HEAD), pltpu.HBM)
                            for a in (keys, values)]
    (spread,) = call(
        spread_kernel, [ANY, ANY], [((16, 2, RUNS, 8, HEAD), BF16)], [pltpu.SemaphoreType.DMA((2 * RUNS,))], 1, "spread",
    )(far_keys, far_values)
    spread = spread.reshape(Z * Y, RUNS * 8, HEAD)
    prev = lax.ppermute(spread, "ctx", [(s, s + 1) for s in range(Z * Y - 1)]).reshape(16, 2, RUNS, 8, HEAD)
    got = lax.all_to_all(spread, "ctx", 0, 0, tiled=True).reshape(BLOCKS * 8, HEAD)
    r = jnp.arange(SLOTS * 8, dtype=jnp.int32)[:, None]
    col = jnp.arange(BLOCKS * 8, dtype=jnp.int32)[None, :]
    pick = (jnp.repeat(place, 8)[None, :] == r // 8) & (col % 8 == r % 8)
    mine = jnp.dot(pick.astype(BF16), got, preferred_element_type=F32)
    mine = mine.astype(BF16).reshape(SLOTS, 8, HEAD)

    def from_z(a, offset):
        return lax.ppermute(a, "ctx", z_pairs(-offset))

    z2, z4, z6 = from_z(mine, 2), from_z(mine, 4), from_z(mine, 6)
    prev, z2, z4, z6 = lax.optimization_barrier((prev, z2, z4, z6))
    a0 = jnp.concatenate([mine, z2, z4, z6], axis=1)
    low = from_z(jnp.concatenate([mine, z6], axis=1), -1)
    high = from_z(jnp.concatenate([mine, z2], axis=1), 1)
    b0 = jnp.concatenate([low, high], axis=1)
    a1, a2, a3 = [lax.ppermute(a0, "ctx", y_pairs(f)) for f in (1, 2, 3)]
    b1, b2, b3 = [lax.ppermute(b0, "ctx", y_pairs(f)) for f in (1, 2, 3)]

    width = output_weight.shape[1]
    kv = pltpu.VMEM((2, SLOTS, HALF, HEAD), BF16)
    rows = ((TOKENS, HEADS * HEAD), BF16)
    part = ((HALF, width), BF16)
    far_queries = pltpu.with_memory_space_constraint(queries, pltpu.HBM)
    far_weight = pltpu.with_memory_space_constraint(output_weight, pltpu.HBM)
    acc, tops, sums, w, q = call(
        early_kernel, [SMEM] * 4 + [ANY] * 6 + [VMEM, ANY, ANY],
        [((TOKENS, HEADS * HEAD), F32)] * 3 + [(output_weight.shape, BF16), rows],
        [kv, pltpu.VMEM((2, 2 * RUNS, ROWS, HEAD), BF16), pltpu.SemaphoreType.DMA((11,))], 8, "early",
    )(table, vert_blocks, slash_offsets, sink_logits, far_queries, far_weight, a0, a2, a1, a3, prev,
      *[pltpu.with_memory_space_constraint(a, pltpu.HBM) for a in (keys, values)])
    att, keep_far, give_far = call(
        late_kernel, [SMEM, SMEM, VMEM, VMEM] + [ANY] * 4 + [VMEM] * 3,
        [rows, part, part], [kv, pltpu.SemaphoreType.DMA((4,))], 0.01, "late",
    )(table, vert_blocks, q, w, b0, b2, b1, b3, acc, tops, sums)
    halves = ((2 * HALF, width // 2), BF16)
    keep_below, keep_above, give_direct, give_relayed = call(
        sides_kernel, [SMEM, VMEM, VMEM], [part, part, halves, halves], [], 0.01, "sides",
    )(table, att, w)
    def swap(a):
        return lax.ppermute(a, "head", CORE_PAIRS)

    def to_x(a, step):
        return lax.ppermute(a, "head", x_pairs(step))

    far, direct, relayed = swap(give_far), swap(give_direct), swap(give_relayed)
    mid = width // 2
    far_left = total_of(keep_far[:, :mid], far[:, :mid])
    far_right = total_of(keep_far[:, mid:], far[:, mid:])
    relay_left, relay_right = to_x(far_left, 1), to_x(far_right, -1)
    keep_own, give_own = call(
        own_kernel, [SMEM, VMEM, VMEM, ANY], [part, part], [], 0.01, "own",
    )(table, att, w, far_left)

    own = swap(give_own)
    right_below = to_x(total_of(keep_below[:, mid:], direct[:HALF]), 1)
    left_above = to_x(total_of(keep_above[:, :mid], direct[HALF:]), -1)
    keep_below, keep_above, relayed, relay_left, relay_right = lax.optimization_barrier(
        (keep_below, keep_above, relayed, relay_left, relay_right))
    left_below = to_x(total_of(keep_below[:, :mid], relayed[:HALF], relay_left), 1)
    right_above = to_x(total_of(keep_above[:, mid:], relayed[HALF:], relay_right), -1)
    return pl.pallas_call(
        final_kernel,
        out_shape=jax.ShapeDtypeStruct((HALF, width), BF16),
        in_specs=[VMEM] * 6,
        out_specs=VMEM,
        compiler_params=pltpu.CompilerParams(vmem_limit_bytes=8 * 2 ** 20),
        name="final",
    )(keep_own, own, left_below, left_above, right_below, right_above)


def solution(mesh):
    return jax.shard_map(
        per_device,
        mesh=mesh,
        in_specs=(
            P("ctx", "head"),
            P("ctx", "head"),
            P("ctx", "head"),
            P("head"),
            P("head", None),
            P("head", None),
            P("head", None),
        ),
        out_specs=P(("ctx", "head"), None),
        check_vma=False,
    )
```

```python
import functools

import jax
import jax.numpy as jnp
from jax import lax
from jax.experimental import pallas as pl
from jax.experimental.pallas import tpu as pltpu
from jax.sharding import PartitionSpec as P

HEAD = 128
ROWS = 128
HALF = 64
SLOTS = 24
LISTED = 8
BANDS = 3
BLOCKS = 128
RUNS = 4
HEADS = 8
TOKENS = RUNS * ROWS
SCALE = HEAD ** -0.5
FACTOR = SCALE * 1.4426950408889634
NEVER = 1 << 20
LOW = -1e30
Z, Y, X = 8, 4, 4
BF16, F32 = jnp.bfloat16, jnp.float32
META = BLOCKS


def z_pairs(step):
    return [(Y * z + y, Y * ((z + step) % Z) + y) for z in range(Z) for y in range(Y)]


def y_pairs(flip):
    return [(Y * z + y, Y * z + (y ^ flip)) for z in range(Z) for y in range(Y)]


def x_pairs(step):
    return [(2 * x + k, 2 * ((x + step) % X) + k) for x in range(X) for k in range(2)]


CORE_PAIRS = [(h, h ^ 1) for h in range(HEADS)]


class Copies:
    def __init__(self, sems):
        self.sems, self.made = sems, []

    def start(self, src, dst):
        made = pltpu.make_async_copy(src, dst, self.sems.at[len(self.made)])
        made.start()
        self.made.append(made)

    def wait(self, count=None):
        for made in self.made[:count]:
            made.wait()
        self.made = [] if count is None else self.made[count:]


def key_places(table, late):
    z, y_half = table[META + 3], table[META + 4]
    n = lax.broadcasted_iota(jnp.int32, (1, HALF), 1)
    part, inner, row = n // 32, (n // 8) % 4, n % 8
    step = jnp.where(inner < 2, -1 - 2 * inner, 2 * inner - 3) if late else 2 * inner
    z_of = (z + step + Z) % Z
    return (z_of * 2 + (y_half ^ part)) * 8 + row


def load_half(copies, odd, own, far, near, cross, kv):
    for kind, parts in ((odd, (own, far)), (1 - odd, (near, cross))):
        for p, part in enumerate(parts):
            copies.start(part, kv.at[kind, :, pl.ds(32 * p, 32)])


def slots_of(table, vert, h):
    return [table[jnp.maximum(vert[h, e], 0)] for e in range(LISTED)]


def listed(kv, kind, slots):
    return jnp.concatenate([kv[kind, slot] for slot in slots], axis=0)


def limits(vert, places, h):
    ids = [vert[h, e] for e in range(LISTED)]
    return jnp.concatenate([places + jnp.where(i >= 0, i * ROWS, NEVER) for i in ids], axis=1)


def near_base(table, vert, slash, h, run, j):
    block = table[META + 2] + run - slash[h, j]
    use = block >= 0
    for e in range(LISTED):
        use = jnp.logical_and(use, vert[h, e] != block)
    return jnp.where(use, block * ROWS, NEVER)


def product(q, keys):
    return lax.dot_general(q, keys, (((1,), (1,)), ((), ())), preferred_element_type=F32)


def wide(column):
    return jnp.broadcast_to(column, (column.shape[0], HEAD))


def across(column_block, count):
    return jnp.concatenate([column_block] * count, axis=1)


def early_kernel(table, vert, slash, sink, q, w, a0, a2, a1, a3, prev, kc, vc, acc, tops, sums, w_out, qs, kv, band, sems):
    copies = Copies(sems)
    copies.start(q, qs)
    for kind, cur in enumerate((kc, vc)):
        copies.start(cur, band.at[kind, pl.ds(RUNS, RUNS)])
    load_half(copies, table[META], a0, a2, a1, a3, kv)
    first = len(copies.made)
    depth = w.shape[0] // 4
    for n in range(4):
        copies.start(w.at[pl.ds(n * depth, depth)], w_out.at[pl.ds(n * depth, depth)])
    for kind in range(2):
        for b in range(RUNS):
            rows = [prev[r, kind, b].astype(F32) for r in range(16)]
            band[kind, b] = jnp.concatenate(rows, axis=0).astype(BF16)
    copies.wait(first)
    token = TOKENS // RUNS * table[META + 2] + lax.broadcasted_iota(jnp.int32, (TOKENS, 1), 0)
    places = key_places(table, False)
    within = lax.broadcasted_iota(jnp.int32, (1, ROWS), 1)
    for h in range(HEADS):
        cols = slice(h * HEAD, (h + 1) * HEAD)
        qh = qs[:, cols]
        slots = slots_of(table, vert, h)
        score = product(qh, listed(kv, 0, slots))
        score = jnp.where(token >= limits(vert, places, h), score, LOW)
        near = []
        for run in range(RUNS):
            rows = slice(run * ROWS, (run + 1) * ROWS)
            keys = jnp.concatenate([band[0, RUNS + run - slash[h, j]] for j in range(BANDS)], axis=0)
            limit = jnp.concatenate(
                [within + near_base(table, vert, slash, h, run, j) for j in range(BANDS)], axis=1)
            near.append(jnp.where(token[rows] >= limit, product(qh[rows], keys), LOW))
        near = jnp.concatenate(near, axis=0)
        raw_sink = sink[h] * (1.0 / SCALE)
        top = jnp.maximum(jnp.max(score, axis=1, keepdims=True), jnp.max(near, axis=1, keepdims=True))
        top = jnp.maximum(top, raw_sink)
        weight = jnp.exp2((score - top) * FACTOR)
        near = jnp.exp2((near - top) * FACTOR)
        total = jnp.sum(weight, axis=1, keepdims=True) + jnp.sum(near, axis=1, keepdims=True)
        total = total + jnp.exp2((raw_sink - top) * FACTOR)
        mixed = jnp.dot(weight.astype(BF16), listed(kv, 1, slots), preferred_element_type=F32)
        near = near.astype(BF16)
        for run in range(RUNS):
            rows = slice(run * ROWS, (run + 1) * ROWS)
            vals = jnp.concatenate([band[1, RUNS + run - slash[h, j]] for j in range(BANDS)], axis=0)
            acc[rows, cols] = mixed[rows] + jnp.dot(near[rows], vals, preferred_element_type=F32)
        tops[:, cols] = wide(top)
        sums[:, cols] = wide(total)
    copies.wait()


def project(att, w, blocks, core, keeps, give):
    def rows(block, side):
        start = pl.multiple_of(block * ROWS + side * HALF, HALF)
        return att[pl.ds(start, HALF), :]

    lhs = jnp.concatenate([rows(b, core) for b in blocks] + [rows(b, 1 - core) for b in blocks], axis=0)
    tile = 512
    for n in range(w.shape[1] // tile):
        cols = slice(n * tile, (n + 1) * tile)
        out = jnp.dot(lhs, w[:, cols], preferred_element_type=F32).astype(BF16)
        for i, keep in enumerate(keeps):
            keep[:, cols] = out[i * HALF:(i + 1) * HALF]
        give(n * tile, tile, out[len(blocks) * HALF:])


def late_kernel(table, vert, qs, w, b0, b2, b1, b3, acc, tops, sums, att, keep, give, kv, sems):
    copies = Copies(sems)
    load_half(copies, table[META], b0, b2, b1, b3, kv)
    copies.wait()
    token = TOKENS // RUNS * table[META + 2] + lax.broadcasted_iota(jnp.int32, (TOKENS, 1), 0)
    places = key_places(table, True)
    for h in range(HEADS):
        cols = slice(h * HEAD, (h + 1) * HEAD)
        slots = slots_of(table, vert, h)
        score = product(qs[:, cols], listed(kv, 0, slots))
        score = jnp.where(token >= limits(vert, places, h), score, LOW)
        before = tops[:, cols]
        top = jnp.maximum(wide(jnp.max(score, axis=1, keepdims=True)), before)
        weight = jnp.exp2((score - across(top, LISTED * HALF // HEAD)) * FACTOR)
        fade = jnp.exp2((before - top) * FACTOR)
        total = wide(jnp.sum(weight, axis=1, keepdims=True)) + fade * sums[:, cols]
        mixed = jnp.dot(weight.astype(BF16), listed(kv, 1, slots), preferred_element_type=F32)
        att[:, cols] = ((mixed + acc[:, cols] * fade) * (1.0 / total)).astype(BF16)
    project(att, w, [(table[META + 5] + 2) % X], table[META + 1], [keep], functools.partial(store, give))


def store(give, start, size, rows):
    give[:, start:start + size] = rows


def sides_kernel(table, att, w, keep_below, keep_above, direct, relayed):
    x, mid = table[META + 5], w.shape[1] // 2

    def give(start, size, rows):
        below, above = rows[:HALF], rows[HALF:]
        at = slice(start % mid, start % mid + size)
        if start < mid:
            relayed[:HALF, at], direct[HALF:, at] = below, above
        else:
            direct[:HALF, at], relayed[HALF:, at] = below, above

    project(att, w, [(x + 1) % X, (x + 3) % X], table[META + 1], [keep_below, keep_above], give)


def own_kernel(table, att, w, after, keep, give):
    project(att, w, [table[META + 5]], table[META + 1], [keep], functools.partial(store, give))


def final_kernel(keep, swapped, left_below, left_above, right_below, right_above, out):
    mid = out.shape[1] // 2
    for start, pair in ((0, (left_below, left_above)), (mid, (right_below, right_above))):
        cols = slice(start, start + mid)
        total = keep[:, cols].astype(F32) + swapped[:, cols].astype(F32)
        for part in pair:
            total = total + part[...].astype(F32)
        out[:, cols] = total.astype(BF16)


SMEM = pl.BlockSpec(memory_space=pltpu.SMEM)
VMEM = pl.BlockSpec(memory_space=pltpu.VMEM)
ANY = pl.BlockSpec(memory_space=pl.ANY)


def call(body, ins, outs, scratch, micros, name):
    return pl.pallas_call(
        body,
        out_shape=tuple(pltpu.VMEM(shape, dtype) for shape, dtype in outs),
        in_specs=ins,
        out_specs=(VMEM,) * len(outs),
        scratch_shapes=scratch,
        compiler_params=pltpu.CompilerParams(vmem_limit_bytes=24 * 2 ** 20),
        cost_estimate=pl.CostEstimate(flops=int(micros * 1e9), bytes_accessed=int(micros * 2 ** 20), transcendentals=0),
        name=name,
    )


def total_of(*terms):
    return functools.reduce(lambda a, b: a + b, [t.astype(F32) for t in terms]).astype(BF16)


def tables(c, x, core, vert_blocks):
    block = jnp.arange(BLOCKS, dtype=jnp.int32)
    present = jnp.any(vert_blocks[:, :, None] == block, axis=(0, 1)).astype(jnp.int32)
    rank = jnp.sum(jnp.where(block[:, None] > block[None, :], present[None, :], 0), axis=1)
    meta = jnp.stack([c % 2, core, RUNS * c, c // Y, (c % Y) // 2, x]).astype(jnp.int32)
    return jnp.where(present > 0, rank, -1), jnp.concatenate([rank, meta])


def spread_kernel(keys, values, out, sems):
    copies = Copies(sems)
    for kind, a in enumerate((keys, values)):
        for b in range(RUNS):
            copies.start(a.at[b], out.at[:, kind, b])
    copies.wait()


def per_device(queries, keys, values, sink_logits, vert_blocks, slash_offsets, output_weight):
    c = lax.axis_index("ctx")
    h = lax.axis_index("head")
    x, core = h // 2, h % 2
    keys = keys.reshape(RUNS, ROWS, HEAD)
    values = values.reshape(RUNS, ROWS, HEAD)
    place, table = tables(c, x, core, vert_blocks)
    far_keys, far_values = [pltpu.with_memory_space_constraint(a.reshape(RUNS, 16, 8, HEAD), pltpu.HBM)
                            for a in (keys, values)]
    (spread,) = call(
        spread_kernel, [ANY, ANY], [((16, 2, RUNS, 8, HEAD), BF16)], [pltpu.SemaphoreType.DMA((2 * RUNS,))], 1, "spread",
    )(far_keys, far_values)
    spread = spread.reshape(Z * Y, RUNS * 8, HEAD)
    prev = lax.ppermute(spread, "ctx", [(s, s + 1) for s in range(Z * Y - 1)]).reshape(16, 2, RUNS, 8, HEAD)
    got = lax.all_to_all(spread, "ctx", 0, 0, tiled=True).reshape(BLOCKS * 8, HEAD)
    r = jnp.arange(SLOTS * 8, dtype=jnp.int32)[:, None]
    col = jnp.arange(BLOCKS * 8, dtype=jnp.int32)[None, :]
    pick = (jnp.repeat(place, 8)[None, :] == r // 8) & (col % 8 == r % 8)
    mine = jnp.dot(pick.astype(BF16), got, preferred_element_type=F32)
    mine = mine.astype(BF16).reshape(SLOTS, 8, HEAD)

    def from_z(a, offset):
        return lax.ppermute(a, "ctx", z_pairs(-offset))

    z2, z4, z6 = from_z(mine, 2), from_z(mine, 4), from_z(mine, 6)
    prev, z2, z4, z6 = lax.optimization_barrier((prev, z2, z4, z6))
    a0 = jnp.concatenate([mine, z2, z4, z6], axis=1)
    low = from_z(jnp.concatenate([mine, z6], axis=1), -1)
    high = from_z(jnp.concatenate([mine, z2], axis=1), 1)
    b0 = jnp.concatenate([low, high], axis=1)
    a1, a2, a3 = [lax.ppermute(a0, "ctx", y_pairs(f)) for f in (1, 2, 3)]
    b1, b2, b3 = [lax.ppermute(b0, "ctx", y_pairs(f)) for f in (1, 2, 3)]

    width = output_weight.shape[1]
    kv = pltpu.VMEM((2, SLOTS, HALF, HEAD), BF16)
    rows = ((TOKENS, HEADS * HEAD), BF16)
    part = ((HALF, width), BF16)
    far_queries = pltpu.with_memory_space_constraint(queries, pltpu.HBM)
    far_weight = pltpu.with_memory_space_constraint(output_weight, pltpu.HBM)
    acc, tops, sums, w, q = call(
        early_kernel, [SMEM] * 4 + [ANY] * 6 + [VMEM, ANY, ANY],
        [((TOKENS, HEADS * HEAD), F32)] * 3 + [(output_weight.shape, BF16), rows],
        [kv, pltpu.VMEM((2, 2 * RUNS, ROWS, HEAD), BF16), pltpu.SemaphoreType.DMA((11,))], 8, "early",
    )(table, vert_blocks, slash_offsets, sink_logits, far_queries, far_weight, a0, a2, a1, a3, prev,
      *[pltpu.with_memory_space_constraint(a, pltpu.HBM) for a in (keys, values)])
    att, keep_far, give_far = call(
        late_kernel, [SMEM, SMEM, VMEM, VMEM] + [ANY] * 4 + [VMEM] * 3,
        [rows, part, part], [kv, pltpu.SemaphoreType.DMA((4,))], 0.01, "late",
    )(table, vert_blocks, q, w, b0, b2, b1, b3, acc, tops, sums)
    halves = ((2 * HALF, width // 2), BF16)
    keep_below, keep_above, give_direct, give_relayed = call(
        sides_kernel, [SMEM, VMEM, VMEM], [part, part, halves, halves], [], 0.01, "sides",
    )(table, att, w)
    def swap(a):
        return lax.ppermute(a, "head", CORE_PAIRS)

    def to_x(a, step):
        return lax.ppermute(a, "head", x_pairs(step))

    far, direct, relayed = swap(give_far), swap(give_direct), swap(give_relayed)
    mid = width // 2
    far_left = total_of(keep_far[:, :mid], far[:, :mid])
    far_right = total_of(keep_far[:, mid:], far[:, mid:])
    relay_left, relay_right = to_x(far_left, 1), to_x(far_right, -1)
    direct_right = total_of(keep_below[:, mid:], direct[:HALF])
    direct_left = total_of(keep_above[:, :mid], direct[HALF:])
    right_below, left_above = to_x(direct_right, 1), to_x(direct_left, -1)
    keep_own, give_own = call(
        own_kernel, [SMEM, VMEM, VMEM, ANY], [part, part], [], 0.01, "own",
    )(table, att, w, direct_right)

    own = swap(give_own)
    keep_below, keep_above, relayed, relay_left, relay_right = lax.optimization_barrier(
        (keep_below, keep_above, relayed, relay_left, relay_right))
    left_below = to_x(total_of(keep_below[:, :mid], relayed[:HALF], relay_left), 1)
    right_above = to_x(total_of(keep_above[:, mid:], relayed[HALF:], relay_right), -1)
    return pl.pallas_call(
        final_kernel,
        out_shape=jax.ShapeDtypeStruct((HALF, width), BF16),
        in_specs=[VMEM] * 6,
        out_specs=VMEM,
        compiler_params=pltpu.CompilerParams(vmem_limit_bytes=8 * 2 ** 20),
        name="final",
    )(keep_own, own, left_below, left_above, right_below, right_above)


def solution(mesh):
    return jax.shard_map(
        per_device,
        mesh=mesh,
        in_specs=(
            P("ctx", "head"),
            P("ctx", "head"),
            P("ctx", "head"),
            P("head"),
            P("head", None),
            P("head", None),
            P("head", None),
        ),
        out_specs=P(("ctx", "head"), None),
        check_vma=False,
    )
```

```python
import functools

import jax
import jax.numpy as jnp
from jax import lax
from jax.experimental import pallas as pl
from jax.experimental.pallas import tpu as pltpu
from jax.sharding import PartitionSpec as P

HEAD = 128
ROWS = 128
HALF = 64
SLOTS = 24
LISTED = 8
BANDS = 3
BLOCKS = 128
RUNS = 4
HEADS = 8
TOKENS = RUNS * ROWS
SCALE = HEAD ** -0.5
FACTOR = SCALE * 1.4426950408889634
NEVER = 1 << 20
LOW = -1e30
Z, Y, X = 8, 4, 4
BF16, F32 = jnp.bfloat16, jnp.float32
META = BLOCKS


def z_pairs(step):
    return [(Y * z + y, Y * ((z + step) % Z) + y) for z in range(Z) for y in range(Y)]


def y_pairs(flip):
    return [(Y * z + y, Y * z + (y ^ flip)) for z in range(Z) for y in range(Y)]


def x_pairs(step):
    return [(2 * x + k, 2 * ((x + step) % X) + k) for x in range(X) for k in range(2)]


CORE_PAIRS = [(h, h ^ 1) for h in range(HEADS)]


class Copies:
    def __init__(self, sems):
        self.sems, self.made = sems, []

    def start(self, src, dst):
        made = pltpu.make_async_copy(src, dst, self.sems.at[len(self.made)])
        made.start()
        self.made.append(made)

    def wait(self, count=None):
        for made in self.made[:count]:
            made.wait()
        self.made = [] if count is None else self.made[count:]


def key_places(table, late):
    z, y_half = table[META + 3], table[META + 4]
    n = lax.broadcasted_iota(jnp.int32, (1, HALF), 1)
    part, inner, row = n // 32, (n // 8) % 4, n % 8
    z_of = ((z ^ int(late)) + 2 * inner) % Z
    return (z_of * 2 + (y_half ^ part)) * 8 + row


def load_half(copies, odd, own, far, near, cross, kv):
    for kind, parts in ((odd, (own, far)), (1 - odd, (near, cross))):
        for p, part in enumerate(parts):
            copies.start(part, kv.at[kind, :, pl.ds(32 * p, 32)])


def slots_of(table, vert, h):
    return [table[jnp.maximum(vert[h, e], 0)] for e in range(LISTED)]


def listed(kv, kind, slots):
    return jnp.concatenate([kv[kind, slot] for slot in slots], axis=0)


def limits(vert, places, h):
    ids = [vert[h, e] for e in range(LISTED)]
    return jnp.concatenate([places + jnp.where(i >= 0, i * ROWS, NEVER) for i in ids], axis=1)


def near_base(table, vert, slash, h, run, j):
    block = table[META + 2] + run - slash[h, j]
    use = block >= 0
    for e in range(LISTED):
        use = jnp.logical_and(use, vert[h, e] != block)
    return jnp.where(use, block * ROWS, NEVER)


def product(q, keys):
    return lax.dot_general(q, keys, (((1,), (1,)), ((), ())), preferred_element_type=F32)


def wide(column):
    return jnp.broadcast_to(column, (column.shape[0], HEAD))


def across(column_block, count):
    return jnp.concatenate([column_block] * count, axis=1)


def early_kernel(table, vert, slash, sink, q, w, a0, a2, a1, a3, prev, kc, vc, acc, tops, sums, w_out, qs, kv, band, sems):
    copies = Copies(sems)
    copies.start(q, qs)
    for kind, cur in enumerate((kc, vc)):
        copies.start(cur, band.at[kind, pl.ds(RUNS, RUNS)])
    load_half(copies, table[META], a0, a2, a1, a3, kv)
    first = len(copies.made)
    depth = w.shape[0] // 4
    for n in range(4):
        copies.start(w.at[pl.ds(n * depth, depth)], w_out.at[pl.ds(n * depth, depth)])
    for kind in range(2):
        for b in range(RUNS):
            rows = [prev[r, kind, b].astype(F32) for r in range(16)]
            band[kind, b] = jnp.concatenate(rows, axis=0).astype(BF16)
    copies.wait(first)
    token = TOKENS // RUNS * table[META + 2] + lax.broadcasted_iota(jnp.int32, (TOKENS, 1), 0)
    places = key_places(table, False)
    within = lax.broadcasted_iota(jnp.int32, (1, ROWS), 1)
    for h in range(HEADS):
        cols = slice(h * HEAD, (h + 1) * HEAD)
        qh = qs[:, cols]
        slots = slots_of(table, vert, h)
        score = product(qh, listed(kv, 0, slots))
        score = jnp.where(token >= limits(vert, places, h), score, LOW)
        near = []
        for run in range(RUNS):
            rows = slice(run * ROWS, (run + 1) * ROWS)
            keys = jnp.concatenate([band[0, RUNS + run - slash[h, j]] for j in range(BANDS)], axis=0)
            limit = jnp.concatenate(
                [within + near_base(table, vert, slash, h, run, j) for j in range(BANDS)], axis=1)
            near.append(jnp.where(token[rows] >= limit, product(qh[rows], keys), LOW))
        near = jnp.concatenate(near, axis=0)
        raw_sink = sink[h] * (1.0 / SCALE)
        top = jnp.maximum(jnp.max(score, axis=1, keepdims=True), jnp.max(near, axis=1, keepdims=True))
        top = jnp.maximum(top, raw_sink)
        weight = jnp.exp2((score - top) * FACTOR)
        near = jnp.exp2((near - top) * FACTOR)
        total = jnp.sum(weight, axis=1, keepdims=True) + jnp.sum(near, axis=1, keepdims=True)
        total = total + jnp.exp2((raw_sink - top) * FACTOR)
        mixed = jnp.dot(weight.astype(BF16), listed(kv, 1, slots), preferred_element_type=F32)
        near = near.astype(BF16)
        for run in range(RUNS):
            rows = slice(run * ROWS, (run + 1) * ROWS)
            vals = jnp.concatenate([band[1, RUNS + run - slash[h, j]] for j in range(BANDS)], axis=0)
            acc[rows, cols] = mixed[rows] + jnp.dot(near[rows], vals, preferred_element_type=F32)
        tops[:, cols] = wide(top)
        sums[:, cols] = wide(total)
    copies.wait()


def project(att, w, blocks, core, keeps, give):
    def rows(block, side):
        start = pl.multiple_of(block * ROWS + side * HALF, HALF)
        return att[pl.ds(start, HALF), :]

    lhs = jnp.concatenate([rows(b, core) for b in blocks] + [rows(b, 1 - core) for b in blocks], axis=0)
    tile = 512
    for n in range(w.shape[1] // tile):
        cols = slice(n * tile, (n + 1) * tile)
        out = jnp.dot(lhs, w[:, cols], preferred_element_type=F32).astype(BF16)
        for i, keep in enumerate(keeps):
            keep[:, cols] = out[i * HALF:(i + 1) * HALF]
        give(n * tile, tile, out[len(blocks) * HALF:])


def late_kernel(table, vert, qs, w, b0, b2, b1, b3, acc, tops, sums, att, keep, give, kv, sems):
    copies = Copies(sems)
    load_half(copies, table[META], b0, b2, b1, b3, kv)
    copies.wait()
    token = TOKENS // RUNS * table[META + 2] + lax.broadcasted_iota(jnp.int32, (TOKENS, 1), 0)
    places = key_places(table, True)
    for h in range(HEADS):
        cols = slice(h * HEAD, (h + 1) * HEAD)
        slots = slots_of(table, vert, h)
        score = product(qs[:, cols], listed(kv, 0, slots))
        score = jnp.where(token >= limits(vert, places, h), score, LOW)
        before = tops[:, cols]
        top = jnp.maximum(wide(jnp.max(score, axis=1, keepdims=True)), before)
        weight = jnp.exp2((score - across(top, LISTED * HALF // HEAD)) * FACTOR)
        fade = jnp.exp2((before - top) * FACTOR)
        total = wide(jnp.sum(weight, axis=1, keepdims=True)) + fade * sums[:, cols]
        mixed = jnp.dot(weight.astype(BF16), listed(kv, 1, slots), preferred_element_type=F32)
        att[:, cols] = ((mixed + acc[:, cols] * fade) * (1.0 / total)).astype(BF16)
    project(att, w, [(table[META + 5] + 2) % X], table[META + 1], [keep], functools.partial(store, give))


def store(give, start, size, rows):
    give[:, start:start + size] = rows


def sides_kernel(table, att, w, keep_below, keep_above, direct, relayed):
    x, mid = table[META + 5], w.shape[1] // 2

    def give(start, size, rows):
        below, above = rows[:HALF], rows[HALF:]
        at = slice(start % mid, start % mid + size)
        if start < mid:
            relayed[:HALF, at], direct[HALF:, at] = below, above
        else:
            direct[:HALF, at], relayed[HALF:, at] = below, above

    project(att, w, [(x + 1) % X, (x + 3) % X], table[META + 1], [keep_below, keep_above], give)


def own_kernel(table, att, w, after, keep, give):
    project(att, w, [table[META + 5]], table[META + 1], [keep], functools.partial(store, give))


def final_kernel(keep, swapped, left_below, left_above, right_below, right_above, out):
    mid = out.shape[1] // 2
    for start, pair in ((0, (left_below, left_above)), (mid, (right_below, right_above))):
        cols = slice(start, start + mid)
        total = keep[:, cols].astype(F32) + swapped[:, cols].astype(F32)
        for part in pair:
            total = total + part[...].astype(F32)
        out[:, cols] = total.astype(BF16)


SMEM = pl.BlockSpec(memory_space=pltpu.SMEM)
VMEM = pl.BlockSpec(memory_space=pltpu.VMEM)
ANY = pl.BlockSpec(memory_space=pl.ANY)


def call(body, ins, outs, scratch, micros, name):
    return pl.pallas_call(
        body,
        out_shape=tuple(pltpu.VMEM(shape, dtype) for shape, dtype in outs),
        in_specs=ins,
        out_specs=(VMEM,) * len(outs),
        scratch_shapes=scratch,
        compiler_params=pltpu.CompilerParams(vmem_limit_bytes=24 * 2 ** 20),
        cost_estimate=pl.CostEstimate(flops=int(micros * 1e9), bytes_accessed=int(micros * 2 ** 20), transcendentals=0),
        name=name,
    )


def total_of(*terms):
    return functools.reduce(lambda a, b: a + b, [t.astype(F32) for t in terms]).astype(BF16)


def tables(c, x, core, vert_blocks):
    block = jnp.arange(BLOCKS, dtype=jnp.int32)
    present = jnp.any(vert_blocks[:, :, None] == block, axis=(0, 1)).astype(jnp.int32)
    rank = jnp.sum(jnp.where(block[:, None] > block[None, :], present[None, :], 0), axis=1)
    meta = jnp.stack([c % 2, core, RUNS * c, c // Y, (c % Y) // 2, x]).astype(jnp.int32)
    return jnp.where(present > 0, rank, -1), jnp.concatenate([rank, meta])


def spread_kernel(keys, values, out, sems):
    copies = Copies(sems)
    for kind, a in enumerate((keys, values)):
        for b in range(RUNS):
            copies.start(a.at[b], out.at[:, kind, b])
    copies.wait()


def per_device(queries, keys, values, sink_logits, vert_blocks, slash_offsets, output_weight):
    c = lax.axis_index("ctx")
    h = lax.axis_index("head")
    x, core = h // 2, h % 2
    keys = keys.reshape(RUNS, ROWS, HEAD)
    values = values.reshape(RUNS, ROWS, HEAD)
    place, table = tables(c, x, core, vert_blocks)
    far_keys, far_values = [pltpu.with_memory_space_constraint(a.reshape(RUNS, 16, 8, HEAD), pltpu.HBM)
                            for a in (keys, values)]
    (spread,) = call(
        spread_kernel, [ANY, ANY], [((16, 2, RUNS, 8, HEAD), BF16)], [pltpu.SemaphoreType.DMA((2 * RUNS,))], 1, "spread",
    )(far_keys, far_values)
    spread = spread.reshape(Z * Y, RUNS * 8, HEAD)
    prev = lax.ppermute(spread, "ctx", [(s, s + 1) for s in range(Z * Y - 1)]).reshape(16, 2, RUNS, 8, HEAD)
    got = lax.all_to_all(spread, "ctx", 0, 0, tiled=True).reshape(BLOCKS * 8, HEAD)
    r = jnp.arange(SLOTS * 8, dtype=jnp.int32)[:, None]
    col = jnp.arange(BLOCKS * 8, dtype=jnp.int32)[None, :]
    pick = (jnp.repeat(place, 8)[None, :] == r // 8) & (col % 8 == r % 8)
    mine = jnp.dot(pick.astype(BF16), got, preferred_element_type=F32)
    mine = mine.astype(BF16).reshape(SLOTS, 8, HEAD)

    def from_z(a, offset):
        return lax.ppermute(a, "ctx", z_pairs(-offset))

    z2, z4, z6 = from_z(mine, 2), from_z(mine, 4), from_z(mine, 6)
    prev, z2, z4, z6 = lax.optimization_barrier((prev, z2, z4, z6))
    a0 = jnp.concatenate([mine, z2, z4, z6], axis=1)
    b0 = lax.ppermute(a0, "ctx", [(Y * z + y, Y * (z ^ 1) + y) for z in range(Z) for y in range(Y)])
    a1, a2, a3 = [lax.ppermute(a0, "ctx", y_pairs(f)) for f in (1, 2, 3)]
    b1, b2, b3 = [lax.ppermute(b0, "ctx", y_pairs(f)) for f in (1, 2, 3)]

    width = output_weight.shape[1]
    kv = pltpu.VMEM((2, SLOTS, HALF, HEAD), BF16)
    rows = ((TOKENS, HEADS * HEAD), BF16)
    part = ((HALF, width), BF16)
    far_queries = pltpu.with_memory_space_constraint(queries, pltpu.HBM)
    far_weight = pltpu.with_memory_space_constraint(output_weight, pltpu.HBM)
    acc, tops, sums, w, q = call(
        early_kernel, [SMEM] * 4 + [ANY] * 6 + [VMEM, ANY, ANY],
        [((TOKENS, HEADS * HEAD), F32)] * 3 + [(output_weight.shape, BF16), rows],
        [kv, pltpu.VMEM((2, 2 * RUNS, ROWS, HEAD), BF16), pltpu.SemaphoreType.DMA((11,))], 8, "early",
    )(table, vert_blocks, slash_offsets, sink_logits, far_queries, far_weight, a0, a2, a1, a3, prev,
      *[pltpu.with_memory_space_constraint(a, pltpu.HBM) for a in (keys, values)])
    att, keep_far, give_far = call(
        late_kernel, [SMEM, SMEM, VMEM, VMEM] + [ANY] * 4 + [VMEM] * 3,
        [rows, part, part], [kv, pltpu.SemaphoreType.DMA((4,))], 0.01, "late",
    )(table, vert_blocks, q, w, b0, b2, b1, b3, acc, tops, sums)
    halves = ((2 * HALF, width // 2), BF16)
    keep_below, keep_above, give_direct, give_relayed = call(
        sides_kernel, [SMEM, VMEM, VMEM], [part, part, halves, halves], [], 0.01, "sides",
    )(table, att, w)
    def swap(a):
        return lax.ppermute(a, "head", CORE_PAIRS)

    def to_x(a, step):
        return lax.ppermute(a, "head", x_pairs(step))

    far, direct, relayed = swap(give_far), swap(give_direct), swap(give_relayed)
    mid = width // 2
    far_left = total_of(keep_far[:, :mid], far[:, :mid])
    far_right = total_of(keep_far[:, mid:], far[:, mid:])
    relay_left, relay_right = to_x(far_left, 1), to_x(far_right, -1)
    direct_right = total_of(keep_below[:, mid:], direct[:HALF])
    direct_left = total_of(keep_above[:, :mid], direct[HALF:])
    right_below, left_above = to_x(direct_right, 1), to_x(direct_left, -1)
    keep_own, give_own = call(
        own_kernel, [SMEM, VMEM, VMEM, ANY], [part, part], [], 0.01, "own",
    )(table, att, w, direct_right)

    own = swap(give_own)
    keep_below, keep_above, relayed, relay_left, relay_right = lax.optimization_barrier(
        (keep_below, keep_above, relayed, relay_left, relay_right))
    left_below = to_x(total_of(keep_below[:, :mid], relayed[:HALF], relay_left), 1)
    right_above = to_x(total_of(keep_above[:, mid:], relayed[HALF:], relay_right), -1)
    return pl.pallas_call(
        final_kernel,
        out_shape=jax.ShapeDtypeStruct((HALF, width), BF16),
        in_specs=[VMEM] * 6,
        out_specs=VMEM,
        compiler_params=pltpu.CompilerParams(vmem_limit_bytes=8 * 2 ** 20),
        name="final",
    )(keep_own, own, left_below, left_above, right_below, right_above)


def solution(mesh):
    return jax.shard_map(
        per_device,
        mesh=mesh,
        in_specs=(
            P("ctx", "head"),
            P("ctx", "head"),
            P("ctx", "head"),
            P("head"),
            P("head", None),
            P("head", None),
            P("head", None),
        ),
        out_specs=P(("ctx", "head"), None),
        check_vma=False,
    )
```

```python
import functools

import jax
import jax.numpy as jnp
from jax import lax
from jax.experimental import pallas as pl
from jax.experimental.pallas import tpu as pltpu
from jax.sharding import PartitionSpec as P

HEAD = 128
ROWS = 128
HALF = 64
SLOTS = 24
LISTED = 8
BANDS = 3
BLOCKS = 128
RUNS = 4
HEADS = 8
TOKENS = RUNS * ROWS
SCALE = HEAD ** -0.5
FACTOR = SCALE * 1.4426950408889634
NEVER = 1 << 20
LOW = -1e30
Z, Y, X = 8, 4, 4
BF16, F32 = jnp.bfloat16, jnp.float32
META = BLOCKS


def z_pairs(step):
    return [(Y * z + y, Y * ((z + step) % Z) + y) for z in range(Z) for y in range(Y)]


def y_pairs(flip):
    return [(Y * z + y, Y * z + (y ^ flip)) for z in range(Z) for y in range(Y)]


def x_pairs(step):
    return [(2 * x + k, 2 * ((x + step) % X) + k) for x in range(X) for k in range(2)]


CORE_PAIRS = [(h, h ^ 1) for h in range(HEADS)]


class Copies:
    def __init__(self, sems):
        self.sems, self.made = sems, []

    def start(self, src, dst):
        made = pltpu.make_async_copy(src, dst, self.sems.at[len(self.made)])
        made.start()
        self.made.append(made)

    def wait(self, count=None):
        for made in self.made[:count]:
            made.wait()
        self.made = [] if count is None else self.made[count:]


def key_places(table, late):
    z, y_half = table[META + 3], table[META + 4]
    n = lax.broadcasted_iota(jnp.int32, (1, HALF), 1)
    part, inner, row = n // 32, (n // 8) % 4, n % 8
    z_of = ((z ^ int(late)) + 2 * inner) % Z
    return (z_of * 2 + (y_half ^ part)) * 8 + row


def load_half(copies, odd, own, far, near, cross, kv):
    for kind, parts in ((odd, (own, far)), (1 - odd, (near, cross))):
        for p, part in enumerate(parts):
            copies.start(part, kv.at[kind, :, pl.ds(32 * p, 32)])


def slots_of(table, vert, h):
    return [table[jnp.maximum(vert[h, e], 0)] for e in range(LISTED)]


def listed(kv, kind, slots):
    return jnp.concatenate([kv[kind, slot] for slot in slots], axis=0)


def limits(vert, places, h):
    ids = [vert[h, e] for e in range(LISTED)]
    return jnp.concatenate([places + jnp.where(i >= 0, i * ROWS, NEVER) for i in ids], axis=1)


def near_base(table, vert, slash, h, run, j):
    block = table[META + 2] + run - slash[h, j]
    use = block >= 0
    for e in range(LISTED):
        use = jnp.logical_and(use, vert[h, e] != block)
    return jnp.where(use, block * ROWS, NEVER)


def product(q, keys):
    return lax.dot_general(q, keys, (((1,), (1,)), ((), ())), preferred_element_type=F32)


def wide(column):
    return jnp.broadcast_to(column, (column.shape[0], HEAD))


def across(column_block, count):
    return jnp.concatenate([column_block] * count, axis=1)


def band_kernel(table, vert, slash, sink, q, w, prev, kc, vc, acc, tops, sums, w_out, qs, band, sems):
    copies = Copies(sems)
    copies.start(q, qs)
    for kind, cur in enumerate((kc, vc)):
        copies.start(cur, band.at[kind, pl.ds(RUNS, RUNS)])
    first = len(copies.made)
    depth = w.shape[0] // 4
    for n in range(4):
        copies.start(w.at[pl.ds(n * depth, depth)], w_out.at[pl.ds(n * depth, depth)])
    for kind in range(2):
        for b in range(RUNS):
            rows = [prev[r, kind, b].astype(F32) for r in range(16)]
            band[kind, b] = jnp.concatenate(rows, axis=0).astype(BF16)
    copies.wait(first)
    token = TOKENS // RUNS * table[META + 2] + lax.broadcasted_iota(jnp.int32, (TOKENS, 1), 0)
    within = lax.broadcasted_iota(jnp.int32, (1, ROWS), 1)
    for h in range(HEADS):
        cols = slice(h * HEAD, (h + 1) * HEAD)
        raw_sink = sink[h] * (1.0 / SCALE)
        score = []
        for run in range(RUNS):
            rows = slice(run * ROWS, (run + 1) * ROWS)
            keys = jnp.concatenate([band[0, RUNS + run - slash[h, j]] for j in range(BANDS)], axis=0)
            limit = jnp.concatenate(
                [within + near_base(table, vert, slash, h, run, j) for j in range(BANDS)], axis=1)
            score.append(jnp.where(token[rows] >= limit, product(qs[rows, cols], keys), LOW))
        score = jnp.concatenate(score, axis=0)
        top = jnp.maximum(jnp.max(score, axis=1, keepdims=True), raw_sink)
        weight = jnp.exp2((score - top) * FACTOR)
        total = jnp.sum(weight, axis=1, keepdims=True) + jnp.exp2((raw_sink - top) * FACTOR)
        weight = weight.astype(BF16)
        for run in range(RUNS):
            rows = slice(run * ROWS, (run + 1) * ROWS)
            vals = jnp.concatenate([band[1, RUNS + run - slash[h, j]] for j in range(BANDS)], axis=0)
            acc[rows, cols] = jnp.dot(weight[rows], vals, preferred_element_type=F32)
        tops[:, cols] = wide(top)
        sums[:, cols] = wide(total)
    copies.wait()


def add_listed(table, vert, qs, kv, late, acc, tops, sums, put):
    token = TOKENS // RUNS * table[META + 2] + lax.broadcasted_iota(jnp.int32, (TOKENS, 1), 0)
    places = key_places(table, late)
    for h in range(HEADS):
        cols = slice(h * HEAD, (h + 1) * HEAD)
        slots = slots_of(table, vert, h)
        score = product(qs[:, cols], listed(kv, 0, slots))
        score = jnp.where(token >= limits(vert, places, h), score, LOW)
        before = tops[:, cols]
        top = jnp.maximum(wide(jnp.max(score, axis=1, keepdims=True)), before)
        weight = jnp.exp2((score - across(top, LISTED * HALF // HEAD)) * FACTOR)
        fade = jnp.exp2((before - top) * FACTOR)
        total = wide(jnp.sum(weight, axis=1, keepdims=True)) + fade * sums[:, cols]
        mixed = jnp.dot(weight.astype(BF16), listed(kv, 1, slots), preferred_element_type=F32)
        put(cols, mixed + acc[:, cols] * fade, top, total)


def early_kernel(table, vert, qs, a0, a2, a1, a3, acc, tops, sums, acc_out, tops_out, sums_out, kv, sems):
    copies = Copies(sems)
    load_half(copies, table[META], a0, a2, a1, a3, kv)
    copies.wait()

    def put(cols, mixed, top, total):
        acc_out[:, cols], tops_out[:, cols], sums_out[:, cols] = mixed, top, total

    add_listed(table, vert, qs, kv, False, acc, tops, sums, put)


def project(att, w, blocks, core, keeps, give):
    def rows(block, side):
        start = pl.multiple_of(block * ROWS + side * HALF, HALF)
        return att[pl.ds(start, HALF), :]

    lhs = jnp.concatenate([rows(b, core) for b in blocks] + [rows(b, 1 - core) for b in blocks], axis=0)
    tile = 512
    for n in range(w.shape[1] // tile):
        cols = slice(n * tile, (n + 1) * tile)
        out = jnp.dot(lhs, w[:, cols], preferred_element_type=F32).astype(BF16)
        for i, keep in enumerate(keeps):
            keep[:, cols] = out[i * HALF:(i + 1) * HALF]
        give(n * tile, tile, out[len(blocks) * HALF:])


def late_kernel(table, vert, qs, w, b0, b2, b1, b3, acc, tops, sums, att, keep, give, kv, sems):
    copies = Copies(sems)
    load_half(copies, table[META], b0, b2, b1, b3, kv)
    copies.wait()

    def put(cols, mixed, top, total):
        att[:, cols] = (mixed * (1.0 / total)).astype(BF16)

    add_listed(table, vert, qs, kv, True, acc, tops, sums, put)
    project(att, w, [(table[META + 5] + 2) % X], table[META + 1], [keep], functools.partial(store, give))


def store(give, start, size, rows):
    give[:, start:start + size] = rows


def sides_kernel(table, att, w, keep_below, keep_above, direct, relayed):
    x, mid = table[META + 5], w.shape[1] // 2

    def give(start, size, rows):
        below, above = rows[:HALF], rows[HALF:]
        at = slice(start % mid, start % mid + size)
        if start < mid:
            relayed[:HALF, at], direct[HALF:, at] = below, above
        else:
            direct[:HALF, at], relayed[HALF:, at] = below, above

    project(att, w, [(x + 1) % X, (x + 3) % X], table[META + 1], [keep_below, keep_above], give)


def own_kernel(table, att, w, after, keep, give):
    project(att, w, [table[META + 5]], table[META + 1], [keep], functools.partial(store, give))


def final_kernel(keep, swapped, left_below, left_above, right_below, right_above, out):
    mid = out.shape[1] // 2
    for start, pair in ((0, (left_below, left_above)), (mid, (right_below, right_above))):
        cols = slice(start, start + mid)
        total = keep[:, cols].astype(F32) + swapped[:, cols].astype(F32)
        for part in pair:
            total = total + part[...].astype(F32)
        out[:, cols] = total.astype(BF16)


SMEM = pl.BlockSpec(memory_space=pltpu.SMEM)
VMEM = pl.BlockSpec(memory_space=pltpu.VMEM)
ANY = pl.BlockSpec(memory_space=pl.ANY)


def call(body, ins, outs, scratch, micros, name):
    return pl.pallas_call(
        body,
        out_shape=tuple(pltpu.VMEM(shape, dtype) for shape, dtype in outs),
        in_specs=ins,
        out_specs=(VMEM,) * len(outs),
        scratch_shapes=scratch,
        compiler_params=pltpu.CompilerParams(vmem_limit_bytes=24 * 2 ** 20),
        cost_estimate=pl.CostEstimate(flops=int(micros * 1e9), bytes_accessed=int(micros * 2 ** 20), transcendentals=0),
        name=name,
    )


def total_of(*terms):
    return functools.reduce(lambda a, b: a + b, [t.astype(F32) for t in terms]).astype(BF16)


def tables(c, x, core, vert_blocks):
    block = jnp.arange(BLOCKS, dtype=jnp.int32)
    present = jnp.any(vert_blocks[:, :, None] == block, axis=(0, 1)).astype(jnp.int32)
    rank = jnp.sum(jnp.where(block[:, None] > block[None, :], present[None, :], 0), axis=1)
    meta = jnp.stack([c % 2, core, RUNS * c, c // Y, (c % Y) // 2, x]).astype(jnp.int32)
    return jnp.where(present > 0, rank, -1), jnp.concatenate([rank, meta])


def spread_kernel(keys, values, out, sems):
    copies = Copies(sems)
    for kind, a in enumerate((keys, values)):
        for b in range(RUNS):
            copies.start(a.at[b], out.at[:, kind, b])
    copies.wait()


def per_device(queries, keys, values, sink_logits, vert_blocks, slash_offsets, output_weight):
    c = lax.axis_index("ctx")
    h = lax.axis_index("head")
    x, core = h // 2, h % 2
    keys = keys.reshape(RUNS, ROWS, HEAD)
    values = values.reshape(RUNS, ROWS, HEAD)
    place, table = tables(c, x, core, vert_blocks)
    far_keys, far_values = [pltpu.with_memory_space_constraint(a.reshape(RUNS, 16, 8, HEAD), pltpu.HBM)
                            for a in (keys, values)]
    (spread,) = call(
        spread_kernel, [ANY, ANY], [((16, 2, RUNS, 8, HEAD), BF16)], [pltpu.SemaphoreType.DMA((2 * RUNS,))], 1, "spread",
    )(far_keys, far_values)
    spread = spread.reshape(Z * Y, RUNS * 8, HEAD)
    prev = lax.ppermute(spread, "ctx", [(s, s + 1) for s in range(Z * Y - 1)]).reshape(16, 2, RUNS, 8, HEAD)
    got = lax.all_to_all(spread, "ctx", 0, 0, tiled=True).reshape(BLOCKS * 8, HEAD)
    r = jnp.arange(SLOTS * 8, dtype=jnp.int32)[:, None]
    col = jnp.arange(BLOCKS * 8, dtype=jnp.int32)[None, :]
    pick = (jnp.repeat(place, 8)[None, :] == r // 8) & (col % 8 == r % 8)
    mine = jnp.dot(pick.astype(BF16), got, preferred_element_type=F32)
    mine = mine.astype(BF16).reshape(SLOTS, 8, HEAD)

    def from_z(a, offset):
        return lax.ppermute(a, "ctx", z_pairs(-offset))

    z2, z4, z6 = from_z(mine, 2), from_z(mine, 4), from_z(mine, 6)
    prev, z2, z4, z6 = lax.optimization_barrier((prev, z2, z4, z6))
    a0 = jnp.concatenate([mine, z2, z4, z6], axis=1)
    b0 = lax.ppermute(a0, "ctx", [(Y * z + y, Y * (z ^ 1) + y) for z in range(Z) for y in range(Y)])
    a1, a2, a3 = [lax.ppermute(a0, "ctx", y_pairs(f)) for f in (1, 2, 3)]

    width = output_weight.shape[1]
    kv = pltpu.VMEM((2, SLOTS, HALF, HEAD), BF16)
    rows = ((TOKENS, HEADS * HEAD), BF16)
    part = ((HALF, width), BF16)
    far_queries = pltpu.with_memory_space_constraint(queries, pltpu.HBM)
    far_weight = pltpu.with_memory_space_constraint(output_weight, pltpu.HBM)
    state = [((TOKENS, HEADS * HEAD), F32)] * 3
    acc, tops, sums, w, q = call(
        band_kernel, [SMEM] * 4 + [ANY] * 2 + [VMEM, ANY, ANY], state + [(output_weight.shape, BF16), rows],
        [pltpu.VMEM((2, 2 * RUNS, ROWS, HEAD), BF16), pltpu.SemaphoreType.DMA((7,))], 3, "band",
    )(table, vert_blocks, slash_offsets, sink_logits, far_queries, far_weight, prev,
      *[pltpu.with_memory_space_constraint(a, pltpu.HBM) for a in (keys, values)])
    b0, acc = lax.optimization_barrier((b0, acc))
    b1, b2, b3 = [lax.ppermute(b0, "ctx", y_pairs(f)) for f in (1, 2, 3)]
    acc, tops, sums = call(
        early_kernel, [SMEM, SMEM, VMEM] + [ANY] * 4 + [VMEM] * 3, state, [kv, pltpu.SemaphoreType.DMA((4,))], 5, "early",
    )(table, vert_blocks, q, a0, a2, a1, a3, acc, tops, sums)
    att, keep_far, give_far = call(
        late_kernel, [SMEM, SMEM, VMEM, VMEM] + [ANY] * 4 + [VMEM] * 3,
        [rows, part, part], [kv, pltpu.SemaphoreType.DMA((4,))], 0.01, "late",
    )(table, vert_blocks, q, w, b0, b2, b1, b3, acc, tops, sums)
    halves = ((2 * HALF, width // 2), BF16)
    keep_below, keep_above, give_direct, give_relayed = call(
        sides_kernel, [SMEM, VMEM, VMEM], [part, part, halves, halves], [], 0.01, "sides",
    )(table, att, w)
    def swap(a):
        return lax.ppermute(a, "head", CORE_PAIRS)

    def to_x(a, step):
        return lax.ppermute(a, "head", x_pairs(step))

    far, direct, relayed = swap(give_far), swap(give_direct), swap(give_relayed)
    mid = width // 2
    far_left = total_of(keep_far[:, :mid], far[:, :mid])
    far_right = total_of(keep_far[:, mid:], far[:, mid:])
    relay_left, relay_right = to_x(far_left, 1), to_x(far_right, -1)
    direct_right = total_of(keep_below[:, mid:], direct[:HALF])
    direct_left = total_of(keep_above[:, :mid], direct[HALF:])
    right_below, left_above = to_x(direct_right, 1), to_x(direct_left, -1)
    keep_own, give_own = call(
        own_kernel, [SMEM, VMEM, VMEM, ANY], [part, part], [], 0.01, "own",
    )(table, att, w, direct_right)

    own = swap(give_own)
    keep_below, keep_above, relayed, relay_left, relay_right = lax.optimization_barrier(
        (keep_below, keep_above, relayed, relay_left, relay_right))
    left_below = to_x(total_of(keep_below[:, :mid], relayed[:HALF], relay_left), 1)
    right_above = to_x(total_of(keep_above[:, mid:], relayed[HALF:], relay_right), -1)
    return pl.pallas_call(
        final_kernel,
        out_shape=jax.ShapeDtypeStruct((HALF, width), BF16),
        in_specs=[VMEM] * 6,
        out_specs=VMEM,
        compiler_params=pltpu.CompilerParams(vmem_limit_bytes=8 * 2 ** 20),
        name="final",
    )(keep_own, own, left_below, left_above, right_below, right_above)


def solution(mesh):
    return jax.shard_map(
        per_device,
        mesh=mesh,
        in_specs=(
            P("ctx", "head"),
            P("ctx", "head"),
            P("ctx", "head"),
            P("head"),
            P("head", None),
            P("head", None),
            P("head", None),
        ),
        out_specs=P(("ctx", "head"), None),
        check_vma=False,
    )
```

```python
import functools

import jax
import jax.numpy as jnp
from jax import lax
from jax.experimental import pallas as pl
from jax.experimental.pallas import tpu as pltpu
from jax.sharding import PartitionSpec as P

HEAD = 128
ROWS = 128
HALF = 64
SLOTS = 24
LISTED = 8
BANDS = 3
BLOCKS = 128
RUNS = 4
HEADS = 8
TOKENS = RUNS * ROWS
SCALE = HEAD ** -0.5
FACTOR = SCALE * 1.4426950408889634
NEVER = 1 << 20
LOW = -1e30
Z, Y, X = 8, 4, 4
BF16, F32 = jnp.bfloat16, jnp.float32
META = BLOCKS
VERT = META + 6
SLASH = VERT + HEADS * LISTED


def z_pairs(step):
    return [(Y * z + y, Y * ((z + step) % Z) + y) for z in range(Z) for y in range(Y)]


def y_pairs(flip):
    return [(Y * z + y, Y * z + (y ^ flip)) for z in range(Z) for y in range(Y)]


def x_pairs(step):
    return [(2 * x + k, 2 * ((x + step) % X) + k) for x in range(X) for k in range(2)]


CORE_PAIRS = [(h, h ^ 1) for h in range(HEADS)]


class Copies:
    def __init__(self, sems):
        self.sems, self.made = sems, []

    def start(self, src, dst):
        made = pltpu.make_async_copy(src, dst, self.sems.at[len(self.made)])
        made.start()
        self.made.append(made)

    def wait(self, count=None):
        for made in self.made[:count]:
            made.wait()
        self.made = [] if count is None else self.made[count:]


def key_places(table, late):
    z, y_half = table[META + 3], table[META + 4]
    n = lax.broadcasted_iota(jnp.int32, (1, HALF), 1)
    part, inner, row = n // 32, (n // 8) % 4, n % 8
    z_of = ((z ^ int(late)) + 2 * inner) % Z
    return (z_of * 2 + (y_half ^ part)) * 8 + row


def load_half(copies, odd, own, far, near, cross, kv):
    for kind, parts in ((odd, (own, far)), (1 - odd, (near, cross))):
        for p, part in enumerate(parts):
            copies.start(part, kv.at[kind, :, pl.ds(32 * p, 32)])


def ids_of(table, h):
    return [table[VERT + h * LISTED + e] for e in range(LISTED)]


def slots_of(table, h):
    return [table[jnp.maximum(i, 0)] for i in ids_of(table, h)]


def listed(kv, kind, slots):
    return jnp.concatenate([kv[kind, slot] for slot in slots], axis=0)


def limits(table, places, h):
    return jnp.concatenate([places + jnp.where(i >= 0, i * ROWS, NEVER) for i in ids_of(table, h)], axis=1)


def near_base(table, ids, run, offset):
    block = table[META + 2] + run - offset
    use = block >= 0
    for i in ids:
        use = jnp.logical_and(use, i != block)
    return jnp.where(use, block * ROWS, NEVER)


def product(q, keys):
    return lax.dot_general(q, keys, (((1,), (1,)), ((), ())), preferred_element_type=F32)


def wide(column):
    return jnp.broadcast_to(column, (column.shape[0], HEAD))


def across(column_block, count):
    return jnp.concatenate([column_block] * count, axis=1)


def band_kernel(table, sink, q, w, prev, kc, vc, acc, tops, sums, w_out, qs, band, sems):
    copies = Copies(sems)
    copies.start(q, qs)
    for kind, cur in enumerate((kc, vc)):
        copies.start(cur, band.at[kind, pl.ds(RUNS, RUNS)])
    first = len(copies.made)
    depth = w.shape[0] // 4
    for n in range(4):
        copies.start(w.at[pl.ds(n * depth, depth)], w_out.at[pl.ds(n * depth, depth)])
    for kind in range(2):
        for b in range(RUNS):
            rows = [prev[r, kind, b].astype(F32) for r in range(16)]
            band[kind, b] = jnp.concatenate(rows, axis=0).astype(BF16)
    copies.wait(first)
    token = TOKENS // RUNS * table[META + 2] + lax.broadcasted_iota(jnp.int32, (TOKENS, 1), 0)
    within = lax.broadcasted_iota(jnp.int32, (1, ROWS), 1)
    for h in range(HEADS):
        cols = slice(h * HEAD, (h + 1) * HEAD)
        raw_sink = sink[h:h + 1, :]
        ids = ids_of(table, h)
        offsets = [table[SLASH + h * BANDS + j] for j in range(BANDS)]
        score = []
        for run in range(RUNS):
            rows = slice(run * ROWS, (run + 1) * ROWS)
            keys = jnp.concatenate([band[0, RUNS + run - offset] for offset in offsets], axis=0)
            limit = jnp.concatenate(
                [within + near_base(table, ids, run, offset) for offset in offsets], axis=1)
            score.append(jnp.where(token[rows] >= limit, product(qs[rows, cols], keys), LOW))
        score = jnp.concatenate(score, axis=0)
        top = jnp.maximum(wide(jnp.max(score, axis=1, keepdims=True)), raw_sink)
        weight = jnp.exp2((score - across(top, BANDS)) * FACTOR)
        total = wide(jnp.sum(weight, axis=1, keepdims=True)) + jnp.exp2((raw_sink - top) * FACTOR)
        weight = weight.astype(BF16)
        for run in range(RUNS):
            rows = slice(run * ROWS, (run + 1) * ROWS)
            vals = jnp.concatenate([band[1, RUNS + run - offset] for offset in offsets], axis=0)
            acc[rows, cols] = jnp.dot(weight[rows], vals, preferred_element_type=F32)
        tops[:, cols] = top
        sums[:, cols] = total
    copies.wait()


def add_listed(table, qs, kv, late, acc, tops, sums, put):
    token = TOKENS // RUNS * table[META + 2] + lax.broadcasted_iota(jnp.int32, (TOKENS, 1), 0)
    places = key_places(table, late)
    for h in range(HEADS):
        cols = slice(h * HEAD, (h + 1) * HEAD)
        slots = slots_of(table, h)
        score = product(qs[:, cols], listed(kv, 0, slots))
        score = jnp.where(token >= limits(table, places, h), score, LOW)
        before = tops[:, cols]
        top = jnp.maximum(wide(jnp.max(score, axis=1, keepdims=True)), before)
        weight = jnp.exp2((score - across(top, LISTED * HALF // HEAD)) * FACTOR)
        fade = jnp.exp2((before - top) * FACTOR)
        total = wide(jnp.sum(weight, axis=1, keepdims=True)) + fade * sums[:, cols]
        mixed = jnp.dot(weight.astype(BF16), listed(kv, 1, slots), preferred_element_type=F32)
        put(cols, mixed + acc[:, cols] * fade, top, total)


def early_kernel(table, qs, a0, a2, a1, a3, acc, tops, sums, acc_out, tops_out, sums_out, kv, sems):
    copies = Copies(sems)
    load_half(copies, table[META], a0, a2, a1, a3, kv)
    copies.wait()

    def put(cols, mixed, top, total):
        acc_out[:, cols], tops_out[:, cols], sums_out[:, cols] = mixed, top, total

    add_listed(table, qs, kv, False, acc, tops, sums, put)


def project(att, w, blocks, core, keeps, give):
    def rows(block, side):
        start = pl.multiple_of(block * ROWS + side * HALF, HALF)
        return att[pl.ds(start, HALF), :]

    lhs = jnp.concatenate([rows(b, core) for b in blocks] + [rows(b, 1 - core) for b in blocks], axis=0)
    tile = 512
    for n in range(w.shape[1] // tile):
        cols = slice(n * tile, (n + 1) * tile)
        out = jnp.dot(lhs, w[:, cols], preferred_element_type=F32).astype(BF16)
        for i, keep in enumerate(keeps):
            keep[:, cols] = out[i * HALF:(i + 1) * HALF]
        give(n * tile, tile, out[len(blocks) * HALF:])


def late_kernel(table, qs, w, b0, b2, b1, b3, acc, tops, sums, att, keep, give, kv, sems):
    copies = Copies(sems)
    load_half(copies, table[META], b0, b2, b1, b3, kv)
    copies.wait()

    def put(cols, mixed, top, total):
        att[:, cols] = (mixed * (1.0 / total)).astype(BF16)

    add_listed(table, qs, kv, True, acc, tops, sums, put)
    project(att, w, [(table[META + 5] + 2) % X], table[META + 1], [keep], functools.partial(store, give))


def store(give, start, size, rows):
    give[:, start:start + size] = rows


def sides_kernel(table, att, w, keep_below, keep_above, direct, relayed):
    x, mid = table[META + 5], w.shape[1] // 2

    def give(start, size, rows):
        below, above = rows[:HALF], rows[HALF:]
        at = slice(start % mid, start % mid + size)
        if start < mid:
            relayed[:HALF, at], direct[HALF:, at] = below, above
        else:
            direct[:HALF, at], relayed[HALF:, at] = below, above

    project(att, w, [(x + 1) % X, (x + 3) % X], table[META + 1], [keep_below, keep_above], give)


def own_kernel(table, att, w, after, keep, give):
    project(att, w, [table[META + 5]], table[META + 1], [keep], functools.partial(store, give))


def final_kernel(keep, swapped, left_below, left_above, right_below, right_above, out):
    mid = out.shape[1] // 2
    for start, pair in ((0, (left_below, left_above)), (mid, (right_below, right_above))):
        cols = slice(start, start + mid)
        total = keep[:, cols].astype(F32) + swapped[:, cols].astype(F32)
        for part in pair:
            total = total + part[...].astype(F32)
        out[:, cols] = total.astype(BF16)


SMEM = pl.BlockSpec(memory_space=pltpu.SMEM)
VMEM = pl.BlockSpec(memory_space=pltpu.VMEM)
ANY = pl.BlockSpec(memory_space=pl.ANY)


def call(body, ins, outs, scratch, micros, name):
    return pl.pallas_call(
        body,
        out_shape=tuple(pltpu.VMEM(shape, dtype) for shape, dtype in outs),
        in_specs=ins,
        out_specs=(VMEM,) * len(outs),
        scratch_shapes=scratch,
        compiler_params=pltpu.CompilerParams(vmem_limit_bytes=24 * 2 ** 20),
        cost_estimate=pl.CostEstimate(flops=int(micros * 1e9), bytes_accessed=int(micros * 2 ** 20), transcendentals=0),
        name=name,
    )


def total_of(*terms):
    return functools.reduce(lambda a, b: a + b, [t.astype(F32) for t in terms]).astype(BF16)


def tables(c, x, core, vert_blocks, slash_offsets):
    block = jnp.arange(BLOCKS, dtype=jnp.int32)
    present = jnp.any(vert_blocks[:, :, None] == block, axis=(0, 1)).astype(jnp.int32)
    rank = jnp.sum(jnp.where(block[:, None] > block[None, :], present[None, :], 0), axis=1)
    meta = jnp.stack([c % 2, core, RUNS * c, c // Y, (c % Y) // 2, x]).astype(jnp.int32)
    table = jnp.concatenate([rank, meta, vert_blocks.reshape(-1), slash_offsets.reshape(-1)])
    return jnp.where(present > 0, rank, -1), table


def spread_kernel(keys, values, out, sems):
    copies = Copies(sems)
    for kind, a in enumerate((keys, values)):
        for b in range(RUNS):
            copies.start(a.at[b], out.at[:, kind, b])
    copies.wait()


def per_device(queries, keys, values, sink_logits, vert_blocks, slash_offsets, output_weight):
    c = lax.axis_index("ctx")
    h = lax.axis_index("head")
    x, core = h // 2, h % 2
    keys = keys.reshape(RUNS, ROWS, HEAD)
    values = values.reshape(RUNS, ROWS, HEAD)
    place, table = tables(c, x, core, vert_blocks, slash_offsets)
    sink = jnp.broadcast_to(sink_logits[:, None] * (1.0 / SCALE), (HEADS, HEAD))
    far_keys, far_values = [pltpu.with_memory_space_constraint(a.reshape(RUNS, 16, 8, HEAD), pltpu.HBM)
                            for a in (keys, values)]
    (spread,) = call(
        spread_kernel, [ANY, ANY], [((16, 2, RUNS, 8, HEAD), BF16)], [pltpu.SemaphoreType.DMA((2 * RUNS,))], 1, "spread",
    )(far_keys, far_values)
    spread = spread.reshape(Z * Y, RUNS * 8, HEAD)
    prev = lax.ppermute(spread, "ctx", [(s, s + 1) for s in range(Z * Y - 1)]).reshape(16, 2, RUNS, 8, HEAD)
    got = lax.all_to_all(spread, "ctx", 0, 0, tiled=True).reshape(BLOCKS * 8, HEAD)
    place, table, sink = lax.optimization_barrier((place, table, sink))
    r = jnp.arange(SLOTS * 8, dtype=jnp.int32)[:, None]
    col = jnp.arange(BLOCKS * 8, dtype=jnp.int32)[None, :]
    pick = (jnp.repeat(place, 8)[None, :] == r // 8) & (col % 8 == r % 8)
    mine = jnp.dot(pick.astype(BF16), got, preferred_element_type=F32)
    mine = mine.astype(BF16).reshape(SLOTS, 8, HEAD)

    def from_z(a, offset):
        return lax.ppermute(a, "ctx", z_pairs(-offset))

    z2, z4, z6 = from_z(mine, 2), from_z(mine, 4), from_z(mine, 6)
    prev, z2, z4, z6 = lax.optimization_barrier((prev, z2, z4, z6))
    a0 = jnp.concatenate([mine, z2, z4, z6], axis=1)
    b0 = lax.ppermute(a0, "ctx", [(Y * z + y, Y * (z ^ 1) + y) for z in range(Z) for y in range(Y)])
    a1, a2, a3 = [lax.ppermute(a0, "ctx", y_pairs(f)) for f in (1, 2, 3)]

    width = output_weight.shape[1]
    kv = pltpu.VMEM((2, SLOTS, HALF, HEAD), BF16)
    rows = ((TOKENS, HEADS * HEAD), BF16)
    part = ((HALF, width), BF16)
    far_queries = pltpu.with_memory_space_constraint(queries, pltpu.HBM)
    far_weight = pltpu.with_memory_space_constraint(output_weight, pltpu.HBM)
    state = [((TOKENS, HEADS * HEAD), F32)] * 3
    acc, tops, sums, w, q = call(
        band_kernel, [SMEM, VMEM] + [ANY] * 2 + [VMEM, ANY, ANY], state + [(output_weight.shape, BF16), rows],
        [pltpu.VMEM((2, 2 * RUNS, ROWS, HEAD), BF16), pltpu.SemaphoreType.DMA((7,))], 3, "band",
    )(table, sink, far_queries, far_weight, prev,
      *[pltpu.with_memory_space_constraint(a, pltpu.HBM) for a in (keys, values)])
    b0, acc = lax.optimization_barrier((b0, acc))
    b1, b2, b3 = [lax.ppermute(b0, "ctx", y_pairs(f)) for f in (1, 2, 3)]
    acc, tops, sums = call(
        early_kernel, [SMEM, VMEM] + [ANY] * 4 + [VMEM] * 3, state, [kv, pltpu.SemaphoreType.DMA((4,))], 5, "early",
    )(table, q, a0, a2, a1, a3, acc, tops, sums)
    att, keep_far, give_far = call(
        late_kernel, [SMEM, VMEM, VMEM] + [ANY] * 4 + [VMEM] * 3,
        [rows, part, part], [kv, pltpu.SemaphoreType.DMA((4,))], 0.01, "late",
    )(table, q, w, b0, b2, b1, b3, acc, tops, sums)
    halves = ((2 * HALF, width // 2), BF16)
    keep_below, keep_above, give_direct, give_relayed = call(
        sides_kernel, [SMEM, VMEM, VMEM], [part, part, halves, halves], [], 0.01, "sides",
    )(table, att, w)
    def swap(a):
        return lax.ppermute(a, "head", CORE_PAIRS)

    def to_x(a, step):
        return lax.ppermute(a, "head", x_pairs(step))

    far, direct, relayed = swap(give_far), swap(give_direct), swap(give_relayed)
    mid = width // 2
    far_left = total_of(keep_far[:, :mid], far[:, :mid])
    far_right = total_of(keep_far[:, mid:], far[:, mid:])
    relay_left, relay_right = to_x(far_left, 1), to_x(far_right, -1)
    direct_right = total_of(keep_below[:, mid:], direct[:HALF])
    direct_left = total_of(keep_above[:, :mid], direct[HALF:])
    right_below, left_above = to_x(direct_right, 1), to_x(direct_left, -1)
    keep_own, give_own = call(
        own_kernel, [SMEM, VMEM, VMEM, ANY], [part, part], [], 0.01, "own",
    )(table, att, w, direct_right)

    own = swap(give_own)
    keep_below, keep_above, relayed, relay_left, relay_right = lax.optimization_barrier(
        (keep_below, keep_above, relayed, relay_left, relay_right))
    left_below = to_x(total_of(keep_below[:, :mid], relayed[:HALF], relay_left), 1)
    right_above = to_x(total_of(keep_above[:, mid:], relayed[HALF:], relay_right), -1)
    return pl.pallas_call(
        final_kernel,
        out_shape=jax.ShapeDtypeStruct((HALF, width), BF16),
        in_specs=[VMEM] * 6,
        out_specs=VMEM,
        compiler_params=pltpu.CompilerParams(vmem_limit_bytes=8 * 2 ** 20),
        name="final",
    )(keep_own, own, left_below, left_above, right_below, right_above)


def solution(mesh):
    return jax.shard_map(
        per_device,
        mesh=mesh,
        in_specs=(
            P("ctx", "head"),
            P("ctx", "head"),
            P("ctx", "head"),
            P("head"),
            P("head", None),
            P("head", None),
            P("head", None),
        ),
        out_specs=P(("ctx", "head"), None),
        check_vma=False,
    )
```

```python
import functools

import jax
import jax.numpy as jnp
from jax import lax
from jax.experimental import pallas as pl
from jax.experimental.pallas import tpu as pltpu
from jax.sharding import PartitionSpec as P

HEAD = 128
ROWS = 128
HALF = 64
SLOTS = 24
LISTED = 8
BANDS = 3
BLOCKS = 128
RUNS = 4
HEADS = 8
TOKENS = RUNS * ROWS
SCALE = HEAD ** -0.5
FACTOR = SCALE * 1.4426950408889634
NEVER = 1 << 20
LOW = -1e30
Z, Y, X = 8, 4, 4
BF16, F32 = jnp.bfloat16, jnp.float32
META = BLOCKS
VERT = META + 6
SLASH = VERT + HEADS * LISTED


def z_pairs(step):
    return [(Y * z + y, Y * ((z + step) % Z) + y) for z in range(Z) for y in range(Y)]


def y_pairs(flip):
    return [(Y * z + y, Y * z + (y ^ flip)) for z in range(Z) for y in range(Y)]


def x_pairs(step):
    return [(2 * x + k, 2 * ((x + step) % X) + k) for x in range(X) for k in range(2)]


CORE_PAIRS = [(h, h ^ 1) for h in range(HEADS)]


class Copies:
    def __init__(self, sems):
        self.sems, self.made = sems, []

    def start(self, src, dst):
        made = pltpu.make_async_copy(src, dst, self.sems.at[len(self.made)])
        made.start()
        self.made.append(made)

    def wait(self, count=None):
        for made in self.made[:count]:
            made.wait()
        self.made = [] if count is None else self.made[count:]


def key_places(table, late):
    z, y_half = table[META + 3], table[META + 4]
    n = lax.broadcasted_iota(jnp.int32, (1, HALF), 1)
    part, inner, row = n // 32, (n // 8) % 4, n % 8
    z_of = ((z ^ int(late)) + 2 * inner) % Z
    return (z_of * 2 + (y_half ^ part)) * 8 + row


def load_half(copies, odd, own, far, near, cross, kv):
    for kind, parts in ((odd, (own, far)), (1 - odd, (near, cross))):
        for p, part in enumerate(parts):
            copies.start(part, kv.at[kind, :, pl.ds(32 * p, 32)])


def ids_of(table, h):
    return [table[VERT + h * LISTED + e] for e in range(LISTED)]


def slots_of(table, h):
    return [table[jnp.maximum(i, 0)] for i in ids_of(table, h)]


def listed(kv, kind, slots):
    return jnp.concatenate([kv[kind, slot] for slot in slots], axis=0)


def limits(table, places, h):
    return jnp.concatenate([places + jnp.where(i >= 0, i * ROWS, NEVER) for i in ids_of(table, h)], axis=1)


def near_base(table, ids, run, offset):
    block = table[META + 2] + run - offset
    use = block >= 0
    for i in ids:
        use = jnp.logical_and(use, i != block)
    return jnp.where(use, block * ROWS, NEVER)


def product(q, keys):
    return lax.dot_general(q, keys, (((1,), (1,)), ((), ())), preferred_element_type=F32)


def wide(column):
    return jnp.broadcast_to(column, (column.shape[0], HEAD))


def across(column_block, count):
    return jnp.concatenate([column_block] * count, axis=1)


def fetch_kernel(q, w, kc, vc, spread, qs, w_out, own, sems):
    copies = Copies(sems)
    copies.start(q, qs)
    for kind, cur in enumerate((kc, vc)):
        copies.start(cur, own.at[kind])
    depth = w.shape[0] // 4
    for n in range(4):
        copies.start(w.at[pl.ds(n * depth, depth)], w_out.at[pl.ds(n * depth, depth)])
    copies.wait()


def band_kernel(table, sink, qs, prev, own, acc, tops, sums, band):
    for kind in range(2):
        for b in range(RUNS):
            rows = [prev[r, kind, b].astype(F32) for r in range(16)]
            band[kind, b] = jnp.concatenate(rows, axis=0).astype(BF16)
            band[kind, RUNS + b] = own[kind, b]
    token = TOKENS // RUNS * table[META + 2] + lax.broadcasted_iota(jnp.int32, (TOKENS, 1), 0)
    within = lax.broadcasted_iota(jnp.int32, (1, ROWS), 1)
    for h in range(HEADS):
        cols = slice(h * HEAD, (h + 1) * HEAD)
        raw_sink = sink[h:h + 1, :]
        ids = ids_of(table, h)
        offsets = [table[SLASH + h * BANDS + j] for j in range(BANDS)]
        score = []
        for run in range(RUNS):
            rows = slice(run * ROWS, (run + 1) * ROWS)
            keys = jnp.concatenate([band[0, RUNS + run - offset] for offset in offsets], axis=0)
            limit = jnp.concatenate(
                [within + near_base(table, ids, run, offset) for offset in offsets], axis=1)
            score.append(jnp.where(token[rows] >= limit, product(qs[rows, cols], keys), LOW))
        score = jnp.concatenate(score, axis=0)
        top = jnp.maximum(wide(jnp.max(score, axis=1, keepdims=True)), raw_sink)
        weight = jnp.exp2((score - across(top, BANDS)) * FACTOR)
        total = wide(jnp.sum(weight, axis=1, keepdims=True)) + jnp.exp2((raw_sink - top) * FACTOR)
        weight = weight.astype(BF16)
        for run in range(RUNS):
            rows = slice(run * ROWS, (run + 1) * ROWS)
            vals = jnp.concatenate([band[1, RUNS + run - offset] for offset in offsets], axis=0)
            acc[rows, cols] = jnp.dot(weight[rows], vals, preferred_element_type=F32)
        tops[:, cols] = top
        sums[:, cols] = total


def add_listed(table, qs, kv, late, acc, tops, sums, put):
    token = TOKENS // RUNS * table[META + 2] + lax.broadcasted_iota(jnp.int32, (TOKENS, 1), 0)
    places = key_places(table, late)
    for h in range(HEADS):
        cols = slice(h * HEAD, (h + 1) * HEAD)
        slots = slots_of(table, h)
        score = product(qs[:, cols], listed(kv, 0, slots))
        score = jnp.where(token >= limits(table, places, h), score, LOW)
        before = tops[:, cols]
        top = jnp.maximum(wide(jnp.max(score, axis=1, keepdims=True)), before)
        weight = jnp.exp2((score - across(top, LISTED * HALF // HEAD)) * FACTOR)
        fade = jnp.exp2((before - top) * FACTOR)
        total = wide(jnp.sum(weight, axis=1, keepdims=True)) + fade * sums[:, cols]
        mixed = jnp.dot(weight.astype(BF16), listed(kv, 1, slots), preferred_element_type=F32)
        put(cols, mixed + acc[:, cols] * fade, top, total)


def early_kernel(table, qs, a0, a2, a1, a3, acc, tops, sums, acc_out, tops_out, sums_out, kv, sems):
    copies = Copies(sems)
    load_half(copies, table[META], a0, a2, a1, a3, kv)
    copies.wait()

    def put(cols, mixed, top, total):
        acc_out[:, cols], tops_out[:, cols], sums_out[:, cols] = mixed, top, total

    add_listed(table, qs, kv, False, acc, tops, sums, put)


def project(att, w, blocks, core, keeps, give):
    def rows(block, side):
        start = pl.multiple_of(block * ROWS + side * HALF, HALF)
        return att[pl.ds(start, HALF), :]

    lhs = jnp.concatenate([rows(b, core) for b in blocks] + [rows(b, 1 - core) for b in blocks], axis=0)
    tile = 512
    for n in range(w.shape[1] // tile):
        cols = slice(n * tile, (n + 1) * tile)
        out = jnp.dot(lhs, w[:, cols], preferred_element_type=F32).astype(BF16)
        for i, keep in enumerate(keeps):
            keep[:, cols] = out[i * HALF:(i + 1) * HALF]
        give(n * tile, tile, out[len(blocks) * HALF:])


def late_kernel(table, qs, w, b0, b2, b1, b3, acc, tops, sums, att, keep, give, kv, sems):
    copies = Copies(sems)
    load_half(copies, table[META], b0, b2, b1, b3, kv)
    copies.wait()

    def put(cols, mixed, top, total):
        att[:, cols] = (mixed * (1.0 / total)).astype(BF16)

    add_listed(table, qs, kv, True, acc, tops, sums, put)
    project(att, w, [(table[META + 5] + 2) % X], table[META + 1], [keep], functools.partial(store, give))


def store(give, start, size, rows):
    give[:, start:start + size] = rows


def sides_kernel(table, att, w, keep_below, keep_above, direct, relayed):
    x, mid = table[META + 5], w.shape[1] // 2

    def give(start, size, rows):
        below, above = rows[:HALF], rows[HALF:]
        at = slice(start % mid, start % mid + size)
        if start < mid:
            relayed[:HALF, at], direct[HALF:, at] = below, above
        else:
            direct[:HALF, at], relayed[HALF:, at] = below, above

    project(att, w, [(x + 1) % X, (x + 3) % X], table[META + 1], [keep_below, keep_above], give)


def own_kernel(table, att, w, after, keep, give):
    project(att, w, [table[META + 5]], table[META + 1], [keep], functools.partial(store, give))


def final_kernel(keep, swapped, left_below, left_above, right_below, right_above, out):
    mid = out.shape[1] // 2
    for start, pair in ((0, (left_below, left_above)), (mid, (right_below, right_above))):
        cols = slice(start, start + mid)
        total = keep[:, cols].astype(F32) + swapped[:, cols].astype(F32)
        for part in pair:
            total = total + part[...].astype(F32)
        out[:, cols] = total.astype(BF16)


SMEM = pl.BlockSpec(memory_space=pltpu.SMEM)
VMEM = pl.BlockSpec(memory_space=pltpu.VMEM)
ANY = pl.BlockSpec(memory_space=pl.ANY)


def call(body, ins, outs, scratch, micros, name):
    return pl.pallas_call(
        body,
        out_shape=tuple(pltpu.VMEM(shape, dtype) for shape, dtype in outs),
        in_specs=ins,
        out_specs=(VMEM,) * len(outs),
        scratch_shapes=scratch,
        compiler_params=pltpu.CompilerParams(vmem_limit_bytes=24 * 2 ** 20),
        cost_estimate=pl.CostEstimate(flops=int(micros * 1e9), bytes_accessed=int(micros * 2 ** 20), transcendentals=0),
        name=name,
    )


def total_of(*terms):
    return functools.reduce(lambda a, b: a + b, [t.astype(F32) for t in terms]).astype(BF16)


def tables(c, x, core, vert_blocks, slash_offsets):
    block = jnp.arange(BLOCKS, dtype=jnp.int32)
    present = jnp.any(vert_blocks[:, :, None] == block, axis=(0, 1)).astype(jnp.int32)
    rank = jnp.sum(jnp.where(block[:, None] > block[None, :], present[None, :], 0), axis=1)
    meta = jnp.stack([c % 2, core, RUNS * c, c // Y, (c % Y) // 2, x]).astype(jnp.int32)
    table = jnp.concatenate([rank, meta, vert_blocks.reshape(-1), slash_offsets.reshape(-1)])
    return jnp.where(present > 0, rank, -1), table


def spread_kernel(keys, values, out, sems):
    copies = Copies(sems)
    for kind, a in enumerate((keys, values)):
        for b in range(RUNS):
            copies.start(a.at[b], out.at[:, kind, b])
    copies.wait()


def per_device(queries, keys, values, sink_logits, vert_blocks, slash_offsets, output_weight):
    c = lax.axis_index("ctx")
    h = lax.axis_index("head")
    x, core = h // 2, h % 2
    keys = keys.reshape(RUNS, ROWS, HEAD)
    values = values.reshape(RUNS, ROWS, HEAD)
    place, table = tables(c, x, core, vert_blocks, slash_offsets)
    sink = jnp.broadcast_to(sink_logits[:, None] * (1.0 / SCALE), (HEADS, HEAD))
    far_keys, far_values = [pltpu.with_memory_space_constraint(a.reshape(RUNS, 16, 8, HEAD), pltpu.HBM)
                            for a in (keys, values)]
    (spread,) = call(
        spread_kernel, [ANY, ANY], [((16, 2, RUNS, 8, HEAD), BF16)], [pltpu.SemaphoreType.DMA((2 * RUNS,))], 1, "spread",
    )(far_keys, far_values)
    spread = spread.reshape(Z * Y, RUNS * 8, HEAD)
    prev = lax.ppermute(spread, "ctx", [(s, s + 1) for s in range(Z * Y - 1)]).reshape(16, 2, RUNS, 8, HEAD)
    got = lax.all_to_all(spread, "ctx", 0, 0, tiled=True).reshape(BLOCKS * 8, HEAD)
    rows = ((TOKENS, HEADS * HEAD), BF16)
    q, w, own = call(
        fetch_kernel, [ANY] * 5, [rows, (output_weight.shape, BF16), ((2, RUNS, ROWS, HEAD), BF16)],
        [pltpu.SemaphoreType.DMA((7,))], 4, "fetch",
    )(*[pltpu.with_memory_space_constraint(a, pltpu.HBM) for a in (queries, output_weight, keys, values)], spread)
    place, table, sink, q, w, own = lax.optimization_barrier((place, table, sink, q, w, own))
    r = jnp.arange(SLOTS * 8, dtype=jnp.int32)[:, None]
    col = jnp.arange(BLOCKS * 8, dtype=jnp.int32)[None, :]
    pick = (jnp.repeat(place, 8)[None, :] == r // 8) & (col % 8 == r % 8)
    mine = jnp.dot(pick.astype(BF16), got, preferred_element_type=F32)
    mine = mine.astype(BF16).reshape(SLOTS, 8, HEAD)

    def from_z(a, offset):
        return lax.ppermute(a, "ctx", z_pairs(-offset))

    z2, z4, z6 = from_z(mine, 2), from_z(mine, 4), from_z(mine, 6)
    prev, z2, z4, z6 = lax.optimization_barrier((prev, z2, z4, z6))
    a0 = jnp.concatenate([mine, z2, z4, z6], axis=1)
    b0 = lax.ppermute(a0, "ctx", [(Y * z + y, Y * (z ^ 1) + y) for z in range(Z) for y in range(Y)])
    a1, a2, a3 = [lax.ppermute(a0, "ctx", y_pairs(f)) for f in (1, 2, 3)]

    width = output_weight.shape[1]
    kv = pltpu.VMEM((2, SLOTS, HALF, HEAD), BF16)
    part = ((HALF, width), BF16)
    state = [((TOKENS, HEADS * HEAD), F32)] * 3
    acc, tops, sums = call(
        band_kernel, [SMEM] + [VMEM] * 4, state, [pltpu.VMEM((2, 2 * RUNS, ROWS, HEAD), BF16)], 3, "band",
    )(table, sink, q, prev, own)
    b0, acc = lax.optimization_barrier((b0, acc))
    b1, b2, b3 = [lax.ppermute(b0, "ctx", y_pairs(f)) for f in (1, 2, 3)]
    acc, tops, sums = call(
        early_kernel, [SMEM, VMEM] + [ANY] * 4 + [VMEM] * 3, state, [kv, pltpu.SemaphoreType.DMA((4,))], 5, "early",
    )(table, q, a0, a2, a1, a3, acc, tops, sums)
    att, keep_far, give_far = call(
        late_kernel, [SMEM, VMEM, VMEM] + [ANY] * 4 + [VMEM] * 3,
        [rows, part, part], [kv, pltpu.SemaphoreType.DMA((4,))], 0.01, "late",
    )(table, q, w, b0, b2, b1, b3, acc, tops, sums)
    halves = ((2 * HALF, width // 2), BF16)
    keep_below, keep_above, give_direct, give_relayed = call(
        sides_kernel, [SMEM, VMEM, VMEM], [part, part, halves, halves], [], 0.01, "sides",
    )(table, att, w)
    def swap(a):
        return lax.ppermute(a, "head", CORE_PAIRS)

    def to_x(a, step):
        return lax.ppermute(a, "head", x_pairs(step))

    far, direct, relayed = swap(give_far), swap(give_direct), swap(give_relayed)
    mid = width // 2
    far_left = total_of(keep_far[:, :mid], far[:, :mid])
    far_right = total_of(keep_far[:, mid:], far[:, mid:])
    relay_left, relay_right = to_x(far_left, 1), to_x(far_right, -1)
    direct_right = total_of(keep_below[:, mid:], direct[:HALF])
    direct_left = total_of(keep_above[:, :mid], direct[HALF:])
    right_below, left_above = to_x(direct_right, 1), to_x(direct_left, -1)
    keep_own, give_own = call(
        own_kernel, [SMEM, VMEM, VMEM, ANY], [part, part], [], 0.01, "own",
    )(table, att, w, direct_right)

    own = swap(give_own)
    keep_below, keep_above, relayed, relay_left, relay_right = lax.optimization_barrier(
        (keep_below, keep_above, relayed, relay_left, relay_right))
    left_below = to_x(total_of(keep_below[:, :mid], relayed[:HALF], relay_left), 1)
    right_above = to_x(total_of(keep_above[:, mid:], relayed[HALF:], relay_right), -1)
    return pl.pallas_call(
        final_kernel,
        out_shape=jax.ShapeDtypeStruct((HALF, width), BF16),
        in_specs=[VMEM] * 6,
        out_specs=VMEM,
        compiler_params=pltpu.CompilerParams(vmem_limit_bytes=8 * 2 ** 20),
        name="final",
    )(keep_own, own, left_below, left_above, right_below, right_above)


def solution(mesh):
    return jax.shard_map(
        per_device,
        mesh=mesh,
        in_specs=(
            P("ctx", "head"),
            P("ctx", "head"),
            P("ctx", "head"),
            P("head"),
            P("head", None),
            P("head", None),
            P("head", None),
        ),
        out_specs=P(("ctx", "head"), None),
        check_vma=False,
    )
```

```python
import functools

import jax
import jax.numpy as jnp
from jax import lax
from jax.experimental import pallas as pl
from jax.experimental.pallas import tpu as pltpu
from jax.sharding import PartitionSpec as P

HEAD = 128
ROWS = 128
HALF = 64
SLOTS = 24
LISTED = 8
BANDS = 3
BLOCKS = 128
RUNS = 4
HEADS = 8
TOKENS = RUNS * ROWS
SCALE = HEAD ** -0.5
FACTOR = SCALE * 1.4426950408889634
NEVER = 1 << 20
LOW = -1e30
Z, Y, X = 8, 4, 4
BF16, F32 = jnp.bfloat16, jnp.float32
META = BLOCKS
VERT = META + 6
SLASH = VERT + HEADS * LISTED


def z_pairs(step):
    return [(Y * z + y, Y * ((z + step) % Z) + y) for z in range(Z) for y in range(Y)]


def y_pairs(flip):
    return [(Y * z + y, Y * z + (y ^ flip)) for z in range(Z) for y in range(Y)]


def x_pairs(step):
    return [(2 * x + k, 2 * ((x + step) % X) + k) for x in range(X) for k in range(2)]


CORE_PAIRS = [(h, h ^ 1) for h in range(HEADS)]


class Copies:
    def __init__(self, sems):
        self.sems, self.made = sems, []

    def start(self, src, dst):
        made = pltpu.make_async_copy(src, dst, self.sems.at[len(self.made)])
        made.start()
        self.made.append(made)

    def wait(self, count=None):
        for made in self.made[:count]:
            made.wait()
        self.made = [] if count is None else self.made[count:]


def key_places(table, late):
    z, y_half = table[META + 3], table[META + 4]
    n = lax.broadcasted_iota(jnp.int32, (1, HALF), 1)
    part, inner, row = n // 32, (n // 8) % 4, n % 8
    z_of = ((z ^ int(late)) + 2 * inner) % Z
    return (z_of * 2 + (y_half ^ part)) * 8 + row


def load_half(copies, odd, own, far, near, cross, kv):
    for kind, parts in ((odd, (own, far)), (1 - odd, (near, cross))):
        for p, part in enumerate(parts):
            copies.start(part, kv.at[kind, :, pl.ds(32 * p, 32)])


def ids_of(table, h):
    return [table[VERT + h * LISTED + e] for e in range(LISTED)]


def slots_of(table, h):
    return [table[jnp.maximum(i, 0)] for i in ids_of(table, h)]


def listed(kv, kind, slots):
    return jnp.concatenate([kv[kind, slot] for slot in slots], axis=0)


def limits(table, places, h):
    return jnp.concatenate([places + jnp.where(i >= 0, i * ROWS, NEVER) for i in ids_of(table, h)], axis=1)


def near_base(table, ids, run, offset):
    block = table[META + 2] + run - offset
    use = block >= 0
    for i in ids:
        use = jnp.logical_and(use, i != block)
    return jnp.where(use, block * ROWS, NEVER)


def product(q, keys):
    return lax.dot_general(q, keys, (((1,), (1,)), ((), ())), preferred_element_type=F32)


def wide(column):
    return jnp.broadcast_to(column, (column.shape[0], HEAD))


def across(column_block, count):
    return jnp.concatenate([column_block] * count, axis=1)


def fetch_kernel(q, kc, vc, spread, qs, own, sems):
    copies = Copies(sems)
    half = q.shape[0] // 2
    for n in range(2):
        copies.start(q.at[pl.ds(n * half, half)], qs.at[pl.ds(n * half, half)])
    for kind, cur in enumerate((kc, vc)):
        copies.start(cur, own.at[kind])
    copies.wait()


def band_kernel(table, sink, qs, prev, own, acc, tops, sums, band):
    for kind in range(2):
        for b in range(RUNS):
            rows = [prev[r, kind, b].astype(F32) for r in range(16)]
            band[kind, b] = jnp.concatenate(rows, axis=0).astype(BF16)
            band[kind, RUNS + b] = own[kind, b]
    token = TOKENS // RUNS * table[META + 2] + lax.broadcasted_iota(jnp.int32, (TOKENS, 1), 0)
    within = lax.broadcasted_iota(jnp.int32, (1, ROWS), 1)
    for h in range(HEADS):
        cols = slice(h * HEAD, (h + 1) * HEAD)
        raw_sink = sink[h:h + 1, :]
        ids = ids_of(table, h)
        offsets = [table[SLASH + h * BANDS + j] for j in range(BANDS)]
        score = []
        for run in range(RUNS):
            rows = slice(run * ROWS, (run + 1) * ROWS)
            keys = jnp.concatenate([band[0, RUNS + run - offset] for offset in offsets], axis=0)
            limit = jnp.concatenate(
                [within + near_base(table, ids, run, offset) for offset in offsets], axis=1)
            score.append(jnp.where(token[rows] >= limit, product(qs[rows, cols], keys), LOW))
        score = jnp.concatenate(score, axis=0)
        top = jnp.maximum(wide(jnp.max(score, axis=1, keepdims=True)), raw_sink)
        weight = jnp.exp2((score - across(top, BANDS)) * FACTOR)
        total = wide(jnp.sum(weight, axis=1, keepdims=True)) + jnp.exp2((raw_sink - top) * FACTOR)
        weight = weight.astype(BF16)
        for run in range(RUNS):
            rows = slice(run * ROWS, (run + 1) * ROWS)
            vals = jnp.concatenate([band[1, RUNS + run - offset] for offset in offsets], axis=0)
            acc[rows, cols] = jnp.dot(weight[rows], vals, preferred_element_type=F32)
        tops[:, cols] = top
        sums[:, cols] = total


def add_listed(table, qs, kv, late, acc, tops, sums, put):
    token = TOKENS // RUNS * table[META + 2] + lax.broadcasted_iota(jnp.int32, (TOKENS, 1), 0)
    places = key_places(table, late)
    for h in range(HEADS):
        cols = slice(h * HEAD, (h + 1) * HEAD)
        slots = slots_of(table, h)
        score = product(qs[:, cols], listed(kv, 0, slots))
        score = jnp.where(token >= limits(table, places, h), score, LOW)
        before = tops[:, cols]
        top = jnp.maximum(wide(jnp.max(score, axis=1, keepdims=True)), before)
        weight = jnp.exp2((score - across(top, LISTED * HALF // HEAD)) * FACTOR)
        fade = jnp.exp2((before - top) * FACTOR)
        total = wide(jnp.sum(weight, axis=1, keepdims=True)) + fade * sums[:, cols]
        mixed = jnp.dot(weight.astype(BF16), listed(kv, 1, slots), preferred_element_type=F32)
        put(cols, mixed + acc[:, cols] * fade, top, total)


def early_kernel(table, qs, w, a0, a2, a1, a3, acc, tops, sums, acc_out, tops_out, sums_out, w_out, kv, sems):
    copies = Copies(sems)
    load_half(copies, table[META], a0, a2, a1, a3, kv)
    first = len(copies.made)
    depth = w.shape[0] // 4
    for n in range(4):
        copies.start(w.at[pl.ds(n * depth, depth)], w_out.at[pl.ds(n * depth, depth)])
    copies.wait(first)

    def put(cols, mixed, top, total):
        acc_out[:, cols], tops_out[:, cols], sums_out[:, cols] = mixed, top, total

    add_listed(table, qs, kv, False, acc, tops, sums, put)
    copies.wait()


def project(att, w, blocks, core, keeps, give):
    def rows(block, side):
        start = pl.multiple_of(block * ROWS + side * HALF, HALF)
        return att[pl.ds(start, HALF), :]

    lhs = jnp.concatenate([rows(b, core) for b in blocks] + [rows(b, 1 - core) for b in blocks], axis=0)
    tile = 512
    for n in range(w.shape[1] // tile):
        cols = slice(n * tile, (n + 1) * tile)
        out = jnp.dot(lhs, w[:, cols], preferred_element_type=F32).astype(BF16)
        for i, keep in enumerate(keeps):
            keep[:, cols] = out[i * HALF:(i + 1) * HALF]
        give(n * tile, tile, out[len(blocks) * HALF:])


def late_kernel(table, qs, w, b0, b2, b1, b3, acc, tops, sums, att, keep, give, kv, sems):
    copies = Copies(sems)
    load_half(copies, table[META], b0, b2, b1, b3, kv)
    copies.wait()

    def put(cols, mixed, top, total):
        att[:, cols] = (mixed * (1.0 / total)).astype(BF16)

    add_listed(table, qs, kv, True, acc, tops, sums, put)
    project(att, w, [(table[META + 5] + 2) % X], table[META + 1], [keep], functools.partial(store, give))


def store(give, start, size, rows):
    give[:, start:start + size] = rows


def sides_kernel(table, att, w, keep_below, keep_above, direct, relayed):
    x, mid = table[META + 5], w.shape[1] // 2

    def give(start, size, rows):
        below, above = rows[:HALF], rows[HALF:]
        at = slice(start % mid, start % mid + size)
        if start < mid:
            relayed[:HALF, at], direct[HALF:, at] = below, above
        else:
            direct[:HALF, at], relayed[HALF:, at] = below, above

    project(att, w, [(x + 1) % X, (x + 3) % X], table[META + 1], [keep_below, keep_above], give)


def own_kernel(table, att, w, after, keep, give):
    project(att, w, [table[META + 5]], table[META + 1], [keep], functools.partial(store, give))


def final_kernel(keep, swapped, left_below, left_above, right_below, right_above, out):
    mid = out.shape[1] // 2
    for start, pair in ((0, (left_below, left_above)), (mid, (right_below, right_above))):
        cols = slice(start, start + mid)
        total = keep[:, cols].astype(F32) + swapped[:, cols].astype(F32)
        for part in pair:
            total = total + part[...].astype(F32)
        out[:, cols] = total.astype(BF16)


SMEM = pl.BlockSpec(memory_space=pltpu.SMEM)
VMEM = pl.BlockSpec(memory_space=pltpu.VMEM)
ANY = pl.BlockSpec(memory_space=pl.ANY)


def call(body, ins, outs, scratch, micros, name):
    return pl.pallas_call(
        body,
        out_shape=tuple(pltpu.VMEM(shape, dtype) for shape, dtype in outs),
        in_specs=ins,
        out_specs=(VMEM,) * len(outs),
        scratch_shapes=scratch,
        compiler_params=pltpu.CompilerParams(vmem_limit_bytes=24 * 2 ** 20),
        cost_estimate=pl.CostEstimate(flops=int(micros * 1e9), bytes_accessed=int(micros * 2 ** 20), transcendentals=0),
        name=name,
    )


def total_of(*terms):
    return functools.reduce(lambda a, b: a + b, [t.astype(F32) for t in terms]).astype(BF16)


def tables(c, x, core, vert_blocks, slash_offsets):
    block = jnp.arange(BLOCKS, dtype=jnp.int32)
    present = jnp.any(vert_blocks[:, :, None] == block, axis=(0, 1)).astype(jnp.int32)
    rank = jnp.sum(jnp.where(block[:, None] > block[None, :], present[None, :], 0), axis=1)
    meta = jnp.stack([c % 2, core, RUNS * c, c // Y, (c % Y) // 2, x]).astype(jnp.int32)
    table = jnp.concatenate([rank, meta, vert_blocks.reshape(-1), slash_offsets.reshape(-1)])
    return jnp.where(present > 0, rank, -1), table


def spread_kernel(keys, values, out, sems):
    copies = Copies(sems)
    for kind, a in enumerate((keys, values)):
        for b in range(RUNS):
            copies.start(a.at[b], out.at[:, kind, b])
    copies.wait()


def per_device(queries, keys, values, sink_logits, vert_blocks, slash_offsets, output_weight):
    c = lax.axis_index("ctx")
    h = lax.axis_index("head")
    x, core = h // 2, h % 2
    keys = keys.reshape(RUNS, ROWS, HEAD)
    values = values.reshape(RUNS, ROWS, HEAD)
    place, table = tables(c, x, core, vert_blocks, slash_offsets)
    sink = jnp.broadcast_to(sink_logits[:, None] * (1.0 / SCALE), (HEADS, HEAD))
    far_keys, far_values = [pltpu.with_memory_space_constraint(a.reshape(RUNS, 16, 8, HEAD), pltpu.HBM)
                            for a in (keys, values)]
    (spread,) = call(
        spread_kernel, [ANY, ANY], [((16, 2, RUNS, 8, HEAD), BF16)], [pltpu.SemaphoreType.DMA((2 * RUNS,))], 1, "spread",
    )(far_keys, far_values)
    spread = spread.reshape(Z * Y, RUNS * 8, HEAD)
    prev = lax.ppermute(spread, "ctx", [(s, s + 1) for s in range(Z * Y - 1)]).reshape(16, 2, RUNS, 8, HEAD)
    got = lax.all_to_all(spread, "ctx", 0, 0, tiled=True).reshape(BLOCKS * 8, HEAD)
    rows = ((TOKENS, HEADS * HEAD), BF16)
    q, own = call(
        fetch_kernel, [ANY] * 4, [rows, ((2, RUNS, ROWS, HEAD), BF16)], [pltpu.SemaphoreType.DMA((4,))], 1, "fetch",
    )(*[pltpu.with_memory_space_constraint(a, pltpu.HBM) for a in (queries, keys, values)], spread)
    place, table, sink, q, own = lax.optimization_barrier((place, table, sink, q, own))
    r = jnp.arange(SLOTS * 8, dtype=jnp.int32)[:, None]
    col = jnp.arange(BLOCKS * 8, dtype=jnp.int32)[None, :]
    pick = (jnp.repeat(place, 8)[None, :] == r // 8) & (col % 8 == r % 8)
    mine = jnp.dot(pick.astype(BF16), got, preferred_element_type=F32)
    mine = mine.astype(BF16).reshape(SLOTS, 8, HEAD)

    def from_z(a, offset):
        return lax.ppermute(a, "ctx", z_pairs(-offset))

    z2, z4, z6 = from_z(mine, 2), from_z(mine, 4), from_z(mine, 6)
    prev, z2, z4, z6 = lax.optimization_barrier((prev, z2, z4, z6))
    a0 = jnp.concatenate([mine, z2, z4, z6], axis=1)
    b0 = lax.ppermute(a0, "ctx", [(Y * z + y, Y * (z ^ 1) + y) for z in range(Z) for y in range(Y)])
    a1, a2, a3 = [lax.ppermute(a0, "ctx", y_pairs(f)) for f in (1, 2, 3)]

    width = output_weight.shape[1]
    kv = pltpu.VMEM((2, SLOTS, HALF, HEAD), BF16)
    part = ((HALF, width), BF16)
    state = [((TOKENS, HEADS * HEAD), F32)] * 3
    acc, tops, sums = call(
        band_kernel, [SMEM] + [VMEM] * 4, state, [pltpu.VMEM((2, 2 * RUNS, ROWS, HEAD), BF16)], 3, "band",
    )(table, sink, q, prev, own)
    b0, acc = lax.optimization_barrier((b0, acc))
    b1, b2, b3 = [lax.ppermute(b0, "ctx", y_pairs(f)) for f in (1, 2, 3)]
    acc, tops, sums, w = call(
        early_kernel, [SMEM, VMEM] + [ANY] * 5 + [VMEM] * 3, state + [(output_weight.shape, BF16)],
        [kv, pltpu.SemaphoreType.DMA((8,))], 5, "early",
    )(table, q, pltpu.with_memory_space_constraint(output_weight, pltpu.HBM), a0, a2, a1, a3, acc, tops, sums)
    att, keep_far, give_far = call(
        late_kernel, [SMEM, VMEM, VMEM] + [ANY] * 4 + [VMEM] * 3,
        [rows, part, part], [kv, pltpu.SemaphoreType.DMA((4,))], 0.01, "late",
    )(table, q, w, b0, b2, b1, b3, acc, tops, sums)
    halves = ((2 * HALF, width // 2), BF16)
    keep_below, keep_above, give_direct, give_relayed = call(
        sides_kernel, [SMEM, VMEM, VMEM], [part, part, halves, halves], [], 0.01, "sides",
    )(table, att, w)
    def swap(a):
        return lax.ppermute(a, "head", CORE_PAIRS)

    def to_x(a, step):
        return lax.ppermute(a, "head", x_pairs(step))

    far, direct, relayed = swap(give_far), swap(give_direct), swap(give_relayed)
    mid = width // 2
    far_left = total_of(keep_far[:, :mid], far[:, :mid])
    far_right = total_of(keep_far[:, mid:], far[:, mid:])
    relay_left, relay_right = to_x(far_left, 1), to_x(far_right, -1)
    direct_right = total_of(keep_below[:, mid:], direct[:HALF])
    direct_left = total_of(keep_above[:, :mid], direct[HALF:])
    right_below, left_above = to_x(direct_right, 1), to_x(direct_left, -1)
    keep_own, give_own = call(
        own_kernel, [SMEM, VMEM, VMEM, ANY], [part, part], [], 0.01, "own",
    )(table, att, w, direct_right)

    own = swap(give_own)
    keep_below, keep_above, relayed, relay_left, relay_right = lax.optimization_barrier(
        (keep_below, keep_above, relayed, relay_left, relay_right))
    left_below = to_x(total_of(keep_below[:, :mid], relayed[:HALF], relay_left), 1)
    right_above = to_x(total_of(keep_above[:, mid:], relayed[HALF:], relay_right), -1)
    return pl.pallas_call(
        final_kernel,
        out_shape=jax.ShapeDtypeStruct((HALF, width), BF16),
        in_specs=[VMEM] * 6,
        out_specs=VMEM,
        compiler_params=pltpu.CompilerParams(vmem_limit_bytes=8 * 2 ** 20),
        name="final",
    )(keep_own, own, left_below, left_above, right_below, right_above)


def solution(mesh):
    return jax.shard_map(
        per_device,
        mesh=mesh,
        in_specs=(
            P("ctx", "head"),
            P("ctx", "head"),
            P("ctx", "head"),
            P("head"),
            P("head", None),
            P("head", None),
            P("head", None),
        ),
        out_specs=P(("ctx", "head"), None),
        check_vma=False,
    )
```

```python
import functools

import jax
import jax.numpy as jnp
from jax import lax
from jax.experimental import pallas as pl
from jax.experimental.pallas import tpu as pltpu
from jax.sharding import PartitionSpec as P

HEAD = 128
ROWS = 128
HALF = 64
SLOTS = 24
LISTED = 8
BANDS = 3
BLOCKS = 128
RUNS = 4
HEADS = 8
TOKENS = RUNS * ROWS
SCALE = HEAD ** -0.5
FACTOR = SCALE * 1.4426950408889634
NEVER = 1 << 20
LOW = -1e30
Z, Y, X = 8, 4, 4
BF16, F32 = jnp.bfloat16, jnp.float32
META = BLOCKS
VERT = META + 6
SLASH = VERT + HEADS * LISTED


def z_pairs(step):
    return [(Y * z + y, Y * ((z + step) % Z) + y) for z in range(Z) for y in range(Y)]


def y_pairs(flip):
    return [(Y * z + y, Y * z + (y ^ flip)) for z in range(Z) for y in range(Y)]


def x_pairs(step):
    return [(2 * x + k, 2 * ((x + step) % X) + k) for x in range(X) for k in range(2)]


CORE_PAIRS = [(h, h ^ 1) for h in range(HEADS)]


class Copies:
    def __init__(self, sems):
        self.sems, self.made = sems, []

    def start(self, src, dst):
        made = pltpu.make_async_copy(src, dst, self.sems.at[len(self.made)])
        made.start()
        self.made.append(made)

    def wait(self, count=None):
        for made in self.made[:count]:
            made.wait()
        self.made = [] if count is None else self.made[count:]


def key_places(table, late):
    z, y_half = table[META + 3], table[META + 4]
    n = lax.broadcasted_iota(jnp.int32, (1, HALF), 1)
    part, inner, row = n // 32, (n // 8) % 4, n % 8
    z_of = ((z ^ int(late)) + 2 * inner) % Z
    return (z_of * 2 + (y_half ^ part)) * 8 + row


def load_half(copies, odd, own, far, near, cross, kv):
    for kind, parts in ((odd, (own, far)), (1 - odd, (near, cross))):
        for p, part in enumerate(parts):
            copies.start(part, kv.at[kind, :, pl.ds(32 * p, 32)])


def ids_of(table, h):
    return [table[VERT + h * LISTED + e] for e in range(LISTED)]


def slots_of(table, h):
    return [table[jnp.maximum(i, 0)] for i in ids_of(table, h)]


def listed(kv, kind, slots):
    return jnp.concatenate([kv[kind, slot] for slot in slots], axis=0)


def limits(table, places, h):
    return jnp.concatenate([places + jnp.where(i >= 0, i * ROWS, NEVER) for i in ids_of(table, h)], axis=1)


def near_base(table, ids, run, offset):
    block = table[META + 2] + run - offset
    use = block >= 0
    for i in ids:
        use = jnp.logical_and(use, i != block)
    return jnp.where(use, block * ROWS, NEVER)


def product(q, keys):
    return lax.dot_general(q, keys, (((1,), (1,)), ((), ())), preferred_element_type=F32)


def wide(column):
    return jnp.broadcast_to(column, (column.shape[0], HEAD))


def across(column_block, count):
    return jnp.concatenate([column_block] * count, axis=1)


def fetch_kernel(q, kc, vc, spread, qs, own, sems):
    copies = Copies(sems)
    half = q.shape[0] // 2
    for n in range(2):
        copies.start(q.at[pl.ds(n * half, half)], qs.at[pl.ds(n * half, half)])
    for kind, cur in enumerate((kc, vc)):
        copies.start(cur, own.at[kind])
    copies.wait()


def band_kernel(table, sink, qs, prev, own, acc, tops, sums, band):
    for kind in range(2):
        for b in range(RUNS):
            rows = [prev[r, kind, b].astype(F32) for r in range(16)]
            band[kind, b] = jnp.concatenate(rows, axis=0).astype(BF16)
            band[kind, RUNS + b] = own[kind, b]
    token = TOKENS // RUNS * table[META + 2] + lax.broadcasted_iota(jnp.int32, (TOKENS, 1), 0)
    within = lax.broadcasted_iota(jnp.int32, (1, ROWS), 1)
    for h in range(HEADS):
        cols = slice(h * HEAD, (h + 1) * HEAD)
        raw_sink = sink[h:h + 1, :]
        ids = ids_of(table, h)
        offsets = [table[SLASH + h * BANDS + j] for j in range(BANDS)]
        score = []
        for run in range(RUNS):
            rows = slice(run * ROWS, (run + 1) * ROWS)
            keys = jnp.concatenate([band[0, RUNS + run - offset] for offset in offsets], axis=0)
            limit = jnp.concatenate(
                [within + near_base(table, ids, run, offset) for offset in offsets], axis=1)
            score.append(jnp.where(token[rows] >= limit, product(qs[rows, cols], keys), LOW))
        score = jnp.concatenate(score, axis=0)
        top = jnp.maximum(wide(jnp.max(score, axis=1, keepdims=True)), raw_sink)
        weight = jnp.exp2((score - across(top, BANDS)) * FACTOR)
        total = wide(jnp.sum(weight, axis=1, keepdims=True)) + jnp.exp2((raw_sink - top) * FACTOR)
        weight = weight.astype(BF16)
        for run in range(RUNS):
            rows = slice(run * ROWS, (run + 1) * ROWS)
            vals = jnp.concatenate([band[1, RUNS + run - offset] for offset in offsets], axis=0)
            acc[rows, cols] = jnp.dot(weight[rows], vals, preferred_element_type=F32)
        tops[:, cols] = top
        sums[:, cols] = total


def add_listed(table, qs, kv, late, acc, tops, sums, put):
    token = TOKENS // RUNS * table[META + 2] + lax.broadcasted_iota(jnp.int32, (TOKENS, 1), 0)
    places = key_places(table, late)
    for h in range(HEADS):
        cols = slice(h * HEAD, (h + 1) * HEAD)
        slots = slots_of(table, h)
        score = product(qs[:, cols], listed(kv, 0, slots))
        score = jnp.where(token >= limits(table, places, h), score, LOW)
        before = tops[:, cols]
        top = jnp.maximum(wide(jnp.max(score, axis=1, keepdims=True)), before)
        weight = jnp.exp2((score - across(top, LISTED * HALF // HEAD)) * FACTOR)
        fade = jnp.exp2((before - top) * FACTOR)
        total = wide(jnp.sum(weight, axis=1, keepdims=True)) + fade * sums[:, cols]
        mixed = jnp.dot(weight.astype(BF16), listed(kv, 1, slots), preferred_element_type=F32)
        put(cols, mixed + acc[:, cols] * fade, top, total)


def early_kernel(table, qs, w, a0, a2, a1, a3, acc, tops, sums, acc_out, tops_out, sums_out, w_out, kv, sems):
    copies = Copies(sems)
    load_half(copies, table[META], a0, a2, a1, a3, kv)
    first = len(copies.made)
    depth = w.shape[0] // 4
    for n in range(4):
        copies.start(w.at[pl.ds(n * depth, depth)], w_out.at[pl.ds(n * depth, depth)])
    copies.wait(first)

    def put(cols, mixed, top, total):
        acc_out[:, cols], tops_out[:, cols], sums_out[:, cols] = mixed, top, total

    add_listed(table, qs, kv, False, acc, tops, sums, put)
    copies.wait()


def project(att, w, blocks, core, keeps, give):
    def rows(block, side):
        start = pl.multiple_of(block * ROWS + side * HALF, HALF)
        return att[pl.ds(start, HALF), :]

    lhs = jnp.concatenate([rows(b, core) for b in blocks] + [rows(b, 1 - core) for b in blocks], axis=0)
    tile = 512
    for n in range(w.shape[1] // tile):
        cols = slice(n * tile, (n + 1) * tile)
        out = jnp.dot(lhs, w[:, cols], preferred_element_type=F32).astype(BF16)
        for i, keep in enumerate(keeps):
            keep[:, cols] = out[i * HALF:(i + 1) * HALF]
        give(n * tile, tile, out[len(blocks) * HALF:])


def late_kernel(table, qs, w, b0, b2, b1, b3, acc, tops, sums, att, keep, give, kv, sems):
    copies = Copies(sems)
    load_half(copies, table[META], b0, b2, b1, b3, kv)
    copies.wait()

    def put(cols, mixed, top, total):
        att[:, cols] = (mixed * (1.0 / total)).astype(BF16)

    add_listed(table, qs, kv, True, acc, tops, sums, put)
    project(att, w, [(table[META + 5] + 2) % X], table[META + 1], [keep], functools.partial(store, give))


def store(give, start, size, rows):
    give[:, start:start + size] = rows


def sides_kernel(table, att, w, keep_below, keep_above, direct, relayed):
    x, mid = table[META + 5], w.shape[1] // 2

    def give(start, size, rows):
        below, above = rows[:HALF], rows[HALF:]
        at = slice(start % mid, start % mid + size)
        if start < mid:
            relayed[:HALF, at], direct[HALF:, at] = below, above
        else:
            direct[:HALF, at], relayed[HALF:, at] = below, above

    project(att, w, [(x + 1) % X, (x + 3) % X], table[META + 1], [keep_below, keep_above], give)


def own_kernel(table, att, w, after, keep, give):
    project(att, w, [table[META + 5]], table[META + 1], [keep], functools.partial(store, give))


def final_kernel(keep, swapped, left_below, left_above, right_below, right_above, out):
    mid = out.shape[1] // 2
    for start, pair in ((0, (left_below, left_above)), (mid, (right_below, right_above))):
        cols = slice(start, start + mid)
        total = keep[:, cols].astype(F32) + swapped[:, cols].astype(F32)
        for part in pair:
            total = total + part[...].astype(F32)
        out[:, cols] = total.astype(BF16)


SMEM = pl.BlockSpec(memory_space=pltpu.SMEM)
VMEM = pl.BlockSpec(memory_space=pltpu.VMEM)
ANY = pl.BlockSpec(memory_space=pl.ANY)


def call(body, ins, outs, scratch, micros, name):
    return pl.pallas_call(
        body,
        out_shape=tuple(pltpu.VMEM(shape, dtype) for shape, dtype in outs),
        in_specs=ins,
        out_specs=(VMEM,) * len(outs),
        scratch_shapes=scratch,
        compiler_params=pltpu.CompilerParams(vmem_limit_bytes=24 * 2 ** 20),
        cost_estimate=pl.CostEstimate(flops=int(micros * 1e9), bytes_accessed=int(micros * 2 ** 20), transcendentals=0),
        name=name,
    )


def total_of(*terms):
    return functools.reduce(lambda a, b: a + b, [t.astype(F32) for t in terms]).astype(BF16)


def tables(c, x, core, vert_blocks, slash_offsets):
    block = jnp.arange(BLOCKS, dtype=jnp.int32)
    present = jnp.any(vert_blocks[:, :, None] == block, axis=(0, 1)).astype(jnp.int32)
    rank = jnp.sum(jnp.where(block[:, None] > block[None, :], present[None, :], 0), axis=1)
    meta = jnp.stack([c % 2, core, RUNS * c, c // Y, (c % Y) // 2, x]).astype(jnp.int32)
    table = jnp.concatenate([rank, meta, vert_blocks.reshape(-1), slash_offsets.reshape(-1)])
    return jnp.where(present > 0, rank, -1), table


def spread_kernel(keys, values, out, sems):
    copies = Copies(sems)
    for kind, a in enumerate((keys, values)):
        for b in range(RUNS):
            copies.start(a.at[b], out.at[:, kind, b])
    copies.wait()


def per_device(queries, keys, values, sink_logits, vert_blocks, slash_offsets, output_weight):
    c = lax.axis_index("ctx")
    h = lax.axis_index("head")
    x, core = h // 2, h % 2
    keys = keys.reshape(RUNS, ROWS, HEAD)
    values = values.reshape(RUNS, ROWS, HEAD)
    place, table = tables(c, x, core, vert_blocks, slash_offsets)
    sink = jnp.broadcast_to(sink_logits[:, None] * (1.0 / SCALE), (HEADS, HEAD))
    far_keys, far_values = [pltpu.with_memory_space_constraint(a.reshape(RUNS, 16, 8, HEAD), pltpu.HBM)
                            for a in (keys, values)]
    (spread,) = call(
        spread_kernel, [ANY, ANY], [((16, 2, RUNS, 8, HEAD), BF16)], [pltpu.SemaphoreType.DMA((2 * RUNS,))], 1, "spread",
    )(far_keys, far_values)
    spread = spread.reshape(Z * Y, RUNS * 8, HEAD)
    prev = lax.ppermute(spread, "ctx", [(s, s + 1) for s in range(Z * Y - 1)]).reshape(16, 2, RUNS, 8, HEAD)
    got = lax.all_to_all(spread, "ctx", 0, 0, tiled=True).reshape(BLOCKS * 8, HEAD)
    rows = ((TOKENS, HEADS * HEAD), BF16)
    q, own = call(
        fetch_kernel, [ANY] * 4, [rows, ((2, RUNS, ROWS, HEAD), BF16)], [pltpu.SemaphoreType.DMA((4,))], 1, "fetch",
    )(*[pltpu.with_memory_space_constraint(a, pltpu.HBM) for a in (queries, keys, values)], spread)
    place, table, sink, q, own = lax.optimization_barrier((place, table, sink, q, own))
    r = jnp.arange(SLOTS * 8, dtype=jnp.int32)[:, None]
    col = jnp.arange(BLOCKS * 8, dtype=jnp.int32)[None, :]
    pick = (jnp.repeat(place, 8)[None, :] == r // 8) & (col % 8 == r % 8)
    mine = jnp.dot(pick.astype(BF16), got, preferred_element_type=F32)
    mine = mine.astype(BF16).reshape(SLOTS, 8, HEAD)

    def from_z(a, offset):
        return lax.ppermute(a, "ctx", z_pairs(-offset))

    z2, z4, z6 = from_z(mine, 2), from_z(mine, 4), from_z(mine, 6)
    prev, z2, z4, z6 = lax.optimization_barrier((prev, z2, z4, z6))
    a0 = jnp.concatenate([mine, z2, z4, z6], axis=1)
    beside = [(Y * z + y, Y * (z ^ 1) + y) for z in range(Z) for y in range(Y)]
    b0 = lax.ppermute(a0, "ctx", beside)
    a1, a2, a3 = [lax.ppermute(a0, "ctx", y_pairs(f)) for f in (1, 2, 3)]

    width = output_weight.shape[1]
    kv = pltpu.VMEM((2, SLOTS, HALF, HEAD), BF16)
    part = ((HALF, width), BF16)
    state = [((TOKENS, HEADS * HEAD), F32)] * 3
    acc, tops, sums = call(
        band_kernel, [SMEM] + [VMEM] * 4, state, [pltpu.VMEM((2, 2 * RUNS, ROWS, HEAD), BF16)], 3, "band",
    )(table, sink, q, prev, own)
    b0, acc = lax.optimization_barrier((b0, acc))
    b1, b3 = [lax.ppermute(b0, "ctx", y_pairs(f)) for f in (1, 3)]
    b2 = lax.ppermute(a2, "ctx", beside)
    acc, tops, sums, w = call(
        early_kernel, [SMEM, VMEM] + [ANY] * 5 + [VMEM] * 3, state + [(output_weight.shape, BF16)],
        [kv, pltpu.SemaphoreType.DMA((8,))], 5, "early",
    )(table, q, pltpu.with_memory_space_constraint(output_weight, pltpu.HBM), a0, a2, a1, a3, acc, tops, sums)
    att, keep_far, give_far = call(
        late_kernel, [SMEM, VMEM, VMEM] + [ANY] * 4 + [VMEM] * 3,
        [rows, part, part], [kv, pltpu.SemaphoreType.DMA((4,))], 0.01, "late",
    )(table, q, w, b0, b2, b1, b3, acc, tops, sums)
    halves = ((2 * HALF, width // 2), BF16)
    keep_below, keep_above, give_direct, give_relayed = call(
        sides_kernel, [SMEM, VMEM, VMEM], [part, part, halves, halves], [], 0.01, "sides",
    )(table, att, w)
    def swap(a):
        return lax.ppermute(a, "head", CORE_PAIRS)

    def to_x(a, step):
        return lax.ppermute(a, "head", x_pairs(step))

    far, direct, relayed = swap(give_far), swap(give_direct), swap(give_relayed)
    mid = width // 2
    far_left = total_of(keep_far[:, :mid], far[:, :mid])
    far_right = total_of(keep_far[:, mid:], far[:, mid:])
    relay_left, relay_right = to_x(far_left, 1), to_x(far_right, -1)
    direct_right = total_of(keep_below[:, mid:], direct[:HALF])
    direct_left = total_of(keep_above[:, :mid], direct[HALF:])
    right_below, left_above = to_x(direct_right, 1), to_x(direct_left, -1)
    keep_own, give_own = call(
        own_kernel, [SMEM, VMEM, VMEM, ANY], [part, part], [], 0.01, "own",
    )(table, att, w, direct_right)

    own = swap(give_own)
    keep_below, keep_above, relayed, relay_left, relay_right = lax.optimization_barrier(
        (keep_below, keep_above, relayed, relay_left, relay_right))
    left_below = to_x(total_of(keep_below[:, :mid], relayed[:HALF], relay_left), 1)
    right_above = to_x(total_of(keep_above[:, mid:], relayed[HALF:], relay_right), -1)
    return pl.pallas_call(
        final_kernel,
        out_shape=jax.ShapeDtypeStruct((HALF, width), BF16),
        in_specs=[VMEM] * 6,
        out_specs=VMEM,
        compiler_params=pltpu.CompilerParams(vmem_limit_bytes=8 * 2 ** 20),
        name="final",
    )(keep_own, own, left_below, left_above, right_below, right_above)


def solution(mesh):
    return jax.shard_map(
        per_device,
        mesh=mesh,
        in_specs=(
            P("ctx", "head"),
            P("ctx", "head"),
            P("ctx", "head"),
            P("head"),
            P("head", None),
            P("head", None),
            P("head", None),
        ),
        out_specs=P(("ctx", "head"), None),
        check_vma=False,
    )
```

```python
import functools

import jax
import jax.numpy as jnp
from jax import lax
from jax.experimental import pallas as pl
from jax.experimental.pallas import tpu as pltpu
from jax.sharding import PartitionSpec as P

HEAD = 128
ROWS = 128
HALF = 64
SLOTS = 24
LISTED = 8
BANDS = 3
BLOCKS = 128
RUNS = 4
HEADS = 8
TOKENS = RUNS * ROWS
SCALE = HEAD ** -0.5
FACTOR = SCALE * 1.4426950408889634
NEVER = 1 << 20
LOW = -1e30
Z, Y, X = 8, 4, 4
BF16, F32 = jnp.bfloat16, jnp.float32
META = BLOCKS
VERT = META + 6
SLASH = VERT + HEADS * LISTED


def z_pairs(step):
    return [(Y * z + y, Y * ((z + step) % Z) + y) for z in range(Z) for y in range(Y)]


def y_pairs(flip):
    return [(Y * z + y, Y * z + (y ^ flip)) for z in range(Z) for y in range(Y)]


def x_pairs(step):
    return [(2 * x + k, 2 * ((x + step) % X) + k) for x in range(X) for k in range(2)]


CORE_PAIRS = [(h, h ^ 1) for h in range(HEADS)]


class Copies:
    def __init__(self, sems):
        self.sems, self.made = sems, []

    def start(self, src, dst):
        made = pltpu.make_async_copy(src, dst, self.sems.at[len(self.made)])
        made.start()
        self.made.append(made)

    def wait(self, count=None):
        for made in self.made[:count]:
            made.wait()
        self.made = [] if count is None else self.made[count:]


def key_places(table, late):
    z, y_half = table[META + 3], table[META + 4]
    n = lax.broadcasted_iota(jnp.int32, (1, HALF), 1)
    part, inner, row = n // 32, (n // 8) % 4, n % 8
    z_of = ((z ^ int(late)) + 2 * inner) % Z
    return (z_of * 2 + (y_half ^ part)) * 8 + row


def load_half(copies, odd, own, far, near, cross, kv):
    for kind, parts in ((odd, (own, far)), (1 - odd, (near, cross))):
        for p, part in enumerate(parts):
            copies.start(part, kv.at[kind, :, pl.ds(32 * p, 32)])


def ids_of(table, h):
    return [table[VERT + h * LISTED + e] for e in range(LISTED)]


def slots_of(table, h):
    return [table[jnp.maximum(i, 0)] for i in ids_of(table, h)]


def listed(kv, kind, slots):
    return jnp.concatenate([kv[kind, slot] for slot in slots], axis=0)


def limits(table, places, h):
    return jnp.concatenate([places + jnp.where(i >= 0, i * ROWS, NEVER) for i in ids_of(table, h)], axis=1)


def near_base(table, ids, run, offset):
    block = table[META + 2] + run - offset
    use = block >= 0
    for i in ids:
        use = jnp.logical_and(use, i != block)
    return jnp.where(use, block * ROWS, NEVER)


def product(q, keys):
    return lax.dot_general(q, keys, (((1,), (1,)), ((), ())), preferred_element_type=F32)


def wide(column):
    return jnp.broadcast_to(column, (column.shape[0], HEAD))


def across(column_block, count):
    return jnp.concatenate([column_block] * count, axis=1)


def fetch_kernel(q, kc, vc, spread, qs, own, sems):
    copies = Copies(sems)
    half = q.shape[0] // 2
    for n in range(2):
        copies.start(q.at[pl.ds(n * half, half)], qs.at[pl.ds(n * half, half)])
    for kind, cur in enumerate((kc, vc)):
        copies.start(cur, own.at[kind])
    copies.wait()


def band_kernel(table, sink, qs, prev, own, acc, tops, sums, band):
    for kind in range(2):
        for b in range(RUNS):
            rows = [prev[r, kind, b].astype(F32) for r in range(16)]
            band[kind, b] = jnp.concatenate(rows, axis=0).astype(BF16)
            band[kind, RUNS + b] = own[kind, b]
    token = TOKENS // RUNS * table[META + 2] + lax.broadcasted_iota(jnp.int32, (TOKENS, 1), 0)
    within = lax.broadcasted_iota(jnp.int32, (1, ROWS), 1)
    for h in range(HEADS):
        cols = slice(h * HEAD, (h + 1) * HEAD)
        raw_sink = sink[h:h + 1, :]
        ids = ids_of(table, h)
        offsets = [table[SLASH + h * BANDS + j] for j in range(BANDS)]
        score = []
        for run in range(RUNS):
            rows = slice(run * ROWS, (run + 1) * ROWS)
            keys = jnp.concatenate([band[0, RUNS + run - offset] for offset in offsets], axis=0)
            limit = jnp.concatenate(
                [within + near_base(table, ids, run, offset) for offset in offsets], axis=1)
            score.append(jnp.where(token[rows] >= limit, product(qs[rows, cols], keys), LOW))
        score = jnp.concatenate(score, axis=0)
        top = jnp.maximum(wide(jnp.max(score, axis=1, keepdims=True)), raw_sink)
        weight = jnp.exp2((score - across(top, BANDS)) * FACTOR)
        total = wide(jnp.sum(weight, axis=1, keepdims=True)) + jnp.exp2((raw_sink - top) * FACTOR)
        weight = weight.astype(BF16)
        for run in range(RUNS):
            rows = slice(run * ROWS, (run + 1) * ROWS)
            vals = jnp.concatenate([band[1, RUNS + run - offset] for offset in offsets], axis=0)
            acc[rows, cols] = jnp.dot(weight[rows], vals, preferred_element_type=F32)
        tops[:, cols] = top
        sums[:, cols] = total


def add_listed(table, qs, kv, late, acc, tops, sums, put):
    token = TOKENS // RUNS * table[META + 2] + lax.broadcasted_iota(jnp.int32, (TOKENS, 1), 0)
    places = key_places(table, late)
    for h in range(HEADS):
        cols = slice(h * HEAD, (h + 1) * HEAD)
        slots = slots_of(table, h)
        score = product(qs[:, cols], listed(kv, 0, slots))
        score = jnp.where(token >= limits(table, places, h), score, LOW)
        before = tops[:, cols]
        top = jnp.maximum(wide(jnp.max(score, axis=1, keepdims=True)), before)
        weight = jnp.exp2((score - across(top, LISTED * HALF // HEAD)) * FACTOR)
        fade = jnp.exp2((before - top) * FACTOR)
        total = wide(jnp.sum(weight, axis=1, keepdims=True)) + fade * sums[:, cols]
        mixed = jnp.dot(weight.astype(BF16), listed(kv, 1, slots), preferred_element_type=F32)
        put(cols, mixed + acc[:, cols] * fade, top, total)


def early_kernel(table, qs, w, a0, a2, a1, a3, acc, tops, sums, acc_out, tops_out, sums_out, w_out, kv, sems):
    copies = Copies(sems)
    load_half(copies, table[META], a0, a2, a1, a3, kv)
    first = len(copies.made)
    depth = w.shape[0] // 4
    for n in range(4):
        copies.start(w.at[pl.ds(n * depth, depth)], w_out.at[pl.ds(n * depth, depth)])
    copies.wait(first)

    def put(cols, mixed, top, total):
        acc_out[:, cols], tops_out[:, cols], sums_out[:, cols] = mixed, top, total

    add_listed(table, qs, kv, False, acc, tops, sums, put)
    copies.wait()


def project(att, w, blocks, core, keeps, give):
    def rows(block, side):
        start = pl.multiple_of(block * ROWS + side * HALF, HALF)
        return att[pl.ds(start, HALF), :]

    lhs = jnp.concatenate([rows(b, core) for b in blocks] + [rows(b, 1 - core) for b in blocks], axis=0)
    tile = 512
    for n in range(w.shape[1] // tile):
        cols = slice(n * tile, (n + 1) * tile)
        out = jnp.dot(lhs, w[:, cols], preferred_element_type=F32).astype(BF16)
        for i, keep in enumerate(keeps):
            keep[:, cols] = out[i * HALF:(i + 1) * HALF]
        give(n * tile, tile, out[len(blocks) * HALF:])


def late_kernel(table, qs, w, b0, b2, b1, b3, acc, tops, sums, att, keep, give, kv, sems):
    copies = Copies(sems)
    load_half(copies, table[META], b0, b2, b1, b3, kv)
    copies.wait()

    def put(cols, mixed, top, total):
        att[:, cols] = (mixed * (1.0 / total)).astype(BF16)

    add_listed(table, qs, kv, True, acc, tops, sums, put)
    project(att, w, [(table[META + 5] + 2) % X], table[META + 1], [keep], functools.partial(store, give))


def store(give, start, size, rows):
    give[:, start:start + size] = rows


def sides_kernel(table, att, w, keep_below, keep_above, direct, relayed):
    x, mid = table[META + 5], w.shape[1] // 2

    def give(start, size, rows):
        below, above = rows[:HALF], rows[HALF:]
        at = slice(start % mid, start % mid + size)
        if start < mid:
            relayed[:HALF, at], direct[HALF:, at] = below, above
        else:
            direct[:HALF, at], relayed[HALF:, at] = below, above

    project(att, w, [(x + 1) % X, (x + 3) % X], table[META + 1], [keep_below, keep_above], give)


def own_kernel(table, att, w, after, keep, give):
    project(att, w, [table[META + 5]], table[META + 1], [keep], functools.partial(store, give))


def final_kernel(keep, swapped, left_below, left_above, right_below, right_above, out):
    mid = out.shape[1] // 2
    for start, pair in ((0, (left_below, left_above)), (mid, (right_below, right_above))):
        cols = slice(start, start + mid)
        total = keep[:, cols].astype(F32) + swapped[:, cols].astype(F32)
        for part in pair:
            total = total + part[...].astype(F32)
        out[:, cols] = total.astype(BF16)


SMEM = pl.BlockSpec(memory_space=pltpu.SMEM)
VMEM = pl.BlockSpec(memory_space=pltpu.VMEM)
ANY = pl.BlockSpec(memory_space=pl.ANY)


def call(body, ins, outs, scratch, micros, name):
    return pl.pallas_call(
        body,
        out_shape=tuple(pltpu.VMEM(shape, dtype) for shape, dtype in outs),
        in_specs=ins,
        out_specs=(VMEM,) * len(outs),
        scratch_shapes=scratch,
        compiler_params=pltpu.CompilerParams(vmem_limit_bytes=24 * 2 ** 20),
        cost_estimate=pl.CostEstimate(flops=int(micros * 1e9), bytes_accessed=int(micros * 2 ** 20), transcendentals=0),
        name=name,
    )


def total_of(*terms):
    return functools.reduce(lambda a, b: a + b, [t.astype(F32) for t in terms]).astype(BF16)


def tables(c, x, core, vert_blocks, slash_offsets):
    block = jnp.arange(BLOCKS, dtype=jnp.int32)
    present = jnp.any(vert_blocks[:, :, None] == block, axis=(0, 1)).astype(jnp.int32)
    rank = jnp.sum(jnp.where(block[:, None] > block[None, :], present[None, :], 0), axis=1)
    meta = jnp.stack([c % 2, core, RUNS * c, c // Y, (c % Y) // 2, x]).astype(jnp.int32)
    table = jnp.concatenate([rank, meta, vert_blocks.reshape(-1), slash_offsets.reshape(-1)])
    return jnp.where(present > 0, rank, -1), table


def spread_kernel(keys, values, out, sems):
    copies = Copies(sems)
    for kind, a in enumerate((keys, values)):
        for b in range(RUNS):
            copies.start(a.at[b], out.at[:, kind, b])
    copies.wait()


def per_device(queries, keys, values, sink_logits, vert_blocks, slash_offsets, output_weight):
    c = lax.axis_index("ctx")
    h = lax.axis_index("head")
    x, core = h // 2, h % 2
    keys = keys.reshape(RUNS, ROWS, HEAD)
    values = values.reshape(RUNS, ROWS, HEAD)
    place, table = tables(c, x, core, vert_blocks, slash_offsets)
    sink = jnp.broadcast_to(sink_logits[:, None] * (1.0 / SCALE), (HEADS, HEAD))
    far_keys, far_values = [pltpu.with_memory_space_constraint(a.reshape(RUNS, 16, 8, HEAD), pltpu.HBM)
                            for a in (keys, values)]
    (spread,) = call(
        spread_kernel, [ANY, ANY], [((16, 2, RUNS, 8, HEAD), BF16)], [pltpu.SemaphoreType.DMA((2 * RUNS,))], 1, "spread",
    )(far_keys, far_values)
    spread = spread.reshape(Z * Y, RUNS * 8, HEAD)
    prev = lax.ppermute(spread, "ctx", [(s, s + 1) for s in range(Z * Y - 1)]).reshape(16, 2, RUNS, 8, HEAD)
    got = lax.all_to_all(spread, "ctx", 0, 0, tiled=True).reshape(BLOCKS * 8, HEAD)
    rows = ((TOKENS, HEADS * HEAD), BF16)
    q, own = call(
        fetch_kernel, [ANY] * 4, [rows, ((2, RUNS, ROWS, HEAD), BF16)], [pltpu.SemaphoreType.DMA((4,))], 1, "fetch",
    )(*[pltpu.with_memory_space_constraint(a, pltpu.HBM) for a in (queries, keys, values)], spread)
    place, table, sink, q, own = lax.optimization_barrier((place, table, sink, q, own))
    r = jnp.arange(SLOTS * 8, dtype=jnp.int32)[:, None]
    col = jnp.arange(BLOCKS * 8, dtype=jnp.int32)[None, :]
    pick = (jnp.repeat(place, 8)[None, :] == r // 8) & (col % 8 == r % 8)
    mine = jnp.dot(pick.astype(BF16), got, preferred_element_type=F32)
    mine = mine.astype(BF16).reshape(SLOTS, 8, HEAD)

    def from_z(a, offset):
        return lax.ppermute(a, "ctx", z_pairs(-offset))

    z2, z4, z6 = from_z(mine, 2), from_z(mine, 4), from_z(mine, 6)
    prev, z2, z4, z6 = lax.optimization_barrier((prev, z2, z4, z6))
    a0 = jnp.concatenate([mine, z2, z4, z6], axis=1)
    beside = [(Y * z + y, Y * (z ^ 1) + y) for z in range(Z) for y in range(Y)]
    b0 = lax.ppermute(a0, "ctx", beside)
    a1, a2, a3 = [lax.ppermute(a0, "ctx", y_pairs(f)) for f in (1, 2, 3)]

    width = output_weight.shape[1]
    kv = pltpu.VMEM((2, SLOTS, HALF, HEAD), BF16)
    part = ((HALF, width), BF16)
    state = [((TOKENS, HEADS * HEAD), F32)] * 3
    acc, tops, sums = call(
        band_kernel, [SMEM] + [VMEM] * 4, state, [pltpu.VMEM((2, 2 * RUNS, ROWS, HEAD), BF16)], 3, "band",
    )(table, sink, q, prev, own)
    b0, acc = lax.optimization_barrier((b0, acc))
    b1, b3 = [lax.ppermute(b0, "ctx", y_pairs(f)) for f in (1, 3)]
    b2 = lax.ppermute(a2, "ctx", beside)
    acc, tops, sums, w = call(
        early_kernel, [SMEM, VMEM] + [ANY] * 5 + [VMEM] * 3, state + [(output_weight.shape, BF16)],
        [kv, pltpu.SemaphoreType.DMA((8,))], 5, "early",
    )(table, q, pltpu.with_memory_space_constraint(output_weight, pltpu.HBM), a0, a2, a1, a3, acc, tops, sums)
    att, keep_far, give_far = call(
        late_kernel, [SMEM, VMEM, VMEM] + [ANY] * 4 + [VMEM] * 3,
        [rows, part, part], [kv, pltpu.SemaphoreType.DMA((4,))], 0.01, "late",
    )(table, q, w, b0, b2, b1, b3, acc, tops, sums)
    halves = ((2 * HALF, width // 2), BF16)
    keep_below, keep_above, give_direct, give_relayed = call(
        sides_kernel, [SMEM, VMEM, VMEM], [part, part, halves, halves], [], 0.01, "sides",
    )(table, att, w)
    def swap(a):
        return lax.ppermute(a, "head", CORE_PAIRS)

    def to_x(a, step):
        return lax.ppermute(a, "head", x_pairs(step))

    far, direct, relayed = swap(give_far), swap(give_direct), swap(give_relayed)
    mid = width // 2
    far_left = total_of(keep_far[:, :mid], far[:, :mid])
    far_right = total_of(keep_far[:, mid:], far[:, mid:])
    relay_left, relay_right = to_x(far_left, 1), to_x(far_right, -1)
    direct_right = total_of(keep_below[:, mid:], direct[:HALF])
    direct_left = total_of(keep_above[:, :mid], direct[HALF:])
    right_below, left_above = to_x(direct_right, 1), to_x(direct_left, -1)
    keep_own, give_own = call(
        own_kernel, [SMEM, VMEM, VMEM, ANY], [part, part], [], 0.01, "own",
    )(table, att, w, relayed)

    own = swap(give_own)
    keep_below, keep_above, relayed, relay_left, relay_right = lax.optimization_barrier(
        (keep_below, keep_above, relayed, relay_left, relay_right))
    left_below = to_x(total_of(keep_below[:, :mid], relayed[:HALF], relay_left), 1)
    right_above = to_x(total_of(keep_above[:, mid:], relayed[HALF:], relay_right), -1)
    return pl.pallas_call(
        final_kernel,
        out_shape=jax.ShapeDtypeStruct((HALF, width), BF16),
        in_specs=[VMEM] * 6,
        out_specs=VMEM,
        compiler_params=pltpu.CompilerParams(vmem_limit_bytes=8 * 2 ** 20),
        name="final",
    )(keep_own, own, left_below, left_above, right_below, right_above)


def solution(mesh):
    return jax.shard_map(
        per_device,
        mesh=mesh,
        in_specs=(
            P("ctx", "head"),
            P("ctx", "head"),
            P("ctx", "head"),
            P("head"),
            P("head", None),
            P("head", None),
            P("head", None),
        ),
        out_specs=P(("ctx", "head"), None),
        check_vma=False,
    )
```

```python
import functools

import jax
import jax.numpy as jnp
from jax import lax
from jax.experimental import pallas as pl
from jax.experimental.pallas import tpu as pltpu
from jax.sharding import PartitionSpec as P

HEAD = 128
ROWS = 128
HALF = 64
SLOTS = 24
LISTED = 8
BANDS = 3
BLOCKS = 128
RUNS = 4
HEADS = 8
TOKENS = RUNS * ROWS
SCALE = HEAD ** -0.5
FACTOR = SCALE * 1.4426950408889634
NEVER = 1 << 20
LOW = -1e30
Z, Y, X = 8, 4, 4
BF16, F32 = jnp.bfloat16, jnp.float32
META = BLOCKS
VERT = META + 6
SLASH = VERT + HEADS * LISTED


def z_pairs(step):
    return [(Y * z + y, Y * ((z + step) % Z) + y) for z in range(Z) for y in range(Y)]


def y_pairs(flip):
    return [(Y * z + y, Y * z + (y ^ flip)) for z in range(Z) for y in range(Y)]


def x_pairs(step):
    return [(2 * x + k, 2 * ((x + step) % X) + k) for x in range(X) for k in range(2)]


CORE_PAIRS = [(h, h ^ 1) for h in range(HEADS)]


class Copies:
    def __init__(self, sems):
        self.sems, self.made = sems, []

    def start(self, src, dst):
        made = pltpu.make_async_copy(src, dst, self.sems.at[len(self.made)])
        made.start()
        self.made.append(made)

    def wait(self, count=None):
        for made in self.made[:count]:
            made.wait()
        self.made = [] if count is None else self.made[count:]


def key_places(table, late):
    z, y_half = table[META + 3], table[META + 4]
    n = lax.broadcasted_iota(jnp.int32, (1, HALF), 1)
    part, inner, row = n // 32, (n // 8) % 4, n % 8
    z_of = ((z ^ int(late)) + 2 * inner) % Z
    return (z_of * 2 + (y_half ^ part)) * 8 + row


def load_half(copies, odd, own, far, near, cross, kv):
    for kind, parts in ((odd, (own, far)), (1 - odd, (near, cross))):
        for p, part in enumerate(parts):
            copies.start(part, kv.at[kind, :, pl.ds(32 * p, 32)])


def ids_of(table, h):
    return [table[VERT + h * LISTED + e] for e in range(LISTED)]


def slots_of(table, h):
    return [table[jnp.maximum(i, 0)] for i in ids_of(table, h)]


def listed(kv, kind, slots):
    return jnp.concatenate([kv[kind, slot] for slot in slots], axis=0)


def limits(table, places, h):
    return jnp.concatenate([places + jnp.where(i >= 0, i * ROWS, NEVER) for i in ids_of(table, h)], axis=1)


def near_base(table, ids, run, offset):
    block = table[META + 2] + run - offset
    use = block >= 0
    for i in ids:
        use = jnp.logical_and(use, i != block)
    return jnp.where(use, block * ROWS, NEVER)


def product(q, keys):
    return lax.dot_general(q, keys, (((1,), (1,)), ((), ())), preferred_element_type=F32)


def wide(column):
    return jnp.broadcast_to(column, (column.shape[0], HEAD))


def across(column_block, count):
    return jnp.concatenate([column_block] * count, axis=1)


def fetch_kernel(q, kc, vc, spread, qs, own, sems):
    copies = Copies(sems)
    half = q.shape[0] // 2
    for n in range(2):
        copies.start(q.at[pl.ds(n * half, half)], qs.at[pl.ds(n * half, half)])
    for kind, cur in enumerate((kc, vc)):
        copies.start(cur, own.at[kind])
    copies.wait()


def band_kernel(table, sink, qs, prev, own, acc, tops, sums, band):
    for kind in range(2):
        for b in range(RUNS):
            rows = [prev[r, kind, b].astype(F32) for r in range(16)]
            band[kind, b] = jnp.concatenate(rows, axis=0).astype(BF16)
            band[kind, RUNS + b] = own[kind, b]
    token = TOKENS // RUNS * table[META + 2] + lax.broadcasted_iota(jnp.int32, (TOKENS, 1), 0)
    within = lax.broadcasted_iota(jnp.int32, (1, ROWS), 1)
    for h in range(HEADS):
        cols = slice(h * HEAD, (h + 1) * HEAD)
        raw_sink = sink[h:h + 1, :]
        ids = ids_of(table, h)
        offsets = [table[SLASH + h * BANDS + j] for j in range(BANDS)]
        score = []
        for run in range(RUNS):
            rows = slice(run * ROWS, (run + 1) * ROWS)
            keys = jnp.concatenate([band[0, RUNS + run - offset] for offset in offsets], axis=0)
            limit = jnp.concatenate(
                [within + near_base(table, ids, run, offset) for offset in offsets], axis=1)
            score.append(jnp.where(token[rows] >= limit, product(qs[rows, cols], keys), LOW))
        score = jnp.concatenate(score, axis=0)
        top = jnp.maximum(wide(jnp.max(score, axis=1, keepdims=True)), raw_sink)
        weight = jnp.exp2((score - across(top, BANDS)) * FACTOR)
        total = wide(jnp.sum(weight, axis=1, keepdims=True)) + jnp.exp2((raw_sink - top) * FACTOR)
        weight = weight.astype(BF16)
        for run in range(RUNS):
            rows = slice(run * ROWS, (run + 1) * ROWS)
            vals = jnp.concatenate([band[1, RUNS + run - offset] for offset in offsets], axis=0)
            acc[rows, cols] = jnp.dot(weight[rows], vals, preferred_element_type=F32)
        tops[:, cols] = top
        sums[:, cols] = total


def add_listed(table, qs, kv, late, acc, tops, sums, put):
    token = TOKENS // RUNS * table[META + 2] + lax.broadcasted_iota(jnp.int32, (TOKENS, 1), 0)
    places = key_places(table, late)
    for h in range(HEADS):
        cols = slice(h * HEAD, (h + 1) * HEAD)
        slots = slots_of(table, h)
        score = product(qs[:, cols], listed(kv, 0, slots))
        score = jnp.where(token >= limits(table, places, h), score, LOW)
        before = tops[:, cols]
        top = jnp.maximum(wide(jnp.max(score, axis=1, keepdims=True)), before)
        weight = jnp.exp2((score - across(top, LISTED * HALF // HEAD)) * FACTOR)
        fade = jnp.exp2((before - top) * FACTOR)
        total = wide(jnp.sum(weight, axis=1, keepdims=True)) + fade * sums[:, cols]
        mixed = jnp.dot(weight.astype(BF16), listed(kv, 1, slots), preferred_element_type=F32)
        put(cols, mixed + acc[:, cols] * fade, top, total)


def early_kernel(table, qs, w, a0, a2, a1, a3, acc, tops, sums, acc_out, tops_out, sums_out, w_out, kv, sems):
    copies = Copies(sems)
    load_half(copies, table[META], a0, a2, a1, a3, kv)
    first = len(copies.made)
    depth = w.shape[0] // 4
    for n in range(4):
        copies.start(w.at[pl.ds(n * depth, depth)], w_out.at[pl.ds(n * depth, depth)])
    copies.wait(first)

    def put(cols, mixed, top, total):
        acc_out[:, cols], tops_out[:, cols], sums_out[:, cols] = mixed, top, total

    add_listed(table, qs, kv, False, acc, tops, sums, put)
    copies.wait()


def project(att, w, blocks, core, keeps, give):
    def rows(block, side):
        start = pl.multiple_of(block * ROWS + side * HALF, HALF)
        return att[pl.ds(start, HALF), :]

    lhs = jnp.concatenate([rows(b, core) for b in blocks] + [rows(b, 1 - core) for b in blocks], axis=0)
    tile = 512
    for n in range(w.shape[1] // tile):
        cols = slice(n * tile, (n + 1) * tile)
        out = jnp.dot(lhs, w[:, cols], preferred_element_type=F32).astype(BF16)
        for i, keep in enumerate(keeps):
            keep[:, cols] = out[i * HALF:(i + 1) * HALF]
        give(n * tile, tile, out[len(blocks) * HALF:])


def late_kernel(table, qs, w, b0, b2, b1, b3, acc, tops, sums, att, keep, give, kv, sems):
    copies = Copies(sems)
    load_half(copies, table[META], b0, b2, b1, b3, kv)
    copies.wait()

    def put(cols, mixed, top, total):
        att[:, cols] = (mixed * (1.0 / total)).astype(BF16)

    add_listed(table, qs, kv, True, acc, tops, sums, put)
    project(att, w, [(table[META + 5] + 2) % X], table[META + 1], [keep], functools.partial(store, give))


def store(give, start, size, rows):
    give[:, start:start + size] = rows


def sides_kernel(table, att, w, keep_below, keep_above, direct, relayed):
    x, mid = table[META + 5], w.shape[1] // 2

    def give(start, size, rows):
        below, above = rows[:HALF], rows[HALF:]
        at = slice(start % mid, start % mid + size)
        if start < mid:
            relayed[:HALF, at], direct[HALF:, at] = below, above
        else:
            direct[:HALF, at], relayed[HALF:, at] = below, above

    project(att, w, [(x + 1) % X, (x + 3) % X], table[META + 1], [keep_below, keep_above], give)


def own_kernel(table, att, w, after, keep, give):
    project(att, w, [table[META + 5]], table[META + 1], [keep], functools.partial(store, give))


def final_kernel(keep, swapped, left_below, left_above, right_below, right_above, out):
    mid = out.shape[1] // 2
    for start, pair in ((0, (left_below, left_above)), (mid, (right_below, right_above))):
        cols = slice(start, start + mid)
        total = keep[:, cols].astype(F32) + swapped[:, cols].astype(F32)
        for part in pair:
            total = total + part[...].astype(F32)
        out[:, cols] = total.astype(BF16)


SMEM = pl.BlockSpec(memory_space=pltpu.SMEM)
VMEM = pl.BlockSpec(memory_space=pltpu.VMEM)
ANY = pl.BlockSpec(memory_space=pl.ANY)


def call(body, ins, outs, scratch, micros, name):
    return pl.pallas_call(
        body,
        out_shape=tuple(pltpu.VMEM(shape, dtype) for shape, dtype in outs),
        in_specs=ins,
        out_specs=(VMEM,) * len(outs),
        scratch_shapes=scratch,
        compiler_params=pltpu.CompilerParams(vmem_limit_bytes=24 * 2 ** 20),
        cost_estimate=pl.CostEstimate(flops=int(micros * 1e9), bytes_accessed=int(micros * 2 ** 20), transcendentals=0),
        name=name,
    )


def total_of(*terms):
    return functools.reduce(lambda a, b: a + b, [t.astype(F32) for t in terms]).astype(BF16)


def tables(c, x, core, vert_blocks, slash_offsets):
    block = jnp.arange(BLOCKS, dtype=jnp.int32)
    present = jnp.any(vert_blocks[:, :, None] == block, axis=(0, 1)).astype(jnp.int32)
    rank = jnp.sum(jnp.where(block[:, None] > block[None, :], present[None, :], 0), axis=1)
    meta = jnp.stack([c % 2, core, RUNS * c, c // Y, (c % Y) // 2, x]).astype(jnp.int32)
    table = jnp.concatenate([rank, meta, vert_blocks.reshape(-1), slash_offsets.reshape(-1)])
    return jnp.where(present > 0, rank, -1), table


def spread_kernel(keys, values, out, sems):
    copies = Copies(sems)
    for kind, a in enumerate((keys, values)):
        for b in range(RUNS):
            copies.start(a.at[b], out.at[:, kind, b])
    copies.wait()


def per_device(queries, keys, values, sink_logits, vert_blocks, slash_offsets, output_weight):
    c = lax.axis_index("ctx")
    h = lax.axis_index("head")
    x, core = h // 2, h % 2
    keys = keys.reshape(RUNS, ROWS, HEAD)
    values = values.reshape(RUNS, ROWS, HEAD)
    place, table = tables(c, x, core, vert_blocks, slash_offsets)
    sink = jnp.broadcast_to(sink_logits[:, None] * (1.0 / SCALE), (HEADS, HEAD))
    far_keys, far_values = [pltpu.with_memory_space_constraint(a.reshape(RUNS, 16, 8, HEAD), pltpu.HBM)
                            for a in (keys, values)]
    (spread,) = call(
        spread_kernel, [ANY, ANY], [((16, 2, RUNS, 8, HEAD), BF16)], [pltpu.SemaphoreType.DMA((2 * RUNS,))], 1, "spread",
    )(far_keys, far_values)
    spread = spread.reshape(Z * Y, RUNS * 8, HEAD)
    prev = lax.ppermute(spread, "ctx", [(s, s + 1) for s in range(Z * Y - 1)]).reshape(16, 2, RUNS, 8, HEAD)
    got = lax.all_to_all(spread, "ctx", 0, 0, tiled=True).reshape(BLOCKS * 8, HEAD)
    rows = ((TOKENS, HEADS * HEAD), BF16)
    q, own = call(
        fetch_kernel, [ANY] * 4, [rows, ((2, RUNS, ROWS, HEAD), BF16)], [pltpu.SemaphoreType.DMA((4,))], 1, "fetch",
    )(*[pltpu.with_memory_space_constraint(a, pltpu.HBM) for a in (queries, keys, values)], spread)
    place, table, sink, q, own = lax.optimization_barrier((place, table, sink, q, own))
    r = jnp.arange(SLOTS * 8, dtype=jnp.int32)[:, None]
    col = jnp.arange(BLOCKS * 8, dtype=jnp.int32)[None, :]
    pick = (jnp.repeat(place, 8)[None, :] == r // 8) & (col % 8 == r % 8)
    mine = jnp.dot(pick.astype(BF16), got, preferred_element_type=F32)
    mine = mine.astype(BF16).reshape(SLOTS, 8, HEAD)

    def from_z(a, offset):
        return lax.ppermute(a, "ctx", z_pairs(-offset))

    z2, z4, z6 = from_z(mine, 2), from_z(mine, 4), from_z(mine, 6)
    state = [((TOKENS, HEADS * HEAD), F32)] * 3
    acc, tops, sums = call(
        band_kernel, [SMEM] + [VMEM] * 4, state, [pltpu.VMEM((2, 2 * RUNS, ROWS, HEAD), BF16)], 3, "band",
    )(table, sink, q, prev, own)
    z2, z4, z6, acc = lax.optimization_barrier((z2, z4, z6, acc))
    a0 = jnp.concatenate([mine, z2, z4, z6], axis=1)
    beside = [(Y * z + y, Y * (z ^ 1) + y) for z in range(Z) for y in range(Y)]
    b0 = lax.ppermute(a0, "ctx", beside)
    a1, a2, a3 = [lax.ppermute(a0, "ctx", y_pairs(f)) for f in (1, 2, 3)]

    width = output_weight.shape[1]
    kv = pltpu.VMEM((2, SLOTS, HALF, HEAD), BF16)
    part = ((HALF, width), BF16)
    b1, b3 = [lax.ppermute(b0, "ctx", y_pairs(f)) for f in (1, 3)]
    b2 = lax.ppermute(a2, "ctx", beside)
    acc, tops, sums, w = call(
        early_kernel, [SMEM, VMEM] + [ANY] * 5 + [VMEM] * 3, state + [(output_weight.shape, BF16)],
        [kv, pltpu.SemaphoreType.DMA((8,))], 5, "early",
    )(table, q, pltpu.with_memory_space_constraint(output_weight, pltpu.HBM), a0, a2, a1, a3, acc, tops, sums)
    att, keep_far, give_far = call(
        late_kernel, [SMEM, VMEM, VMEM] + [ANY] * 4 + [VMEM] * 3,
        [rows, part, part], [kv, pltpu.SemaphoreType.DMA((4,))], 0.01, "late",
    )(table, q, w, b0, b2, b1, b3, acc, tops, sums)
    halves = ((2 * HALF, width // 2), BF16)
    keep_below, keep_above, give_direct, give_relayed = call(
        sides_kernel, [SMEM, VMEM, VMEM], [part, part, halves, halves], [], 0.01, "sides",
    )(table, att, w)
    def swap(a):
        return lax.ppermute(a, "head", CORE_PAIRS)

    def to_x(a, step):
        return lax.ppermute(a, "head", x_pairs(step))

    far, direct, relayed = swap(give_far), swap(give_direct), swap(give_relayed)
    mid = width // 2
    far_left = total_of(keep_far[:, :mid], far[:, :mid])
    far_right = total_of(keep_far[:, mid:], far[:, mid:])
    relay_left, relay_right = to_x(far_left, 1), to_x(far_right, -1)
    direct_right = total_of(keep_below[:, mid:], direct[:HALF])
    direct_left = total_of(keep_above[:, :mid], direct[HALF:])
    right_below, left_above = to_x(direct_right, 1), to_x(direct_left, -1)
    keep_own, give_own = call(
        own_kernel, [SMEM, VMEM, VMEM, ANY], [part, part], [], 0.01, "own",
    )(table, att, w, relayed)

    own = swap(give_own)
    keep_below, keep_above, relayed, relay_left, relay_right = lax.optimization_barrier(
        (keep_below, keep_above, relayed, relay_left, relay_right))
    left_below = to_x(total_of(keep_below[:, :mid], relayed[:HALF], relay_left), 1)
    right_above = to_x(total_of(keep_above[:, mid:], relayed[HALF:], relay_right), -1)
    return pl.pallas_call(
        final_kernel,
        out_shape=jax.ShapeDtypeStruct((HALF, width), BF16),
        in_specs=[VMEM] * 6,
        out_specs=VMEM,
        compiler_params=pltpu.CompilerParams(vmem_limit_bytes=8 * 2 ** 20),
        name="final",
    )(keep_own, own, left_below, left_above, right_below, right_above)


def solution(mesh):
    return jax.shard_map(
        per_device,
        mesh=mesh,
        in_specs=(
            P("ctx", "head"),
            P("ctx", "head"),
            P("ctx", "head"),
            P("head"),
            P("head", None),
            P("head", None),
            P("head", None),
        ),
        out_specs=P(("ctx", "head"), None),
        check_vma=False,
    )
```

```python
import functools

import jax
import jax.numpy as jnp
from jax import lax
from jax.experimental import pallas as pl
from jax.experimental.pallas import tpu as pltpu
from jax.sharding import PartitionSpec as P

HEAD = 128
ROWS = 128
HALF = 64
SLOTS = 24
LISTED = 8
BANDS = 3
BLOCKS = 128
RUNS = 4
HEADS = 8
TOKENS = RUNS * ROWS
SCALE = HEAD ** -0.5
FACTOR = SCALE * 1.4426950408889634
NEVER = 1 << 20
LOW = -1e30
Z, Y, X = 8, 4, 4
BF16, F32 = jnp.bfloat16, jnp.float32
META = BLOCKS
VERT = META + 6
SLASH = VERT + HEADS * LISTED


def z_pairs(step):
    return [(Y * z + y, Y * ((z + step) % Z) + y) for z in range(Z) for y in range(Y)]


def y_pairs(flip):
    return [(Y * z + y, Y * z + (y ^ flip)) for z in range(Z) for y in range(Y)]


def x_pairs(step):
    return [(2 * x + k, 2 * ((x + step * (1 - 2 * k)) % X) + k) for x in range(X) for k in range(2)]


CORE_PAIRS = [(h, h ^ 1) for h in range(HEADS)]


class Copies:
    def __init__(self, sems):
        self.sems, self.made = sems, []

    def start(self, src, dst):
        made = pltpu.make_async_copy(src, dst, self.sems.at[len(self.made)])
        made.start()
        self.made.append(made)

    def wait(self, count=None):
        for made in self.made[:count]:
            made.wait()
        self.made = [] if count is None else self.made[count:]


def key_places(table, late):
    z, y_half = table[META + 3], table[META + 4]
    n = lax.broadcasted_iota(jnp.int32, (1, HALF), 1)
    part, inner, row = n // 32, (n // 8) % 4, n % 8
    z_of = ((z ^ int(late)) + 2 * inner) % Z
    return (z_of * 2 + (y_half ^ part)) * 8 + row


def load_half(copies, odd, own, far, near, cross, kv):
    for kind, parts in ((odd, (own, far)), (1 - odd, (near, cross))):
        for p, part in enumerate(parts):
            copies.start(part, kv.at[kind, :, pl.ds(32 * p, 32)])


def ids_of(table, h):
    return [table[VERT + h * LISTED + e] for e in range(LISTED)]


def slots_of(table, h):
    return [table[jnp.maximum(i, 0)] for i in ids_of(table, h)]


def listed(kv, kind, slots):
    return jnp.concatenate([kv[kind, slot] for slot in slots], axis=0)


def limits(table, places, h):
    return jnp.concatenate([places + jnp.where(i >= 0, i * ROWS, NEVER) for i in ids_of(table, h)], axis=1)


def near_base(table, ids, run, offset):
    block = table[META + 2] + run - offset
    use = block >= 0
    for i in ids:
        use = jnp.logical_and(use, i != block)
    return jnp.where(use, block * ROWS, NEVER)


def product(q, keys):
    return lax.dot_general(q, keys, (((1,), (1,)), ((), ())), preferred_element_type=F32)


def wide(column):
    return jnp.broadcast_to(column, (column.shape[0], HEAD))


def across(column_block, count):
    return jnp.concatenate([column_block] * count, axis=1)


def fetch_kernel(q, kc, vc, spread, qs, own, sems):
    copies = Copies(sems)
    half = q.shape[0] // 2
    for n in range(2):
        copies.start(q.at[pl.ds(n * half, half)], qs.at[pl.ds(n * half, half)])
    for kind, cur in enumerate((kc, vc)):
        copies.start(cur, own.at[kind])
    copies.wait()


def band_kernel(table, sink, qs, prev, own, acc, tops, sums, band):
    for kind in range(2):
        for b in range(RUNS):
            rows = [prev[r, kind, b].astype(F32) for r in range(16)]
            band[kind, b] = jnp.concatenate(rows, axis=0).astype(BF16)
            band[kind, RUNS + b] = own[kind, b]
    token = TOKENS // RUNS * table[META + 2] + lax.broadcasted_iota(jnp.int32, (TOKENS, 1), 0)
    within = lax.broadcasted_iota(jnp.int32, (1, ROWS), 1)
    for h in range(HEADS):
        cols = slice(h * HEAD, (h + 1) * HEAD)
        raw_sink = sink[h:h + 1, :]
        ids = ids_of(table, h)
        offsets = [table[SLASH + h * BANDS + j] for j in range(BANDS)]
        score = []
        for run in range(RUNS):
            rows = slice(run * ROWS, (run + 1) * ROWS)
            keys = jnp.concatenate([band[0, RUNS + run - offset] for offset in offsets], axis=0)
            limit = jnp.concatenate(
                [within + near_base(table, ids, run, offset) for offset in offsets], axis=1)
            score.append(jnp.where(token[rows] >= limit, product(qs[rows, cols], keys), LOW))
        score = jnp.concatenate(score, axis=0)
        top = jnp.maximum(wide(jnp.max(score, axis=1, keepdims=True)), raw_sink)
        weight = jnp.exp2((score - across(top, BANDS)) * FACTOR)
        total = wide(jnp.sum(weight, axis=1, keepdims=True)) + jnp.exp2((raw_sink - top) * FACTOR)
        weight = weight.astype(BF16)
        for run in range(RUNS):
            rows = slice(run * ROWS, (run + 1) * ROWS)
            vals = jnp.concatenate([band[1, RUNS + run - offset] for offset in offsets], axis=0)
            acc[rows, cols] = jnp.dot(weight[rows], vals, preferred_element_type=F32)
        tops[:, cols] = top
        sums[:, cols] = total


def add_listed(table, qs, kv, late, acc, tops, sums, put):
    token = TOKENS // RUNS * table[META + 2] + lax.broadcasted_iota(jnp.int32, (TOKENS, 1), 0)
    places = key_places(table, late)
    for h in range(HEADS):
        cols = slice(h * HEAD, (h + 1) * HEAD)
        slots = slots_of(table, h)
        score = product(qs[:, cols], listed(kv, 0, slots))
        score = jnp.where(token >= limits(table, places, h), score, LOW)
        before = tops[:, cols]
        top = jnp.maximum(wide(jnp.max(score, axis=1, keepdims=True)), before)
        weight = jnp.exp2((score - across(top, LISTED * HALF // HEAD)) * FACTOR)
        fade = jnp.exp2((before - top) * FACTOR)
        total = wide(jnp.sum(weight, axis=1, keepdims=True)) + fade * sums[:, cols]
        mixed = jnp.dot(weight.astype(BF16), listed(kv, 1, slots), preferred_element_type=F32)
        put(cols, mixed + acc[:, cols] * fade, top, total)


def early_kernel(table, qs, w, a0, a2, a1, a3, acc, tops, sums, acc_out, tops_out, sums_out, w_out, kv, sems):
    copies = Copies(sems)
    load_half(copies, table[META], a0, a2, a1, a3, kv)
    first = len(copies.made)
    depth = w.shape[0] // 4
    for n in range(4):
        copies.start(w.at[pl.ds(n * depth, depth)], w_out.at[pl.ds(n * depth, depth)])
    copies.wait(first)

    def put(cols, mixed, top, total):
        acc_out[:, cols], tops_out[:, cols], sums_out[:, cols] = mixed, top, total

    add_listed(table, qs, kv, False, acc, tops, sums, put)
    copies.wait()


def project(att, w, blocks, core, keeps, give):
    def rows(block, side):
        start = pl.multiple_of(block * ROWS + side * HALF, HALF)
        return att[pl.ds(start, HALF), :]

    lhs = jnp.concatenate([rows(b, core) for b in blocks] + [rows(b, 1 - core) for b in blocks], axis=0)
    tile = 512
    for n in range(w.shape[1] // tile):
        cols = slice(n * tile, (n + 1) * tile)
        out = jnp.dot(lhs, w[:, cols], preferred_element_type=F32).astype(BF16)
        for i, keep in enumerate(keeps):
            keep[:, cols] = out[i * HALF:(i + 1) * HALF]
        give(n * tile, tile, out[len(blocks) * HALF:])


def late_kernel(table, qs, w, b0, b2, b1, b3, acc, tops, sums, att, keep, give, kv, sems):
    copies = Copies(sems)
    load_half(copies, table[META], b0, b2, b1, b3, kv)
    copies.wait()

    def put(cols, mixed, top, total):
        att[:, cols] = (mixed * (1.0 / total)).astype(BF16)

    add_listed(table, qs, kv, True, acc, tops, sums, put)
    project(att, w, [(table[META + 5] + 2) % X], table[META + 1], [keep], functools.partial(store, give))


def store(give, start, size, rows):
    give[:, start:start + size] = rows


def sides_kernel(table, att, w, keep_next, keep_prev, direct, relayed):
    x, step = table[META + 5], 1 - 2 * table[META + 1]

    def give(start, size, rows):
        direct[:, start:start + size] = rows[:HALF]
        relayed[:, start:start + size] = rows[HALF:]

    project(att, w, [(x + step + X) % X, (x - step + X) % X], table[META + 1], [keep_next, keep_prev], give)


def own_kernel(table, att, w, after, keep, give):
    project(att, w, [table[META + 5]], table[META + 1], [keep], functools.partial(store, give))


def final_kernel(keep, swapped, direct, last, out):
    total = keep[...].astype(F32) + swapped[...].astype(F32)
    out[...] = (total + direct[...].astype(F32) + last[...].astype(F32)).astype(BF16)


SMEM = pl.BlockSpec(memory_space=pltpu.SMEM)
VMEM = pl.BlockSpec(memory_space=pltpu.VMEM)
ANY = pl.BlockSpec(memory_space=pl.ANY)


def call(body, ins, outs, scratch, micros, name):
    return pl.pallas_call(
        body,
        out_shape=tuple(pltpu.VMEM(shape, dtype) for shape, dtype in outs),
        in_specs=ins,
        out_specs=(VMEM,) * len(outs),
        scratch_shapes=scratch,
        compiler_params=pltpu.CompilerParams(vmem_limit_bytes=24 * 2 ** 20),
        cost_estimate=pl.CostEstimate(flops=int(micros * 1e9), bytes_accessed=int(micros * 2 ** 20), transcendentals=0),
        name=name,
    )


def total_of(*terms):
    return functools.reduce(lambda a, b: a + b, [t.astype(F32) for t in terms]).astype(BF16)


def tables(c, x, core, vert_blocks, slash_offsets):
    block = jnp.arange(BLOCKS, dtype=jnp.int32)
    present = jnp.any(vert_blocks[:, :, None] == block, axis=(0, 1)).astype(jnp.int32)
    rank = jnp.sum(jnp.where(block[:, None] > block[None, :], present[None, :], 0), axis=1)
    meta = jnp.stack([c % 2, core, RUNS * c, c // Y, (c % Y) // 2, x]).astype(jnp.int32)
    table = jnp.concatenate([rank, meta, vert_blocks.reshape(-1), slash_offsets.reshape(-1)])
    return jnp.where(present > 0, rank, -1), table


def spread_kernel(keys, values, out, sems):
    copies = Copies(sems)
    for kind, a in enumerate((keys, values)):
        for b in range(RUNS):
            copies.start(a.at[b], out.at[:, kind, b])
    copies.wait()


def per_device(queries, keys, values, sink_logits, vert_blocks, slash_offsets, output_weight):
    c = lax.axis_index("ctx")
    h = lax.axis_index("head")
    x, core = h // 2, h % 2
    keys = keys.reshape(RUNS, ROWS, HEAD)
    values = values.reshape(RUNS, ROWS, HEAD)
    place, table = tables(c, x, core, vert_blocks, slash_offsets)
    sink = jnp.broadcast_to(sink_logits[:, None] * (1.0 / SCALE), (HEADS, HEAD))
    far_keys, far_values = [pltpu.with_memory_space_constraint(a.reshape(RUNS, 16, 8, HEAD), pltpu.HBM)
                            for a in (keys, values)]
    (spread,) = call(
        spread_kernel, [ANY, ANY], [((16, 2, RUNS, 8, HEAD), BF16)], [pltpu.SemaphoreType.DMA((2 * RUNS,))], 1, "spread",
    )(far_keys, far_values)
    spread = spread.reshape(Z * Y, RUNS * 8, HEAD)
    prev = lax.ppermute(spread, "ctx", [(s, s + 1) for s in range(Z * Y - 1)]).reshape(16, 2, RUNS, 8, HEAD)
    got = lax.all_to_all(spread, "ctx", 0, 0, tiled=True).reshape(BLOCKS * 8, HEAD)
    rows = ((TOKENS, HEADS * HEAD), BF16)
    q, own = call(
        fetch_kernel, [ANY] * 4, [rows, ((2, RUNS, ROWS, HEAD), BF16)], [pltpu.SemaphoreType.DMA((4,))], 1, "fetch",
    )(*[pltpu.with_memory_space_constraint(a, pltpu.HBM) for a in (queries, keys, values)], spread)
    place, table, sink, q, own = lax.optimization_barrier((place, table, sink, q, own))
    r = jnp.arange(SLOTS * 8, dtype=jnp.int32)[:, None]
    col = jnp.arange(BLOCKS * 8, dtype=jnp.int32)[None, :]
    pick = (jnp.repeat(place, 8)[None, :] == r // 8) & (col % 8 == r % 8)
    mine = jnp.dot(pick.astype(BF16), got, preferred_element_type=F32)
    mine = mine.astype(BF16).reshape(SLOTS, 8, HEAD)

    def from_z(a, offset):
        return lax.ppermute(a, "ctx", z_pairs(-offset))

    z2, z4, z6 = from_z(mine, 2), from_z(mine, 4), from_z(mine, 6)
    prev, z2, z4, z6 = lax.optimization_barrier((prev, z2, z4, z6))
    a0 = jnp.concatenate([mine, z2, z4, z6], axis=1)
    beside = [(Y * z + y, Y * (z ^ 1) + y) for z in range(Z) for y in range(Y)]
    b0 = lax.ppermute(a0, "ctx", beside)
    a1, a2, a3 = [lax.ppermute(a0, "ctx", y_pairs(f)) for f in (1, 2, 3)]

    width = output_weight.shape[1]
    kv = pltpu.VMEM((2, SLOTS, HALF, HEAD), BF16)
    part = ((HALF, width), BF16)
    state = [((TOKENS, HEADS * HEAD), F32)] * 3
    acc, tops, sums = call(
        band_kernel, [SMEM] + [VMEM] * 4, state, [pltpu.VMEM((2, 2 * RUNS, ROWS, HEAD), BF16)], 3, "band",
    )(table, sink, q, prev, own)
    b0, acc = lax.optimization_barrier((b0, acc))
    b1, b3 = [lax.ppermute(b0, "ctx", y_pairs(f)) for f in (1, 3)]
    b2 = lax.ppermute(a2, "ctx", beside)
    acc, tops, sums, w = call(
        early_kernel, [SMEM, VMEM] + [ANY] * 5 + [VMEM] * 3, state + [(output_weight.shape, BF16)],
        [kv, pltpu.SemaphoreType.DMA((8,))], 5, "early",
    )(table, q, pltpu.with_memory_space_constraint(output_weight, pltpu.HBM), a0, a2, a1, a3, acc, tops, sums)
    att, keep_far, give_far = call(
        late_kernel, [SMEM, VMEM, VMEM] + [ANY] * 4 + [VMEM] * 3,
        [rows, part, part], [kv, pltpu.SemaphoreType.DMA((4,))], 0.01, "late",
    )(table, q, w, b0, b2, b1, b3, acc, tops, sums)
    keep_next, keep_prev, give_direct, give_relayed = call(
        sides_kernel, [SMEM, VMEM, VMEM], [part] * 4, [], 0.01, "sides",
    )(table, att, w)

    def swap(a):
        return lax.ppermute(a, "head", CORE_PAIRS)

    def to_x(a, step):
        return lax.ppermute(a, "head", x_pairs(step))

    far, direct, relayed = swap(give_far), swap(give_direct), swap(give_relayed)
    relay = to_x(total_of(keep_far, far), 1)
    from_direct = to_x(total_of(keep_prev, direct), -1)
    keep_own, give_own = call(
        own_kernel, [SMEM, VMEM, VMEM, ANY], [part, part], [], 0.01, "own",
    )(table, att, w, relayed)

    own = swap(give_own)
    keep_next, relayed, relay = lax.optimization_barrier((keep_next, relayed, relay))
    from_last = to_x(total_of(keep_next, relayed, relay), 1)
    return pl.pallas_call(
        final_kernel,
        out_shape=jax.ShapeDtypeStruct((HALF, width), BF16),
        in_specs=[VMEM] * 4,
        out_specs=VMEM,
        compiler_params=pltpu.CompilerParams(vmem_limit_bytes=8 * 2 ** 20),
        name="final",
    )(keep_own, own, from_direct, from_last)


def solution(mesh):
    return jax.shard_map(
        per_device,
        mesh=mesh,
        in_specs=(
            P("ctx", "head"),
            P("ctx", "head"),
            P("ctx", "head"),
            P("head"),
            P("head", None),
            P("head", None),
            P("head", None),
        ),
        out_specs=P(("ctx", "head"), None),
        check_vma=False,
    )
```

```python
import functools

import jax
import jax.numpy as jnp
from jax import lax
from jax.experimental import pallas as pl
from jax.experimental.pallas import tpu as pltpu
from jax.sharding import PartitionSpec as P

HEAD = 128
ROWS = 128
HALF = 64
SLOTS = 24
LISTED = 8
BANDS = 3
BLOCKS = 128
RUNS = 4
HEADS = 8
TOKENS = RUNS * ROWS
SCALE = HEAD ** -0.5
FACTOR = SCALE * 1.4426950408889634
NEVER = 1 << 20
LOW = -1e30
Z, Y, X = 8, 4, 4
BF16, F32 = jnp.bfloat16, jnp.float32
META = BLOCKS
VERT = META + 6
SLASH = VERT + HEADS * LISTED


def z_pairs(step):
    return [(Y * z + y, Y * ((z + step) % Z) + y) for z in range(Z) for y in range(Y)]


def y_pairs(flip):
    return [(Y * z + y, Y * z + (y ^ flip)) for z in range(Z) for y in range(Y)]


def x_pairs(step):
    return [(2 * x + k, 2 * ((x + step) % X) + k) for x in range(X) for k in range(2)]


CORE_PAIRS = [(h, h ^ 1) for h in range(HEADS)]


class Copies:
    def __init__(self, sems):
        self.sems, self.made = sems, []

    def start(self, src, dst):
        made = pltpu.make_async_copy(src, dst, self.sems.at[len(self.made)])
        made.start()
        self.made.append(made)

    def wait(self, count=None):
        for made in self.made[:count]:
            made.wait()
        self.made = [] if count is None else self.made[count:]


def key_places(table, late):
    z, y_half = table[META + 3], table[META + 4]
    n = lax.broadcasted_iota(jnp.int32, (1, HALF), 1)
    part, inner, row = n // 32, (n // 8) % 4, n % 8
    z_of = ((z ^ int(late)) + 2 * inner) % Z
    return (z_of * 2 + (y_half ^ part)) * 8 + row


def load_half(copies, odd, own, far, near, cross, kv):
    for kind, parts in ((odd, (own, far)), (1 - odd, (near, cross))):
        for p, part in enumerate(parts):
            copies.start(part, kv.at[kind, :, pl.ds(32 * p, 32)])


def ids_of(table, h):
    return [table[VERT + h * LISTED + e] for e in range(LISTED)]


def slots_of(table, h):
    return [table[jnp.maximum(i, 0)] for i in ids_of(table, h)]


def listed(kv, kind, slots):
    return jnp.concatenate([kv[kind, slot] for slot in slots], axis=0)


def limits(table, places, h):
    return jnp.concatenate([places + jnp.where(i >= 0, i * ROWS, NEVER) for i in ids_of(table, h)], axis=1)


def near_base(table, ids, run, offset):
    block = table[META + 2] + run - offset
    use = block >= 0
    for i in ids:
        use = jnp.logical_and(use, i != block)
    return jnp.where(use, block * ROWS, NEVER)


def product(q, keys):
    return lax.dot_general(q, keys, (((1,), (1,)), ((), ())), preferred_element_type=F32)


def wide(column):
    return jnp.broadcast_to(column, (column.shape[0], HEAD))


def across(column_block, count):
    return jnp.concatenate([column_block] * count, axis=1)


def fetch_kernel(q, kc, vc, spread, qs, own, sems):
    copies = Copies(sems)
    half = q.shape[0] // 2
    for n in range(2):
        copies.start(q.at[pl.ds(n * half, half)], qs.at[pl.ds(n * half, half)])
    for kind, cur in enumerate((kc, vc)):
        copies.start(cur, own.at[kind])
    copies.wait()


def band_kernel(table, sink, qs, prev, own, acc, tops, sums, band):
    for kind in range(2):
        for b in range(RUNS):
            rows = [prev[r, kind, b].astype(F32) for r in range(16)]
            band[kind, b] = jnp.concatenate(rows, axis=0).astype(BF16)
            band[kind, RUNS + b] = own[kind, b]
    token = TOKENS // RUNS * table[META + 2] + lax.broadcasted_iota(jnp.int32, (TOKENS, 1), 0)
    within = lax.broadcasted_iota(jnp.int32, (1, ROWS), 1)
    for h in range(HEADS):
        cols = slice(h * HEAD, (h + 1) * HEAD)
        raw_sink = sink[h:h + 1, :]
        ids = ids_of(table, h)
        offsets = [table[SLASH + h * BANDS + j] for j in range(BANDS)]
        score = []
        for run in range(RUNS):
            rows = slice(run * ROWS, (run + 1) * ROWS)
            keys = jnp.concatenate([band[0, RUNS + run - offset] for offset in offsets], axis=0)
            limit = jnp.concatenate(
                [within + near_base(table, ids, run, offset) for offset in offsets], axis=1)
            score.append(jnp.where(token[rows] >= limit, product(qs[rows, cols], keys), LOW))
        score = jnp.concatenate(score, axis=0)
        top = jnp.maximum(wide(jnp.max(score, axis=1, keepdims=True)), raw_sink)
        weight = jnp.exp2((score - across(top, BANDS)) * FACTOR)
        total = wide(jnp.sum(weight, axis=1, keepdims=True)) + jnp.exp2((raw_sink - top) * FACTOR)
        weight = weight.astype(BF16)
        for run in range(RUNS):
            rows = slice(run * ROWS, (run + 1) * ROWS)
            vals = jnp.concatenate([band[1, RUNS + run - offset] for offset in offsets], axis=0)
            acc[rows, cols] = jnp.dot(weight[rows], vals, preferred_element_type=F32)
        tops[:, cols] = top
        sums[:, cols] = total


def add_listed(table, qs, kv, late, acc, tops, sums, put):
    token = TOKENS // RUNS * table[META + 2] + lax.broadcasted_iota(jnp.int32, (TOKENS, 1), 0)
    places = key_places(table, late)
    for h in range(HEADS):
        cols = slice(h * HEAD, (h + 1) * HEAD)
        slots = slots_of(table, h)
        score = product(qs[:, cols], listed(kv, 0, slots))
        score = jnp.where(token >= limits(table, places, h), score, LOW)
        before = tops[:, cols]
        top = jnp.maximum(wide(jnp.max(score, axis=1, keepdims=True)), before)
        weight = jnp.exp2((score - across(top, LISTED * HALF // HEAD)) * FACTOR)
        fade = jnp.exp2((before - top) * FACTOR)
        total = wide(jnp.sum(weight, axis=1, keepdims=True)) + fade * sums[:, cols]
        mixed = jnp.dot(weight.astype(BF16), listed(kv, 1, slots), preferred_element_type=F32)
        put(cols, mixed + acc[:, cols] * fade, top, total)


def early_kernel(table, qs, w, a0, a2, a1, a3, acc, tops, sums, acc_out, tops_out, sums_out, w_out, kv, sems):
    copies = Copies(sems)
    load_half(copies, table[META], a0, a2, a1, a3, kv)
    first = len(copies.made)
    depth = w.shape[0] // 4
    for n in range(4):
        copies.start(w.at[pl.ds(n * depth, depth)], w_out.at[pl.ds(n * depth, depth)])
    copies.wait(first)

    def put(cols, mixed, top, total):
        acc_out[:, cols], tops_out[:, cols], sums_out[:, cols] = mixed, top, total

    add_listed(table, qs, kv, False, acc, tops, sums, put)
    copies.wait()


def project(att, w, blocks, core, keeps, give):
    def rows(block, side):
        start = pl.multiple_of(block * ROWS + side * HALF, HALF)
        return att[pl.ds(start, HALF), :]

    lhs = jnp.concatenate([rows(b, core) for b in blocks] + [rows(b, 1 - core) for b in blocks], axis=0)
    tile = 512
    for n in range(w.shape[1] // tile):
        cols = slice(n * tile, (n + 1) * tile)
        out = jnp.dot(lhs, w[:, cols], preferred_element_type=F32).astype(BF16)
        for i, keep in enumerate(keeps):
            keep[:, cols] = out[i * HALF:(i + 1) * HALF]
        give(n * tile, tile, out[len(blocks) * HALF:])


def late_kernel(table, qs, w, b0, b2, b1, b3, acc, tops, sums, att, keep, give, kv, sems):
    copies = Copies(sems)
    load_half(copies, table[META], b0, b2, b1, b3, kv)
    copies.wait()

    def put(cols, mixed, top, total):
        att[:, cols] = (mixed * (1.0 / total)).astype(BF16)

    add_listed(table, qs, kv, True, acc, tops, sums, put)
    project(att, w, [(table[META + 5] + 2) % X], table[META + 1], [keep], functools.partial(store, give))


def store(give, start, size, rows):
    give[:, start:start + size] = rows


def sides_kernel(table, att, w, keep_below, keep_above, direct, relayed):
    x, mid = table[META + 5], w.shape[1] // 2

    def give(start, size, rows):
        below, above = rows[:HALF], rows[HALF:]
        at = slice(start % mid, start % mid + size)
        if start < mid:
            relayed[:HALF, at], direct[HALF:, at] = below, above
        else:
            direct[:HALF, at], relayed[HALF:, at] = below, above

    project(att, w, [(x + 1) % X, (x + 3) % X], table[META + 1], [keep_below, keep_above], give)


def own_kernel(table, att, w, after, keep, give):
    project(att, w, [table[META + 5]], table[META + 1], [keep], functools.partial(store, give))


def final_kernel(keep, swapped, left_below, left_above, right_below, right_above, out):
    mid = out.shape[1] // 2
    for start, pair in ((0, (left_below, left_above)), (mid, (right_below, right_above))):
        cols = slice(start, start + mid)
        total = keep[:, cols].astype(F32) + swapped[:, cols].astype(F32)
        for part in pair:
            total = total + part[...].astype(F32)
        out[:, cols] = total.astype(BF16)


SMEM = pl.BlockSpec(memory_space=pltpu.SMEM)
VMEM = pl.BlockSpec(memory_space=pltpu.VMEM)
ANY = pl.BlockSpec(memory_space=pl.ANY)


def call(body, ins, outs, scratch, micros, name):
    return pl.pallas_call(
        body,
        out_shape=tuple(pltpu.VMEM(shape, dtype) for shape, dtype in outs),
        in_specs=ins,
        out_specs=(VMEM,) * len(outs),
        scratch_shapes=scratch,
        compiler_params=pltpu.CompilerParams(vmem_limit_bytes=24 * 2 ** 20),
        cost_estimate=pl.CostEstimate(flops=int(micros * 1e9), bytes_accessed=int(micros * 2 ** 20), transcendentals=0),
        name=name,
    )


def total_of(*terms):
    return functools.reduce(lambda a, b: a + b, [t.astype(F32) for t in terms]).astype(BF16)


def tables(c, x, core, vert_blocks, slash_offsets):
    block = jnp.arange(BLOCKS, dtype=jnp.int32)
    present = jnp.any(vert_blocks[:, :, None] == block, axis=(0, 1)).astype(jnp.int32)
    rank = jnp.sum(jnp.where(block[:, None] > block[None, :], present[None, :], 0), axis=1)
    meta = jnp.stack([c % 2, core, RUNS * c, c // Y, (c % Y) // 2, x]).astype(jnp.int32)
    table = jnp.concatenate([rank, meta, vert_blocks.reshape(-1), slash_offsets.reshape(-1)])
    return jnp.where(present > 0, rank, -1), table


def spread_kernel(keys, values, out, sems):
    copies = Copies(sems)
    for kind, a in enumerate((keys, values)):
        for b in range(RUNS):
            copies.start(a.at[b], out.at[:, kind, b])
    copies.wait()


def per_device(queries, keys, values, sink_logits, vert_blocks, slash_offsets, output_weight):
    c = lax.axis_index("ctx")
    h = lax.axis_index("head")
    x, core = h // 2, h % 2
    keys = keys.reshape(RUNS, ROWS, HEAD)
    values = values.reshape(RUNS, ROWS, HEAD)
    place, table = tables(c, x, core, vert_blocks, slash_offsets)
    sink = jnp.broadcast_to(sink_logits[:, None] * (1.0 / SCALE), (HEADS, HEAD))
    far_keys, far_values = [pltpu.with_memory_space_constraint(a.reshape(RUNS, 16, 8, HEAD), pltpu.HBM)
                            for a in (keys, values)]
    (spread,) = call(
        spread_kernel, [ANY, ANY], [((16, 2, RUNS, 8, HEAD), BF16)], [pltpu.SemaphoreType.DMA((2 * RUNS,))], 1, "spread",
    )(far_keys, far_values)
    spread = spread.reshape(Z * Y, RUNS * 8, HEAD)
    prev = lax.ppermute(spread, "ctx", [(s, s + 1) for s in range(Z * Y - 1)]).reshape(16, 2, RUNS, 8, HEAD)
    got = lax.all_to_all(spread, "ctx", 0, 0, tiled=True).reshape(BLOCKS * 8, HEAD)
    rows = ((TOKENS, HEADS * HEAD), BF16)
    q, own = call(
        fetch_kernel, [ANY] * 4, [rows, ((2, RUNS, ROWS, HEAD), BF16)], [pltpu.SemaphoreType.DMA((4,))], 1, "fetch",
    )(*[pltpu.with_memory_space_constraint(a, pltpu.HBM) for a in (queries, keys, values)], spread)
    place, table, sink, q, own = lax.optimization_barrier((place, table, sink, q, own))
    r = jnp.arange(SLOTS * 8, dtype=jnp.int32)[:, None]
    col = jnp.arange(BLOCKS * 8, dtype=jnp.int32)[None, :]
    pick = (jnp.repeat(place, 8)[None, :] == r // 8) & (col % 8 == r % 8)
    mine = jnp.dot(pick.astype(BF16), got, preferred_element_type=F32)
    mine = mine.astype(BF16).reshape(SLOTS, 8, HEAD)

    def from_z(a, offset):
        return lax.ppermute(a, "ctx", z_pairs(-offset))

    z4, z2, z6 = from_z(mine, 4), from_z(mine, 2), from_z(mine, 6)
    prev, z4, z2, z6 = lax.optimization_barrier((prev, z4, z2, z6))
    a0 = jnp.concatenate([mine, z2, z4, z6], axis=1)
    beside = [(Y * z + y, Y * (z ^ 1) + y) for z in range(Z) for y in range(Y)]
    b0 = lax.ppermute(a0, "ctx", beside)
    a1, a2, a3 = [lax.ppermute(a0, "ctx", y_pairs(f)) for f in (1, 2, 3)]

    width = output_weight.shape[1]
    kv = pltpu.VMEM((2, SLOTS, HALF, HEAD), BF16)
    part = ((HALF, width), BF16)
    state = [((TOKENS, HEADS * HEAD), F32)] * 3
    acc, tops, sums = call(
        band_kernel, [SMEM] + [VMEM] * 4, state, [pltpu.VMEM((2, 2 * RUNS, ROWS, HEAD), BF16)], 3, "band",
    )(table, sink, q, prev, own)
    b0, acc = lax.optimization_barrier((b0, acc))
    b1, b3 = [lax.ppermute(b0, "ctx", y_pairs(f)) for f in (1, 3)]
    b2 = lax.ppermute(a2, "ctx", beside)
    acc, tops, sums, w = call(
        early_kernel, [SMEM, VMEM] + [ANY] * 5 + [VMEM] * 3, state + [(output_weight.shape, BF16)],
        [kv, pltpu.SemaphoreType.DMA((8,))], 5, "early",
    )(table, q, pltpu.with_memory_space_constraint(output_weight, pltpu.HBM), a0, a2, a1, a3, acc, tops, sums)
    att, keep_far, give_far = call(
        late_kernel, [SMEM, VMEM, VMEM] + [ANY] * 4 + [VMEM] * 3,
        [rows, part, part], [kv, pltpu.SemaphoreType.DMA((4,))], 0.01, "late",
    )(table, q, w, b0, b2, b1, b3, acc, tops, sums)
    halves = ((2 * HALF, width // 2), BF16)
    keep_below, keep_above, give_direct, give_relayed = call(
        sides_kernel, [SMEM, VMEM, VMEM], [part, part, halves, halves], [], 0.01, "sides",
    )(table, att, w)
    def swap(a):
        return lax.ppermute(a, "head", CORE_PAIRS)

    def to_x(a, step):
        return lax.ppermute(a, "head", x_pairs(step))

    far, direct, relayed = swap(give_far), swap(give_direct), swap(give_relayed)
    mid = width // 2
    far_left = total_of(keep_far[:, :mid], far[:, :mid])
    far_right = total_of(keep_far[:, mid:], far[:, mid:])
    relay_left, relay_right = to_x(far_left, 1), to_x(far_right, -1)
    direct_right = total_of(keep_below[:, mid:], direct[:HALF])
    direct_left = total_of(keep_above[:, :mid], direct[HALF:])
    right_below, left_above = to_x(direct_right, 1), to_x(direct_left, -1)
    keep_own, give_own = call(
        own_kernel, [SMEM, VMEM, VMEM, ANY], [part, part], [], 0.01, "own",
    )(table, att, w, direct_right)

    own = swap(give_own)
    keep_below, keep_above, relayed, relay_left, relay_right = lax.optimization_barrier(
        (keep_below, keep_above, relayed, relay_left, relay_right))
    left_below = to_x(total_of(keep_below[:, :mid], relayed[:HALF], relay_left), 1)
    right_above = to_x(total_of(keep_above[:, mid:], relayed[HALF:], relay_right), -1)
    return pl.pallas_call(
        final_kernel,
        out_shape=jax.ShapeDtypeStruct((HALF, width), BF16),
        in_specs=[VMEM] * 6,
        out_specs=VMEM,
        compiler_params=pltpu.CompilerParams(vmem_limit_bytes=8 * 2 ** 20),
        name="final",
    )(keep_own, own, left_below, left_above, right_below, right_above)


def solution(mesh):
    return jax.shard_map(
        per_device,
        mesh=mesh,
        in_specs=(
            P("ctx", "head"),
            P("ctx", "head"),
            P("ctx", "head"),
            P("head"),
            P("head", None),
            P("head", None),
            P("head", None),
        ),
        out_specs=P(("ctx", "head"), None),
        check_vma=False,
    )
```

```python
import functools

import jax
import jax.numpy as jnp
from jax import lax
from jax.experimental import pallas as pl
from jax.experimental.pallas import tpu as pltpu
from jax.sharding import PartitionSpec as P

HEAD = 128
ROWS = 128
HALF = 64
SLOTS = 24
LISTED = 8
BANDS = 3
BLOCKS = 128
RUNS = 4
HEADS = 8
TOKENS = RUNS * ROWS
SCALE = HEAD ** -0.5
FACTOR = SCALE * 1.4426950408889634
NEVER = 1 << 20
LOW = -1e30
Z, Y, X = 8, 4, 4
BF16, F32 = jnp.bfloat16, jnp.float32
META = BLOCKS
VERT = META + 6
SLASH = VERT + HEADS * LISTED


def z_pairs(step):
    return [(Y * z + y, Y * ((z + step) % Z) + y) for z in range(Z) for y in range(Y)]


def y_pairs(flip):
    return [(Y * z + y, Y * z + (y ^ flip)) for z in range(Z) for y in range(Y)]


def x_pairs(step):
    return [(2 * x + k, 2 * ((x + step) % X) + k) for x in range(X) for k in range(2)]


CORE_PAIRS = [(h, h ^ 1) for h in range(HEADS)]


class Copies:
    def __init__(self, sems):
        self.sems, self.made = sems, []

    def start(self, src, dst):
        made = pltpu.make_async_copy(src, dst, self.sems.at[len(self.made)])
        made.start()
        self.made.append(made)

    def wait(self, count=None):
        for made in self.made[:count]:
            made.wait()
        self.made = [] if count is None else self.made[count:]


def key_places(table, late):
    z, y_half = table[META + 3], table[META + 4]
    n = lax.broadcasted_iota(jnp.int32, (1, HALF), 1)
    part, inner, row = n // 32, (n // 8) % 4, n % 8
    z_of = ((z ^ int(late)) + 2 * inner) % Z
    return (z_of * 2 + (y_half ^ part)) * 8 + row


def load_half(copies, odd, own, far, near, cross, kv):
    for kind, parts in ((odd, (own, far)), (1 - odd, (near, cross))):
        for p, part in enumerate(parts):
            copies.start(part, kv.at[kind, :, pl.ds(32 * p, 32)])


def ids_of(table, h):
    return [table[VERT + h * LISTED + e] for e in range(LISTED)]


def slots_of(table, h):
    return [table[jnp.maximum(i, 0)] for i in ids_of(table, h)]


def listed(kv, kind, slots):
    return jnp.concatenate([kv[kind, slot] for slot in slots], axis=0)


def limits(table, places, h):
    return jnp.concatenate([places + jnp.where(i >= 0, i * ROWS, NEVER) for i in ids_of(table, h)], axis=1)


def near_base(table, ids, run, offset):
    block = table[META + 2] + run - offset
    use = block >= 0
    for i in ids:
        use = jnp.logical_and(use, i != block)
    return jnp.where(use, block * ROWS, NEVER)


def product(q, keys):
    return lax.dot_general(q, keys, (((1,), (1,)), ((), ())), preferred_element_type=F32)


def wide(column):
    return jnp.broadcast_to(column, (column.shape[0], HEAD))


def across(column_block, count):
    return jnp.concatenate([column_block] * count, axis=1)


def fetch_kernel(q, kc, vc, spread, qs, own, sems):
    copies = Copies(sems)
    half = q.shape[0] // 2
    for n in range(2):
        copies.start(q.at[pl.ds(n * half, half)], qs.at[pl.ds(n * half, half)])
    for kind, cur in enumerate((kc, vc)):
        copies.start(cur, own.at[kind])
    copies.wait()


def band_kernel(table, sink, qs, prev, own, acc, tops, sums, band):
    for kind in range(2):
        for b in range(RUNS):
            rows = [prev[r, kind, b].astype(F32) for r in range(16)]
            band[kind, b] = jnp.concatenate(rows, axis=0).astype(BF16)
            band[kind, RUNS + b] = own[kind, b]
    token = TOKENS // RUNS * table[META + 2] + lax.broadcasted_iota(jnp.int32, (TOKENS, 1), 0)
    within = lax.broadcasted_iota(jnp.int32, (1, ROWS), 1)
    for h in range(HEADS):
        cols = slice(h * HEAD, (h + 1) * HEAD)
        raw_sink = sink[h:h + 1, :]
        ids = ids_of(table, h)
        offsets = [table[SLASH + h * BANDS + j] for j in range(BANDS)]
        score = []
        for run in range(RUNS):
            rows = slice(run * ROWS, (run + 1) * ROWS)
            keys = jnp.concatenate([band[0, RUNS + run - offset] for offset in offsets], axis=0)
            limit = jnp.concatenate(
                [within + near_base(table, ids, run, offset) for offset in offsets], axis=1)
            score.append(jnp.where(token[rows] >= limit, product(qs[rows, cols], keys), LOW))
        score = jnp.concatenate(score, axis=0)
        top = jnp.maximum(wide(jnp.max(score, axis=1, keepdims=True)), raw_sink)
        weight = jnp.exp2((score - across(top, BANDS)) * FACTOR)
        total = wide(jnp.sum(weight, axis=1, keepdims=True)) + jnp.exp2((raw_sink - top) * FACTOR)
        weight = weight.astype(BF16)
        for run in range(RUNS):
            rows = slice(run * ROWS, (run + 1) * ROWS)
            vals = jnp.concatenate([band[1, RUNS + run - offset] for offset in offsets], axis=0)
            acc[rows, cols] = jnp.dot(weight[rows], vals, preferred_element_type=F32)
        tops[:, cols] = top
        sums[:, cols] = total


def add_listed(table, qs, kv, late, acc, tops, sums, put):
    token = TOKENS // RUNS * table[META + 2] + lax.broadcasted_iota(jnp.int32, (TOKENS, 1), 0)
    places = key_places(table, late)
    for h in range(HEADS):
        cols = slice(h * HEAD, (h + 1) * HEAD)
        slots = slots_of(table, h)
        score = product(qs[:, cols], listed(kv, 0, slots))
        score = jnp.where(token >= limits(table, places, h), score, LOW)
        before = tops[:, cols]
        top = jnp.maximum(wide(jnp.max(score, axis=1, keepdims=True)), before)
        weight = jnp.exp2((score - across(top, LISTED * HALF // HEAD)) * FACTOR)
        fade = jnp.exp2((before - top) * FACTOR)
        total = wide(jnp.sum(weight, axis=1, keepdims=True)) + fade * sums[:, cols]
        mixed = jnp.dot(weight.astype(BF16), listed(kv, 1, slots), preferred_element_type=F32)
        put(cols, mixed + acc[:, cols] * fade, top, total)


def early_kernel(table, qs, w, a0, a2, a1, a3, acc, tops, sums, acc_out, tops_out, sums_out, w_out, kv, sems):
    copies = Copies(sems)
    load_half(copies, table[META], a0, a2, a1, a3, kv)
    first = len(copies.made)
    depth = w.shape[0] // 4
    for n in range(4):
        copies.start(w.at[pl.ds(n * depth, depth)], w_out.at[pl.ds(n * depth, depth)])
    copies.wait(first)

    def put(cols, mixed, top, total):
        acc_out[:, cols], tops_out[:, cols], sums_out[:, cols] = mixed, top, total

    add_listed(table, qs, kv, False, acc, tops, sums, put)
    copies.wait()


def project(att, w, blocks, core, keeps, give):
    def rows(block, side):
        start = pl.multiple_of(block * ROWS + side * HALF, HALF)
        return att[pl.ds(start, HALF), :]

    lhs = jnp.concatenate([rows(b, core) for b in blocks] + [rows(b, 1 - core) for b in blocks], axis=0)
    tile = 512
    for n in range(w.shape[1] // tile):
        cols = slice(n * tile, (n + 1) * tile)
        out = jnp.dot(lhs, w[:, cols], preferred_element_type=F32).astype(BF16)
        for i, keep in enumerate(keeps):
            keep[:, cols] = out[i * HALF:(i + 1) * HALF]
        give(n * tile, tile, out[len(blocks) * HALF:])


def late_kernel(table, qs, w, b0, b2, b1, b3, acc, tops, sums, att, keep, give, kv, sems):
    copies = Copies(sems)
    load_half(copies, table[META], b0, b2, b1, b3, kv)
    copies.wait()

    def put(cols, mixed, top, total):
        att[:, cols] = (mixed * (1.0 / total)).astype(BF16)

    add_listed(table, qs, kv, True, acc, tops, sums, put)
    project(att, w, [(table[META + 5] + 2) % X], table[META + 1], [keep], functools.partial(store, give))


def store(give, start, size, rows):
    give[:, start:start + size] = rows


def sides_kernel(table, att, w, keep_below, keep_above, direct, relayed):
    x, mid = table[META + 5], w.shape[1] // 2

    def give(start, size, rows):
        below, above = rows[:HALF], rows[HALF:]
        at = slice(start % mid, start % mid + size)
        if start < mid:
            relayed[:HALF, at], direct[HALF:, at] = below, above
        else:
            direct[:HALF, at], relayed[HALF:, at] = below, above

    project(att, w, [(x + 1) % X, (x + 3) % X], table[META + 1], [keep_below, keep_above], give)


def own_kernel(table, att, w, after, keep, give):
    project(att, w, [table[META + 5]], table[META + 1], [keep], functools.partial(store, give))


def final_kernel(keep, swapped, left_below, left_above, right_below, right_above, out, held, sems):
    copies = Copies(sems)
    mid = out.shape[1] // 2
    for start, pair in ((0, (left_below, left_above)), (mid, (right_below, right_above))):
        cols = slice(start, start + mid)
        total = keep[:, cols].astype(F32) + swapped[:, cols].astype(F32)
        for part in pair:
            total = total + part[...].astype(F32)
        held[:, cols] = total.astype(BF16)
        copies.start(held.at[:, pl.ds(start, mid)], out.at[:, pl.ds(start, mid)])
    copies.wait()


SMEM = pl.BlockSpec(memory_space=pltpu.SMEM)
VMEM = pl.BlockSpec(memory_space=pltpu.VMEM)
ANY = pl.BlockSpec(memory_space=pl.ANY)


def call(body, ins, outs, scratch, micros, name):
    return pl.pallas_call(
        body,
        out_shape=tuple(pltpu.VMEM(shape, dtype) for shape, dtype in outs),
        in_specs=ins,
        out_specs=(VMEM,) * len(outs),
        scratch_shapes=scratch,
        compiler_params=pltpu.CompilerParams(vmem_limit_bytes=24 * 2 ** 20),
        cost_estimate=pl.CostEstimate(flops=int(micros * 1e9), bytes_accessed=int(micros * 2 ** 20), transcendentals=0),
        name=name,
    )


def total_of(*terms):
    return functools.reduce(lambda a, b: a + b, [t.astype(F32) for t in terms]).astype(BF16)


def tables(c, x, core, vert_blocks, slash_offsets):
    block = jnp.arange(BLOCKS, dtype=jnp.int32)
    present = jnp.any(vert_blocks[:, :, None] == block, axis=(0, 1)).astype(jnp.int32)
    rank = jnp.sum(jnp.where(block[:, None] > block[None, :], present[None, :], 0), axis=1)
    meta = jnp.stack([c % 2, core, RUNS * c, c // Y, (c % Y) // 2, x]).astype(jnp.int32)
    table = jnp.concatenate([rank, meta, vert_blocks.reshape(-1), slash_offsets.reshape(-1)])
    return jnp.where(present > 0, rank, -1), table


def spread_kernel(keys, values, out, sems):
    copies = Copies(sems)
    for kind, a in enumerate((keys, values)):
        for b in range(RUNS):
            copies.start(a.at[b], out.at[:, kind, b])
    copies.wait()


def per_device(queries, keys, values, sink_logits, vert_blocks, slash_offsets, output_weight):
    c = lax.axis_index("ctx")
    h = lax.axis_index("head")
    x, core = h // 2, h % 2
    keys = keys.reshape(RUNS, ROWS, HEAD)
    values = values.reshape(RUNS, ROWS, HEAD)
    place, table = tables(c, x, core, vert_blocks, slash_offsets)
    sink = jnp.broadcast_to(sink_logits[:, None] * (1.0 / SCALE), (HEADS, HEAD))
    far_keys, far_values = [pltpu.with_memory_space_constraint(a.reshape(RUNS, 16, 8, HEAD), pltpu.HBM)
                            for a in (keys, values)]
    (spread,) = call(
        spread_kernel, [ANY, ANY], [((16, 2, RUNS, 8, HEAD), BF16)], [pltpu.SemaphoreType.DMA((2 * RUNS,))], 1, "spread",
    )(far_keys, far_values)
    spread = spread.reshape(Z * Y, RUNS * 8, HEAD)
    prev = lax.ppermute(spread, "ctx", [(s, s + 1) for s in range(Z * Y - 1)]).reshape(16, 2, RUNS, 8, HEAD)
    got = lax.all_to_all(spread, "ctx", 0, 0, tiled=True).reshape(BLOCKS * 8, HEAD)
    rows = ((TOKENS, HEADS * HEAD), BF16)
    q, own = call(
        fetch_kernel, [ANY] * 4, [rows, ((2, RUNS, ROWS, HEAD), BF16)], [pltpu.SemaphoreType.DMA((4,))], 1, "fetch",
    )(*[pltpu.with_memory_space_constraint(a, pltpu.HBM) for a in (queries, keys, values)], spread)
    place, table, sink, q, own = lax.optimization_barrier((place, table, sink, q, own))
    r = jnp.arange(SLOTS * 8, dtype=jnp.int32)[:, None]
    col = jnp.arange(BLOCKS * 8, dtype=jnp.int32)[None, :]
    pick = (jnp.repeat(place, 8)[None, :] == r // 8) & (col % 8 == r % 8)
    mine = jnp.dot(pick.astype(BF16), got, preferred_element_type=F32)
    mine = mine.astype(BF16).reshape(SLOTS, 8, HEAD)

    def from_z(a, offset):
        return lax.ppermute(a, "ctx", z_pairs(-offset))

    z2, z4, z6 = from_z(mine, 2), from_z(mine, 4), from_z(mine, 6)
    prev, z2, z4, z6 = lax.optimization_barrier((prev, z2, z4, z6))
    a0 = jnp.concatenate([mine, z2, z4, z6], axis=1)
    beside = [(Y * z + y, Y * (z ^ 1) + y) for z in range(Z) for y in range(Y)]
    b0 = lax.ppermute(a0, "ctx", beside)
    a1, a2, a3 = [lax.ppermute(a0, "ctx", y_pairs(f)) for f in (1, 2, 3)]

    width = output_weight.shape[1]
    kv = pltpu.VMEM((2, SLOTS, HALF, HEAD), BF16)
    part = ((HALF, width), BF16)
    state = [((TOKENS, HEADS * HEAD), F32)] * 3
    acc, tops, sums = call(
        band_kernel, [SMEM] + [VMEM] * 4, state, [pltpu.VMEM((2, 2 * RUNS, ROWS, HEAD), BF16)], 3, "band",
    )(table, sink, q, prev, own)
    b0, acc = lax.optimization_barrier((b0, acc))
    b1, b3 = [lax.ppermute(b0, "ctx", y_pairs(f)) for f in (1, 3)]
    b2 = lax.ppermute(a2, "ctx", beside)
    acc, tops, sums, w = call(
        early_kernel, [SMEM, VMEM] + [ANY] * 5 + [VMEM] * 3, state + [(output_weight.shape, BF16)],
        [kv, pltpu.SemaphoreType.DMA((8,))], 5, "early",
    )(table, q, pltpu.with_memory_space_constraint(output_weight, pltpu.HBM), a0, a2, a1, a3, acc, tops, sums)
    att, keep_far, give_far = call(
        late_kernel, [SMEM, VMEM, VMEM] + [ANY] * 4 + [VMEM] * 3,
        [rows, part, part], [kv, pltpu.SemaphoreType.DMA((4,))], 0.01, "late",
    )(table, q, w, b0, b2, b1, b3, acc, tops, sums)
    halves = ((2 * HALF, width // 2), BF16)
    keep_below, keep_above, give_direct, give_relayed = call(
        sides_kernel, [SMEM, VMEM, VMEM], [part, part, halves, halves], [], 0.01, "sides",
    )(table, att, w)
    def swap(a):
        return lax.ppermute(a, "head", CORE_PAIRS)

    def to_x(a, step):
        return lax.ppermute(a, "head", x_pairs(step))

    far, direct, relayed = swap(give_far), swap(give_direct), swap(give_relayed)
    mid = width // 2
    far_left = total_of(keep_far[:, :mid], far[:, :mid])
    far_right = total_of(keep_far[:, mid:], far[:, mid:])
    relay_left, relay_right = to_x(far_left, 1), to_x(far_right, -1)
    direct_right = total_of(keep_below[:, mid:], direct[:HALF])
    direct_left = total_of(keep_above[:, :mid], direct[HALF:])
    right_below, left_above = to_x(direct_right, 1), to_x(direct_left, -1)
    keep_own, give_own = call(
        own_kernel, [SMEM, VMEM, VMEM, ANY], [part, part], [], 0.01, "own",
    )(table, att, w, direct_right)

    own = swap(give_own)
    keep_below, keep_above, relayed, relay_left, relay_right = lax.optimization_barrier(
        (keep_below, keep_above, relayed, relay_left, relay_right))
    left_below = to_x(total_of(keep_below[:, :mid], relayed[:HALF], relay_left), 1)
    right_above = to_x(total_of(keep_above[:, mid:], relayed[HALF:], relay_right), -1)
    return pl.pallas_call(
        final_kernel,
        out_shape=jax.ShapeDtypeStruct((HALF, width), BF16),
        in_specs=[VMEM] * 6,
        out_specs=ANY,
        scratch_shapes=[pltpu.VMEM((HALF, width), BF16), pltpu.SemaphoreType.DMA((2,))],
        compiler_params=pltpu.CompilerParams(vmem_limit_bytes=8 * 2 ** 20),
        name="final",
    )(keep_own, own, left_below, left_above, right_below, right_above)


def solution(mesh):
    return jax.shard_map(
        per_device,
        mesh=mesh,
        in_specs=(
            P("ctx", "head"),
            P("ctx", "head"),
            P("ctx", "head"),
            P("head"),
            P("head", None),
            P("head", None),
            P("head", None),
        ),
        out_specs=P(("ctx", "head"), None),
        check_vma=False,
    )
```
